32 devices in a mesh: dp: 8 (over z, x), mp: 4 (over y, core).
Axes of the slice: x: 2, y: 2, z: 4, core: 2. Of those that a mesh axis runs over, the one named last changes fastest.
Arguments:
- latent: bfloat16 [262144, 256], P(('dp', 'mp')), may hold values from -6 to 6
- chance_code: int32 [262144], P(('dp', 'mp')), may hold values from 0 to 31
- importance: int32 [262144], P(('dp', 'mp')), may hold values from 21 to 2835
- value_bin: int32 [262144], P(('dp', 'mp')), may hold values from 0 to 600
- reward_bin: int32 [262144], P(('dp', 'mp')), may hold values from 0 to 600
- action_taken: int32 [262144], P(('dp', 'mp')), may hold values from 0 to 3
- code_target: int32 [262144], P(('dp', 'mp')), may hold values from 0 to 31
- stem_weight: float32 [256, 256], P('mp', 'dp'), may hold values from -0.375 to 0.375
- stem_moment: float32 [256, 256], P('mp', 'dp'), may hold values from -2.5 to 2.5
- stem_square: float32 [256, 256], P('mp', 'dp'), may hold values from 0.026 to 0.104
- up_weight: float32 [4, 256, 256], P(None, 'dp', 'mp'), may hold values from -0.5 to 0.5
- up_moment: float32 [4, 256, 256], P(None, 'dp', 'mp'), may hold values from -2.5 to 2.5
- up_square: float32 [4, 256, 256], P(None, 'dp', 'mp'), may hold values from 0.026 to 0.104
- down_weight: float32 [4, 256, 256], P(None, 'mp', 'dp'), may hold values from -0.5 to 0.5
- down_moment: float32 [4, 256, 256], P(None, 'mp', 'dp'), may hold values from -2.5 to 2.5
- down_square: float32 [4, 256, 256], P(None, 'mp', 'dp'), may hold values from 0.026 to 0.104
- head_weight: float32 [256, 1238], P(('dp', 'mp')), may hold values from -0.75 to 0.75
- head_moment: float32 [256, 1238], P(('dp', 'mp')), may hold values from -2.5 to 2.5
- head_square: float32 [256, 1238], P(('dp', 'mp')), may hold values from 0.026 to 0.104
- chance_table: float32 [32, 256], P(None, ('dp', 'mp')), may hold values from -1.8 to 1.8
- table_moment: float32 [32, 256], P(None, ('dp', 'mp')), may hold values from -2.5 to 2.5
- table_square: float32 [32, 256], P(None, ('dp', 'mp')), may hold values from 0.026 to 0.104
- norm_params: float32 [5, 2, 256], P(None, None, ('dp', 'mp')), may hold values from -1.5 to 2.5
- norm_moment: float32 [5, 2, 256], P(None, None, ('dp', 'mp')), may hold values from -4 to 4
- norm_square: float32 [5, 2, 256], P(None, None, ('dp', 'mp')), may hold values from 0.23428571 to 0.9342857
Outputs:
- grad_norm: float32 [], replicated
- latent_grad: float32 [262144, 256], P(('dp', 'mp'))
- new_stem: float32 [256, 256], P('mp', 'dp')
- stem_first: float32 [256, 256], P('mp', 'dp')
- stem_second: float32 [256, 256], P('mp', 'dp')
- stem_copy: bfloat16 [256, 256], P('mp', 'dp')
- new_up: float32 [4, 256, 256], P(None, 'dp', 'mp')
- up_first: float32 [4, 256, 256], P(None, 'dp', 'mp')
- up_second: float32 [4, 256, 256], P(None, 'dp', 'mp')
- up_copy: bfloat16 [4, 256, 256], P(None, 'dp', 'mp')
- new_down: float32 [4, 256, 256], P(None, 'mp', 'dp')
- down_first: float32 [4, 256, 256], P(None, 'mp', 'dp')
- down_second: float32 [4, 256, 256], P(None, 'mp', 'dp')
- down_copy: bfloat16 [4, 256, 256], P(None, 'mp', 'dp')
- new_head: float32 [256, 1238], P(('dp', 'mp'))
- head_first: float32 [256, 1238], P(('dp', 'mp'))
- head_second: float32 [256, 1238], P(('dp', 'mp'))
- head_copy: bfloat16 [256, 1238], P(('dp', 'mp'))
- new_table: float32 [32, 256], P(None, ('dp', 'mp'))
- table_first: float32 [32, 256], P(None, ('dp', 'mp'))
- table_second: float32 [32, 256], P(None, ('dp', 'mp'))
- table_copy: bfloat16 [32, 256], P(None, ('dp', 'mp'))
- new_norms: float32 [5, 2, 256], P(None, None, ('dp', 'mp'))
- norms_first: float32 [5, 2, 256], P(None, None, ('dp', 'mp'))
- norms_second: float32 [5, 2, 256], P(None, None, ('dp', 'mp'))
The draws below stay inside these ranges and needn't reach their ends.
All inputs are finite; a program needn't handle non-finite values.
Results may differ from the reference program's by a relative error of at most 0.0055.
The reference program's roundings to bfloat16 on the way count: a program that leaves them out, or rounds other values in their place, can miss the bound.
Values may be sent and summed in bfloat16 or wider, within the bound.
A program may use at most 256 MiB of HBM per device.

```python
import math
from functools import partial
import jax
import jax.numpy as jnp
from jax import lax

D = 256
BINS = 601
ACTIONS = 4
CODES = 32
LAYERS = 4
STEP = 10
TOK_DEV = 8192
TOKENS = 262144
HEADS = 1238
PARAMS = 917504
N_DP = 8
N_MP = 4


def rising(count, spread_ratio):
    along = jnp.arange(count, dtype=jnp.float32) / count
    return (1.0 + (spread_ratio - 1.0) * along) * (2.0 / (1.0 + spread_ratio))


def draw_latent(key, part):
    key = jax.random.fold_in(key, 1)
    values = jnp.clip(jax.random.normal(key, (TOKENS, D), jnp.float32), -4.0, 4.0)
    spread_ratio = 3.0
    return (values * rising(D, spread_ratio)[None, :]).astype(jnp.bfloat16)


def draw_up_weight(key, part):
    key = jax.random.fold_in(key, 2)
    values = jnp.clip(jax.random.normal(key, (LAYERS, D, D), jnp.float32), -4.0, 4.0)
    spread_ratio = 3.0
    return values * D ** (-0.5) * rising(D, spread_ratio)[None, None, :]


def draw_down_weight(key, part):
    key = jax.random.fold_in(key, 3)
    values = jnp.clip(jax.random.normal(key, (LAYERS, D, D), jnp.float32), -4.0, 4.0)
    spread_ratio = 3.0
    return values * D ** (-0.5) * rising(D, spread_ratio)[None, :, None]


def draw_norm_params(key, part):
    key = jax.random.fold_in(key, 4)
    key_gain, key_shift = jax.random.split(key)
    gain_noise = jnp.clip(jax.random.normal(key_gain, (LAYERS + 1, D), jnp.float32), -4.0, 4.0)
    shift_noise = jnp.clip(jax.random.normal(key_shift, (LAYERS + 1, D), jnp.float32), -4.0, 4.0)
    spread_ratio = 3.0
    gains = rising(D, spread_ratio)[None, :] * (1.0 + 0.1 * gain_noise)
    shifts = 0.3 * shift_noise
    return jnp.stack([gains, shifts], axis=1)


def draw_importance(key, part):
    key = jax.random.fold_in(key, 5)
    row_index = jnp.arange(TOKENS, dtype=jnp.int32)
    device_index = row_index // TOK_DEV
    data_index = device_index // N_MP
    model_index = device_index % N_MP
    levels = jax.random.randint(key, (TOKENS,), 0, 16, dtype=jnp.int32)
    within = row_index % TOK_DEV
    levels = jnp.where(within == 0, 15, jnp.where(within == 1, 0, levels))
    heavy = 1 + levels * levels // 16
    return heavy * (N_DP - 1 + 2 * data_index) * (N_MP - 1 + 2 * model_index)


def place_ends(drawn, stream_key, low, high):
    longest = drawn.shape.index(max(drawn.shape))
    spots = []
    for shift in (0, 1):
        where = [jax.random.randint(jax.random.fold_in(stream_key, axis), (), 0, length) for axis, length in enumerate(drawn.shape)]
        where[longest] = (where[longest] + shift) % drawn.shape[longest]
        spots.append(tuple(where))
    return drawn.at[spots[0]].set(low).at[spots[1]].set(high)


def level_of(rng, extent, cuts, low, high):
    loudness, own = 1.0, jax.random.fold_in(rng, 6)
    for axis_at, blocks in cuts:
        draws = jnp.exp(jax.random.uniform(jax.random.fold_in(own, axis_at), (blocks,), jnp.float32, low / len(cuts), high / len(cuts)))
        loudness = loudness * jnp.repeat(draws, extent[axis_at] // blocks).reshape([-1 if axis == axis_at else 1 for axis in range(len(extent))])
    return loudness


def normal_values(rng, dims, width, limit, shards=(), held_as=jnp.bfloat16):
    result = width * jax.random.normal(rng, dims, jnp.float32)
    if shards:
        result = result * level_of(rng, dims, shards, -0.22, 0.18)
    return jnp.clip(result, -limit, limit).astype(held_as)


def setup_inputs(seed: int = 0) -> dict:
    arg_keys = jax.random.split(jax.random.key(seed), 26)
    return {
        "latent": draw_latent(jax.random.fold_in(arg_keys[25], 71), 0),
        "chance_code": place_ends(jax.random.randint(arg_keys[1], (TOKENS,), 0, CODES), jax.random.fold_in(arg_keys[1], 1), 0, CODES - 1).astype(jnp.int32),
        "importance": draw_importance(jax.random.fold_in(arg_keys[25], 71), 0),
        "value_bin": place_ends(jax.random.randint(arg_keys[3], (TOKENS,), 0, BINS), jax.random.fold_in(arg_keys[3], 1), 0, BINS - 1).astype(jnp.int32),
        "reward_bin": place_ends(jax.random.randint(arg_keys[4], (TOKENS,), 0, BINS), jax.random.fold_in(arg_keys[4], 1), 0, BINS - 1).astype(jnp.int32),
        "action_taken": place_ends(jax.random.randint(arg_keys[5], (TOKENS,), 0, ACTIONS), jax.random.fold_in(arg_keys[5], 1), 0, ACTIONS - 1).astype(jnp.int32),
        "code_target": place_ends(jax.random.randint(arg_keys[6], (TOKENS,), 0, CODES), jax.random.fold_in(arg_keys[6], 1), 0, CODES - 1).astype(jnp.int32),
        "stem_weight": normal_values(arg_keys[7], (D, D), D ** -0.5, 0.375, ((0, 4), (1, 8)), jnp.float32),
        "stem_moment": normal_values(arg_keys[8], (D, D), (0.33 * TOKENS ** 0.5 * PARAMS ** -0.5), 2.5, ((0, 4), (1, 8)), jnp.float32),
        "stem_square": jnp.clip(jnp.exp(math.log(0.104) - 1.3862944 * jax.random.uniform(arg_keys[9], (D, D), jnp.float32) ** level_of(arg_keys[9], (D, D), ((0, 4), (1, 8)), -0.2, 0.2)), 0.026, 0.104),
        "up_weight": draw_up_weight(jax.random.fold_in(arg_keys[25], 71), 0),
        "up_moment": normal_values(arg_keys[11], (LAYERS, D, D), (0.33 * TOKENS ** 0.5 * PARAMS ** -0.5), 2.5, ((1, 8), (2, 4)), jnp.float32),
        "up_square": jnp.clip(jnp.exp(math.log(0.104) - 1.3862944 * jax.random.uniform(arg_keys[12], (LAYERS, D, D), jnp.float32) ** level_of(arg_keys[12], (LAYERS, D, D), ((1, 8), (2, 4)), -0.2, 0.2)), 0.026, 0.104),
        "down_weight": draw_down_weight(jax.random.fold_in(arg_keys[25], 71), 0),
        "down_moment": normal_values(arg_keys[14], (LAYERS, D, D), (0.33 * TOKENS ** 0.5 * PARAMS ** -0.5), 2.5, ((1, 4), (2, 8)), jnp.float32),
        "down_square": jnp.clip(jnp.exp(math.log(0.104) - 1.3862944 * jax.random.uniform(arg_keys[15], (LAYERS, D, D), jnp.float32) ** level_of(arg_keys[15], (LAYERS, D, D), ((1, 4), (2, 8)), -0.2, 0.2)), 0.026, 0.104),
        "head_weight": normal_values(arg_keys[16], (D, HEADS), (D // 4) ** -0.5, 0.75, ((0, 32),), jnp.float32),
        "head_moment": normal_values(arg_keys[17], (D, HEADS), (0.33 * TOKENS ** 0.5 * PARAMS ** -0.5), 2.5, ((0, 32),), jnp.float32),
        "head_square": jnp.clip(jnp.exp(math.log(0.104) - 1.3862944 * jax.random.uniform(arg_keys[18], (D, HEADS), jnp.float32) ** level_of(arg_keys[18], (D, HEADS), ((0, 32),), -0.2, 0.2)), 0.026, 0.104),
        "chance_table": normal_values(arg_keys[19], (CODES, D), 0.3, 1.8, ((1, 32),), jnp.float32),
        "table_moment": normal_values(arg_keys[20], (CODES, D), (0.33 * TOKENS ** 0.5 * PARAMS ** -0.5), 2.5, ((1, 32),), jnp.float32),
        "table_square": jnp.clip(jnp.exp(math.log(0.104) - 1.3862944 * jax.random.uniform(arg_keys[21], (CODES, D), jnp.float32) ** level_of(arg_keys[21], (CODES, D), ((1, 32),), -0.2, 0.2)), 0.026, 0.104),
        "norm_params": draw_norm_params(jax.random.fold_in(arg_keys[25], 71), 0),
        "norm_moment": normal_values(arg_keys[23], (LAYERS + 1, 2, D), (1.0 * TOKENS ** 0.5 * PARAMS ** -0.5), 4.0, ((2, 32),), jnp.float32),
        "norm_square": jnp.clip(jnp.exp(math.log(0.9342857) - 1.3832409 * jax.random.uniform(arg_keys[24], (LAYERS + 1, 2, D), jnp.float32) ** level_of(arg_keys[24], (LAYERS + 1, 2, D), ((2, 32),), -0.2, 0.2)), 0.23428571, 0.9342857),
    }


beta_one = 0.9
beta_two = 0.99
eps_adam = 1e-08
eps_norm = 1e-05
matrix_rate = 0.2
vector_rate = 0.6
decay_rate = 0.1
clip_scale = 3.0

@jax.custom_vjp
def low(v):
    return lax.optimization_barrier(v.astype(jnp.bfloat16)).astype(jnp.float32)

@jax.custom_vjp
def low_back(v):
    return v

def low_keep(v):
    return (low(v), None)

def low_pass(kept, grad):
    return (grad,)

def back_keep(v):
    return (v, None)

def back_low(kept, grad):
    return (low(grad),)
low.defvjp(low_keep, low_pass)
low_back.defvjp(back_keep, back_low)

def product(left, right):
    return jnp.dot(left, right, precision=lax.Precision.HIGHEST, preferred_element_type=jnp.float32)

def layer_norm(stream, gain, shift):
    centered = stream - lax.optimization_barrier(jnp.mean(stream, axis=-1, keepdims=True))
    spread = lax.optimization_barrier(jnp.mean(centered * centered, axis=-1, keepdims=True))
    return centered * lax.rsqrt(spread + eps_norm) * gain + shift

def normed(stream, gain, shift):
    return jax.nn.gelu(layer_norm(stream, gain, shift))

def cross_entropy(logits, target):
    picked = jnp.take_along_axis(logits, target[:, None].astype(jnp.int32), axis=1)[:, 0]
    return jax.nn.logsumexp(logits, axis=1) - picked

def block_loss(params, latent_rows, code_rows, value_rows, reward_rows, action_rows, target_rows, coef_rows):
    stem_matrix, upward, downward, head_matrix, code_table, norm_table = params
    code_hot = (code_rows[:, None] == jnp.arange(CODES, dtype=jnp.int32)[None, :]).astype(jnp.float32)
    pre_stem = low_back(product(latent_rows, stem_matrix)) + product(code_hot, code_table)
    stream = normed(pre_stem, norm_table[0, 0], norm_table[0, 1])
    for layer_idx in range(LAYERS):
        active = low(normed(stream, norm_table[layer_idx + 1, 0], norm_table[layer_idx + 1, 1]))
        inner = low_back(product(active, upward[layer_idx]))
        gated = low(jax.nn.gelu(inner))
        stream = stream + low_back(product(gated, downward[layer_idx]))
    logits = low_back(product(low(stream), head_matrix))
    per_row = cross_entropy(logits[:, :BINS], value_rows)
    per_row = per_row + cross_entropy(logits[:, BINS:2 * BINS], reward_rows)
    per_row = per_row + cross_entropy(logits[:, 2 * BINS:2 * BINS + ACTIONS], action_rows)
    per_row = per_row + cross_entropy(logits[:, 2 * BINS + ACTIONS:], target_rows)
    return jnp.sum(coef_rows * per_row)

def total_loss(extras, stem_matrix, upward, downward, head_matrix, code_table, norm_table, latent_values):
    params = (low(stem_matrix), low(upward), low(downward), low(head_matrix), low(code_table), low(norm_table))
    block_size = math.gcd(TOKENS, 4096)
    block_count = TOKENS // block_size
    pieces_all = (latent_values.reshape(block_count, block_size, D),) + tuple((member.reshape((block_count, block_size)) for member in extras))

    def scan_step(carry, pieces):
        return (carry + jax.checkpoint(block_loss)(params, *pieces), None)
    total, unused = lax.scan(scan_step, jnp.zeros((), jnp.float32), pieces_all)
    return total

def adamw(weight, moment, square, grad, rate, decay):
    first = beta_one * moment + (1.0 - beta_one) * grad
    second = beta_two * square + (1.0 - beta_two) * grad * grad
    first_hat = first / (1.0 - beta_one ** STEP)
    second_hat = second / (1.0 - beta_two ** STEP)
    updated = weight - rate * (first_hat / (jnp.sqrt(second_hat) + eps_adam) + decay * weight)
    return (updated, first, second)

def reference(latent, chance_code, importance, value_bin, reward_bin, action_taken, code_target, stem_weight, stem_moment, stem_square, up_weight, up_moment, up_square, down_weight, down_moment, down_square, head_weight, head_moment, head_square, chance_table, table_moment, table_square, norm_params, norm_moment, norm_square):
    weight_values = importance.astype(jnp.float32)
    coef = TOKENS * weight_values / jnp.sum(weight_values)
    extras = (chance_code, value_bin, reward_bin, action_taken, code_target, coef)
    loss_value, pullback = jax.vjp(partial(total_loss, extras), stem_weight, up_weight, down_weight, head_weight, chance_table, norm_params, latent.astype(jnp.float32))
    grads = pullback(jnp.ones((), jnp.float32))
    squares = jnp.stack([jnp.sum(member * member) for member in grads[:6]])
    grad_norm = jnp.sqrt(jnp.sum(squares))
    ratio = jnp.minimum(1.0, clip_scale * math.sqrt(TOKENS) / grad_norm)
    stem_new, stem_first, stem_second = adamw(stem_weight, stem_moment, stem_square, grads[0] * ratio, matrix_rate, decay_rate)
    up_new, up_first, up_second = adamw(up_weight, up_moment, up_square, grads[1] * ratio, matrix_rate, decay_rate)
    down_new, down_first, down_second = adamw(down_weight, down_moment, down_square, grads[2] * ratio, matrix_rate, decay_rate)
    head_new, head_first, head_second = adamw(head_weight, head_moment, head_square, grads[3] * ratio, matrix_rate, decay_rate)
    table_new, table_first, table_second = adamw(chance_table, table_moment, table_square, grads[4] * ratio, matrix_rate, decay_rate)
    norms_new, norms_first, norms_second = adamw(norm_params, norm_moment, norm_square, grads[5] * ratio, vector_rate, 0.0)
    return (grad_norm, grads[6], stem_new, stem_first, stem_second, stem_new.astype(jnp.bfloat16), up_new, up_first, up_second, up_new.astype(jnp.bfloat16), down_new, down_first, down_second, down_new.astype(jnp.bfloat16), head_new, head_first, head_second, head_new.astype(jnp.bfloat16), table_new, table_first, table_second, table_new.astype(jnp.bfloat16), norms_new, norms_first, norms_second)
```

```python
import math
import functools

import jax
import jax.numpy as jnp
from jax import lax
from jax.experimental import pallas as pl
from jax.experimental.pallas import tpu as pltpu
from jax.sharding import PartitionSpec as P

D = 256
BINS = 601
ACTIONS = 4
CODES = 32
LAYERS = 4
STEP = 10

VALUE_AT = 0
REWARD_AT = 608
CHANCE_AT = 1216
POLICY_AT = 1248
ROWS = 1264
DEPTH = 1280

beta_one = 0.9
beta_two = 0.99
eps_adam = 1e-08
eps_norm = 1e-05
matrix_rate = 0.2
vector_rate = 0.6
decay_rate = 0.1
clip_scale = 3.0

GELU_A = math.sqrt(2.0 / math.pi)
GELU_B = GELU_A * 0.044715
LOG2E = 1.4426950408889634
LANES = 256
CHAINS = 2
CHUNK = 16
BF = jnp.bfloat16
F32 = jnp.float32
MESH = pl.DeviceIdType.MESH
MATRICES = 1 + 2 * LAYERS
NORM_LANE = 32
SUM_LANE = 64
SUM_ROW = 10


def dot_nn(left, right):
    return lax.dot_general(left, right, (((1,), (0,)), ((), ())), preferred_element_type=F32)


def dot_nt(left, right):
    return lax.dot_general(left, right, (((1,), (1,)), ((), ())), preferred_element_type=F32)


def dot_tn(left, right):
    return lax.dot_general(left, right, (((0,), (0,)), ((), ())), preferred_element_type=F32)


def gelu_pair(v):
    square = v * v
    gate = 1.0 + jnp.tanh(v * (GELU_A + GELU_B * square))
    value = v * gate
    slope = gate + value * (2.0 - gate) * (GELU_A + 3.0 * GELU_B * square)
    return value, slope


def fold_rows(total, part):
    for at in range(0, part.shape[0], 8):
        piece = part[at : at + 8]
        total = piece if total is None else total + piece
    return total


def peak_rows(total, part):
    for at in range(0, part.shape[0], 8):
        piece = part[at : at + 8]
        total = piece if total is None else jnp.maximum(total, piece)
    return total


def orders_of(dp, mp):
    def step(axis, low, size):
        return (axis, low, size) if size > 1 else None

    far_dp, near_dp = step("dp", 2, dp // 2), step("dp", 1, 2)
    far_mp, near_mp = step("mp", 2, mp // 2), step("mp", 1, 2)
    return (
        [member for member in (far_dp, near_dp, far_mp, near_mp) if member],
        [member for member in (far_dp, far_mp, near_dp, near_mp) if member],
    )


def digit_of(step, data, model):
    axis, low, ways = step
    return ((data if axis == "dp" else model) // low) % ways


def slot_of(order, data, model):
    place, weight = 0, 1
    for step in order:
        place = place + digit_of(step, data, model) * weight
        weight *= step[2]
    return place


def partner_of(step, away):
    axis, low, ways = step
    index = lax.axis_index(axis)
    digit = (index // low) % ways
    other = (digit + away) % ways
    return {axis: index + (other - digit) * low}, other - digit


def sizes_of(order):
    sizes = [1]
    for step in order:
        sizes.append(sizes[-1] * step[2])
    return sizes


class Packing:
    def __init__(self, dp, mp):
        self.dp, self.mp, self.count = dp, mp, dp * mp
        self.deep, self.wide, self.own = D // dp, D // mp, D // (dp * mp)
        self.per = 128 // self.wide
        self.groups = -(-MATRICES // self.per)
        self.head_at = self.groups * self.deep
        self.tail_at = -(-(self.head_at + self.own * (DEPTH // 128)) // 8) * 8
        self.rows = -(-(self.tail_at + 16) // 32) * 32
        self.half = self.rows // 2
        self.orders = orders_of(dp, mp)
        self.sizes = [sizes_of(order) for order in self.orders]
        self.most = max(step[2] for step in self.orders[0])

    def split(self, begin, end):
        side = 1 if begin >= self.half else 0
        assert begin >= self.half or end <= self.half
        return side, slice(begin - side * self.half, end - side * self.half)


def pad_lanes(array, lanes):
    missing = lanes - array.shape[1]
    return array if missing == 0 else jnp.concatenate([array, jnp.zeros((array.shape[0], missing), array.dtype)], axis=1)


def spread_head(head):
    rows = head.shape[0]

    def blank(count):
        return jnp.zeros((rows, count), head.dtype)

    return jnp.concatenate(
        [
            head[:, :BINS],
            blank(REWARD_AT - BINS),
            head[:, BINS : 2 * BINS],
            blank(CHANCE_AT - REWARD_AT - BINS),
            head[:, 2 * BINS + ACTIONS :],
            head[:, 2 * BINS : 2 * BINS + ACTIONS],
            blank(DEPTH - POLICY_AT - ACTIONS),
        ],
        axis=1,
    )


def gather_head(padded):
    return jnp.concatenate(
        [
            padded[:, VALUE_AT : VALUE_AT + BINS],
            padded[:, REWARD_AT : REWARD_AT + BINS],
            padded[:, POLICY_AT : POLICY_AT + ACTIONS],
            padded[:, CHANCE_AT : CHANCE_AT + CODES],
        ],
        axis=1,
    )


def send_kernel(packing, stem, up, down, head, table, norm, weight, near, far, block, send_sem, recv_sem):
    kinds = (near, far)
    partners = [(step, away) for step in packing.orders[0] for away in range(1, step[2])]
    barrier = pltpu.get_barrier_semaphore()
    for step, away in partners:
        pl.semaphore_signal(barrier, inc=1, device_id=partner_of(step, away)[0], device_id_type=MESH)

    block[...] = jnp.zeros_like(block)
    matrices = [stem[...]] + [up[layer] for layer in range(LAYERS)] + [down[layer] for layer in range(LAYERS)]
    for group in range(packing.groups):
        members = matrices[group * packing.per : (group + 1) * packing.per]
        block[group * packing.deep : (group + 1) * packing.deep, :] = pad_lanes(jnp.concatenate(members, axis=1), 128)
    padded = spread_head(head[...])
    for tile in range(DEPTH // 128):
        at = packing.head_at + packing.own * tile
        block[at : at + packing.own, :] = padded[:, tile * 128 : (tile + 1) * 128]
    at = packing.tail_at
    block[at : at + packing.own, 0:CODES] = table[...]
    for layer in range(LAYERS + 1):
        block[at + 2 * layer : at + 2 * layer + 2, NORM_LANE : NORM_LANE + packing.own] = norm[layer]
    amount = jnp.sum(jnp.sum(weight[...].astype(F32), axis=0, keepdims=True), axis=1, keepdims=True)
    amount = jnp.broadcast_to(amount, (1, 128))
    for row in range(SUM_ROW, SUM_ROW + 3):
        part = amount.astype(BF).astype(F32)
        block[at + row : at + row + 1, SUM_LANE:128] = part[:, SUM_LANE:128]
        amount = amount - part
    data, model = lax.axis_index("dp"), lax.axis_index("mp")
    slots = [slot_of(order, data, model) for order in packing.orders]
    for side in range(2):
        kinds[side][slots[side]] = block[side * packing.half : (side + 1) * packing.half, :].astype(BF)

    pl.semaphore_wait(barrier, len(partners))

    def copies_of(side, number):
        step, size = packing.orders[side][number], packing.sizes[side][number]
        held = kinds[side].at[pl.ds((slots[side] // size) * size, size)]
        return [
            pltpu.make_async_remote_copy(
                src_ref=held,
                dst_ref=held,
                send_sem=send_sem.at[side, number, away],
                recv_sem=recv_sem.at[side, number, away],
                device_id=partner_of(step, away)[0],
                device_id_type=MESH,
            )
            for away in range(1, step[2])
        ]

    steps = len(packing.orders[0])
    copies = [[copies_of(side, number) for number in range(steps)] for side in range(2)]
    for number in range(steps + 1):
        for side in range(2):
            if number:
                for member in copies[side][number - 1]:
                    member.wait_recv()
            if number < steps:
                for member in copies[side][number]:
                    member.start()
    for side in range(2):
        for number in range(steps):
            for member in copies[side][number]:
                member.wait_send()


def send_weights(packing, stem, up, down, head, table, norm, weight):
    steps = len(packing.orders[0])
    shape = jax.ShapeDtypeStruct((packing.count, packing.half, 128), BF)
    return pl.pallas_call(
        functools.partial(send_kernel, packing),
        out_shape=[shape, shape],
        in_specs=[pl.BlockSpec()] * 7,
        out_specs=[pl.BlockSpec(memory_space=pltpu.VMEM)] * 2,
        scratch_shapes=[
            pltpu.VMEM((packing.rows, 128), F32),
            pltpu.SemaphoreType.DMA((2, steps, packing.most)),
            pltpu.SemaphoreType.DMA((2, steps, packing.most)),
        ],
        compiler_params=pltpu.CompilerParams(
            collective_id=0, has_side_effects=True, vmem_limit_bytes=48 * 1024 * 1024
        ),
        name="send_weights",
    )(stem, up, down, head, table, norm, weight)


def reduce_kernel(
    packing,
    near_in,
    far_in,
    own,
    squares,
    near,
    far,
    near_out,
    far_out,
    near_got,
    far_got,
    across,
    along,
    send_sem,
    recv_sem,
    part_send,
    part_recv,
):
    steps = len(packing.orders[0])
    data, model = lax.axis_index("dp"), lax.axis_index("mp")
    barrier = pltpu.get_barrier_semaphore()
    for away in range(1, packing.mp):
        pl.semaphore_signal(barrier, inc=1, device_id={"mp": (model + away) % packing.mp}, device_id_type=MESH)
    for away in range(1, packing.dp):
        pl.semaphore_signal(barrier, inc=1, device_id={"dp": (data + away) % packing.dp}, device_id_type=MESH)

    slots = [slot_of(order, data, model) for order in packing.orders]
    given, held, sent, got = (near_in, far_in), (near, far), (near_out, far_out), (near_got, far_got)

    def source_of(side, number):
        return given[side] if number == steps - 1 else held[side]

    def mine_of(side, number):
        size = packing.sizes[side][number]
        return (slots[side] // size) * size

    def place_of(side, number, away):
        size = packing.sizes[side][number]
        return pl.ds(size * away, size)

    def pack(side, number):
        step, size = packing.orders[side][number], packing.sizes[side][number]
        for away in range(1, step[2]):
            block = mine_of(side, number) + partner_of(step, away)[1] * size
            sent[side][place_of(side, number, away)] = source_of(side, number)[pl.ds(block, size)].astype(BF)

    def copies_of(side, number):
        step = packing.orders[side][number]
        return [
            pltpu.make_async_remote_copy(
                src_ref=sent[side].at[place_of(side, number, away)],
                dst_ref=got[side].at[place_of(side, number, away)],
                send_sem=send_sem.at[side, number, away],
                recv_sem=recv_sem.at[side, number, away],
                device_id=partner_of(step, away)[0],
                device_id_type=MESH,
            )
            for away in range(1, step[2])
        ]

    def take(side, number):
        rows = pl.ds(mine_of(side, number), packing.sizes[side][number])
        total = source_of(side, number)[rows]
        for away in range(1, packing.orders[side][number][2]):
            total = total + got[side][place_of(side, number, away)].astype(F32)
        held[side][rows] = total

    copies = [[copies_of(side, number) for number in range(steps)] for side in range(2)]
    for side in range(2):
        pack(side, steps - 1)
    pl.semaphore_wait(barrier, packing.mp + packing.dp - 2)
    for number in range(steps - 1, -1, -1):
        for side in range(2):
            if number < steps - 1:
                for member in copies[side][number + 1]:
                    member.wait_recv()
                take(side, number + 1)
                pack(side, number)
            for member in copies[side][number]:
                member.start()
    total = None
    for side in range(2):
        for member in copies[side][0]:
            member.wait_recv()
        take(side, 0)
        block = held[side][slots[side]]
        own[side * packing.half : (side + 1) * packing.half, :] = block
        total = fold_rows(total, block * block)

    def exchange(axis, index, count, buffer, value, first):
        buffer[index] = value
        going = []
        for away in range(1, count):
            going.append(
                pltpu.make_async_remote_copy(
                    src_ref=buffer.at[index],
                    dst_ref=buffer.at[index],
                    send_sem=part_send.at[first + away],
                    recv_sem=part_recv.at[first + away],
                    device_id={axis: (index + away) % count},
                    device_id_type=MESH,
                )
            )
            going[-1].start()
        for member in going:
            member.wait_recv()
        whole = buffer[0]
        for other in range(1, count):
            whole = whole + buffer[other]
        return whole, going

    total, going = exchange("mp", model, packing.mp, across, total, 0)
    total, more = exchange("dp", data, packing.dp, along, total, packing.mp)
    squares[...] = total
    for member in going + more:
        member.wait_send()
    for side in range(2):
        for number in range(steps):
            for member in copies[side][number]:
                member.wait_send()


def reduce_grads(packing, near, far):
    steps = len(packing.orders[0])
    vmem = pl.BlockSpec(memory_space=pltpu.VMEM)
    return pl.pallas_call(
        functools.partial(reduce_kernel, packing),
        out_shape=[jax.ShapeDtypeStruct((packing.rows, 128), F32), jax.ShapeDtypeStruct((8, 128), F32)],
        in_specs=[vmem] * 2,
        out_specs=[vmem] * 2,
        scratch_shapes=[pltpu.VMEM((packing.count, packing.half, 128), F32)] * 2
        + [pltpu.VMEM((packing.count, packing.half, 128), BF)] * 4
        + [
            pltpu.VMEM((packing.mp, 8, 128), F32),
            pltpu.VMEM((packing.dp, 8, 128), F32),
            pltpu.SemaphoreType.DMA((2, steps, packing.most)),
            pltpu.SemaphoreType.DMA((2, steps, packing.most)),
            pltpu.SemaphoreType.DMA((packing.mp + packing.dp,)),
            pltpu.SemaphoreType.DMA((packing.mp + packing.dp,)),
        ],
        compiler_params=pltpu.CompilerParams(
            collective_id=1, has_side_effects=True, vmem_limit_bytes=60 * 1024 * 1024
        ),
        name="reduce_grads",
    )(near, far)


def adam_rows(weight, moment, square, grad, rate, decay):
    first = beta_one * moment + (1.0 - beta_one) * grad
    second = beta_two * square + (1.0 - beta_two) * grad * grad
    first_hat = first / (1.0 - beta_one**STEP)
    second_hat = second / (1.0 - beta_two**STEP)
    updated = weight - rate * (first_hat / (jnp.sqrt(second_hat) + eps_adam) + decay * weight)
    return (updated, first, second)


def update_kernel(packing, rows_all, own, squares, *refs):
    ins, outs = refs[:18], refs[18:]
    grad_norm, outs = outs[0], outs[1:]
    whole = jnp.sum(jnp.sum(squares[...], axis=0, keepdims=True), axis=1, keepdims=True)
    norm = jnp.sqrt(whole)
    grad_norm[...] = norm
    ratio = jnp.minimum(1.0, clip_scale * math.sqrt(rows_all) / norm)

    def apply(which, index, grad, rate=matrix_rate, decay=decay_rate):
        weight, moment, square = (ins[3 * which + kind][index] for kind in range(3))
        base = 4 * which
        new, first, second = adam_rows(weight, moment, square, grad * ratio, rate, decay)
        outs[base][index] = new
        outs[base + 1][index] = first
        outs[base + 2][index] = second
        if which < 5:
            outs[base + 3][index] = new.astype(BF)

    def matrix(member):
        at = (member // packing.per) * packing.deep
        lane = (member % packing.per) * packing.wide
        return own[at : at + packing.deep, lane : lane + packing.wide]

    apply(0, ..., matrix(0))
    for layer in range(LAYERS):
        apply(1, layer, matrix(1 + layer))
        apply(2, layer, matrix(1 + LAYERS + layer))
    tiles = [
        own[packing.head_at + packing.own * tile : packing.head_at + packing.own * (tile + 1), :]
        for tile in range(DEPTH // 128)
    ]
    apply(3, ..., gather_head(jnp.concatenate(tiles, axis=1)))
    at = packing.tail_at
    apply(4, ..., own[at : at + packing.own, 0:CODES])
    for layer in range(LAYERS + 1):
        apply(
            5,
            layer,
            own[at + 2 * layer : at + 2 * layer + 2, NORM_LANE : NORM_LANE + packing.own],
            vector_rate,
            0.0,
        )


def update(packing, rows_all, own, squares, groups):
    ins = [member for group in groups for member in group]
    outs = [jax.ShapeDtypeStruct((1, 1), F32)]
    for which, group in enumerate(groups):
        outs += [jax.ShapeDtypeStruct(group[0].shape, F32)] * 3
        if which < 5:
            outs.append(jax.ShapeDtypeStruct(group[0].shape, BF))
    return pl.pallas_call(
        functools.partial(update_kernel, packing, rows_all),
        out_shape=outs,
        in_specs=[pl.BlockSpec()] * (2 + len(ins)),
        out_specs=[pl.BlockSpec()] * len(outs),
        compiler_params=pltpu.CompilerParams(vmem_limit_bytes=48 * 1024 * 1024),
        name="update",
    )(own, squares, *ins)


def train_kernel(
    packing,
    rows_all,
    chains,
    lat_ref,
    code_ref,
    weight_ref,
    value_ref,
    reward_ref,
    action_ref,
    target_ref,
    near_in,
    far_in,
    lat_grad,
    near_out,
    far_out,
    stem_acc,
    table_acc,
    up_acc,
    down_acc,
    head_acc,
    stem_t,
    table_t,
    up_t,
    up_n,
    down_t,
    down_n,
    head_t,
    head_n,
    scale_s,
    wide_s,
    head_wide,
    stream_s,
    centered_s,
    slope_s,
    inner_slope_s,
    rstd_s,
    act_s,
    gated_s,
    branch_s,
    inner_grad_s,
    logit_s,
    low_s,
    top_s,
    pre_s,
    hot_s,
    norm_s,
    norm_part,
):
    step = pl.program_id(0)
    devices = [(data, model) for data in range(packing.dp) for model in range(packing.mp)]

    @pl.when(step == 0)
    def _():
        held = (near_in, far_in)

        def rows_of(device, begin, end):
            side, rows = packing.split(begin, end)
            return held[side][slot_of(packing.orders[side], *device)].astype(F32)[rows]

        for data in range(packing.dp):
            for group in range(packing.groups):
                begin = group * packing.deep
                parts = [rows_of((data, model), begin, begin + packing.deep) for model in range(packing.mp)]
                for member in range(min(packing.per, MATRICES - group * packing.per)):
                    lane = member * packing.wide
                    wide_s[group * packing.per + member, data * packing.deep : (data + 1) * packing.deep, :] = (
                        jnp.concatenate([part[:, lane : lane + packing.wide] for part in parts], axis=1)
                    )
        stem_t[...] = wide_s[0].astype(BF)
        for layer in range(LAYERS):
            half_up = 0.5 * wide_s[1 + layer]
            half_down = 0.5 * wide_s[1 + LAYERS + layer]
            up_n[layer] = half_up.astype(BF)
            up_t[layer] = half_up.T.astype(BF)
            down_t[layer] = half_down.astype(BF)
            down_n[layer] = half_down.T.astype(BF)
        norm_parts = []
        total = None
        for device in devices:
            at = (device[0] * packing.mp + device[1]) * packing.own
            for tile in range(DEPTH // 128):
                begin = packing.head_at + packing.own * tile
                head_wide[at : at + packing.own, tile * 128 : (tile + 1) * 128] = rows_of(
                    device, begin, begin + packing.own
                )
            tail = rows_of(device, packing.tail_at, packing.tail_at + 16)
            table_acc[at : at + packing.own, :] = tail[0 : packing.own, 0:CODES]
            norm_parts.append(tail[:, NORM_LANE : NORM_LANE + packing.own])
            amount = tail[SUM_ROW : SUM_ROW + 1] + tail[SUM_ROW + 1 : SUM_ROW + 2] + tail[SUM_ROW + 2 : SUM_ROW + 3]
            total = amount if total is None else total + amount
        table_t[...] = table_acc[...].astype(BF)
        head_n[...] = head_wide[...].astype(BF)
        for at in range(0, DEPTH, D):
            turned = head_wide[:, at : at + D].T.astype(BF)
            end = min(D, ROWS - at)
            head_t[at : at + end, :] = turned[0:end]
        norms = jnp.concatenate(norm_parts, axis=1)
        columns = jnp.concatenate([norms, jnp.zeros((128 - norms.shape[0], D), F32)], axis=0).T
        for which in range(2 * (LAYERS + 1)):
            norm_s[which] = jnp.broadcast_to(columns[:, which : which + 1], (D, 128))
        scale_s[...] = jnp.broadcast_to(rows_all / total[:, SUM_LANE : SUM_LANE + 1], (1, LANES))

        stem_acc[...] = jnp.zeros_like(stem_acc)
        table_acc[...] = jnp.zeros_like(table_acc)
        up_acc[...] = jnp.zeros_like(up_acc)
        down_acc[...] = jnp.zeros_like(down_acc)
        head_acc[...] = jnp.zeros_like(head_acc)
        norm_part[...] = jnp.zeros_like(norm_part)
        low_s[...] = jnp.zeros_like(low_s)

    def norm_rows(which, at):
        half = norm_s[which, at : at + CHUNK, :]
        return jnp.concatenate([half] * (LANES // 128), axis=1)

    def add_norm(which, at, part):
        total = part[:, 0:128]
        for lane in range(128, LANES, 128):
            total = total + part[:, lane : lane + 128]
        norm_part[which, at : at + CHUNK, :] += total

    def chain(index):
        cols = slice(index * LANES, (index + 1) * LANES)

        def row_of(ref):
            return ref[cols].reshape(1, LANES)

        def norm_forward(layer, total, sink):
            mean = jnp.sum(total, axis=0, keepdims=True) * (1.0 / D)
            squares = None
            for at in range(0, D, CHUNK):
                rows = slice(at, at + CHUNK)
                centered = stream_s[rows, cols] - mean
                centered_s[layer, rows, cols] = centered
                squares = fold_rows(squares, centered * centered)
            spread = jnp.sum(squares, axis=0, keepdims=True) * (1.0 / D)
            rstd = lax.rsqrt(spread + eps_norm)
            rstd_s[layer, :, cols] = rstd
            total = None
            for at in range(0, D, CHUNK):
                rows = slice(at, at + CHUNK)
                scaled = centered_s[layer, rows, cols] * rstd
                value, slope = gelu_pair(scaled * norm_rows(2 * layer, at) + norm_rows(2 * layer + 1, at))
                if sink is None:
                    value = 0.5 * value
                    slope_s[layer, rows, cols] = 0.5 * slope
                    stream_s[rows, cols] = value
                    total = fold_rows(total, value)
                else:
                    slope_s[layer, rows, cols] = slope
                    sink[layer - 1, rows, cols] = value.astype(BF)
            return total

        def norm_backward(layer, grad_of, emit):
            rstd = rstd_s[layer, :, cols]
            first = second = None
            for at in range(0, D, CHUNK):
                rows = slice(at, at + CHUNK)
                grad = grad_of(rows) * slope_s[layer, rows, cols]
                centered = centered_s[layer, rows, cols]
                add_norm(2 * layer + 1, at, grad)
                grad = grad * rstd
                add_norm(2 * layer, at, grad * centered)
                wide = grad * norm_rows(2 * layer, at)
                slope_s[layer, rows, cols] = wide
                first = fold_rows(first, wide)
                second = fold_rows(second, wide * centered)
            shift = jnp.sum(first, axis=0, keepdims=True) * (1.0 / D)
            slant = jnp.sum(second, axis=0, keepdims=True) * (1.0 / D) * (rstd * rstd)
            for at in range(0, D, CHUNK):
                rows = slice(at, at + CHUNK)
                emit(rows, (slope_s[layer, rows, cols] - shift) - centered_s[layer, rows, cols] * slant)

        hot = (lax.broadcasted_iota(jnp.int32, (CODES, LANES), 0) == row_of(code_ref)).astype(F32).astype(BF)
        hot_s[:, cols] = hot
        pre = dot_nt(stem_t[...], lat_ref[cols, :]) + dot_nn(table_t[...], hot)
        yield
        total = None
        for at in range(0, D, CHUNK):
            rows = slice(at, at + CHUNK)
            stream_s[rows, cols] = pre[rows]
            total = fold_rows(total, pre[rows])
        total = norm_forward(0, total, None)
        yield
        for layer in range(1, LAYERS + 1):
            norm_forward(layer, total, act_s)
            yield
            inner = dot_nn(up_t[layer - 1], act_s[layer - 1, :, cols])
            yield
            for at in range(0, D, CHUNK):
                rows = slice(at, at + CHUNK)
                value, slope = gelu_pair(inner[rows])
                inner_slope_s[layer - 1, rows, cols] = slope
                gated_s[layer - 1, rows, cols] = value.astype(BF)
            yield
            branch = dot_nn(down_t[layer - 1], gated_s[layer - 1, :, cols])
            yield
            total = None
            for at in range(0, D, CHUNK):
                rows = slice(at, at + CHUNK)
                stream = stream_s[rows, cols] + branch[rows]
                if layer < LAYERS:
                    stream_s[rows, cols] = stream
                    total = fold_rows(total, stream)
                else:
                    top_s[rows, cols] = stream.astype(BF)
        yield
        logit_s[:, cols] = dot_nn(head_t[...], top_s[:, cols])
        yield
        coef = row_of(weight_ref).astype(F32) * scale_s[...]
        sections = (
            (VALUE_AT, BINS, value_ref),
            (REWARD_AT, BINS, reward_ref),
            (CHANCE_AT, CODES, target_ref),
            (POLICY_AT, ACTIONS, action_ref),
        )
        for begin, count, target_ref_of in sections:
            padded = -(-count // 8) * 8
            if padded != count:
                last = slice(begin + padded - 8, begin + padded)
                keep = lax.broadcasted_iota(jnp.int32, (8, LANES), 0) < count - (padded - 8)
                logit_s[last, cols] = jnp.where(keep, logit_s[last, cols], -1e30)
            peak = None
            for at in range(0, padded, CHUNK):
                rows = slice(begin + at, begin + min(at + CHUNK, padded))
                peak = peak_rows(peak, logit_s[rows, cols])
            peak = jnp.max(peak, axis=0, keepdims=True)
            mass = None
            for at in range(0, padded, CHUNK):
                rows = slice(begin + at, begin + min(at + CHUNK, padded))
                power = jnp.exp2((logit_s[rows, cols] - peak) * LOG2E)
                logit_s[rows, cols] = power
                mass = fold_rows(mass, power)
            scale = coef / jnp.sum(mass, axis=0, keepdims=True)
            target = row_of(target_ref_of)
            stored = -(-count // 16) * 16
            for at in range(0, padded, CHUNK):
                end = min(at + CHUNK, padded)
                rows = slice(begin + at, begin + end)
                soft = logit_s[rows, cols] * scale
                place = lax.broadcasted_iota(jnp.int32, soft.shape, 0) + at
                soft = jnp.where(place == target, soft - coef, soft)
                if end == padded and padded != stored:
                    soft = jnp.concatenate([soft, jnp.zeros((stored - padded, LANES), F32)], axis=0)
                    rows = slice(begin + at, begin + stored)
                low_s[rows, cols] = soft.astype(BF)
            yield
        grad = dot_nn(head_n[...], low_s[:, cols])
        yield
        if index == chains - 1:
            head_acc[...] += dot_nt(low_s[0:ROWS, :], top_s[...])
        for layer in range(LAYERS, 0, -1):
            if layer == LAYERS:
                for at in range(0, D, CHUNK):
                    rows = slice(at, at + CHUNK)
                    stream_s[rows, cols] = grad[rows]
                    branch_s[layer - 1, rows, cols] = grad[rows].astype(BF)
            yield
            gated_grad = dot_nn(down_n[layer - 1], branch_s[layer - 1, :, cols])
            yield
            for at in range(0, D, CHUNK):
                rows = slice(at, at + CHUNK)
                inner_grad_s[layer - 1, rows, cols] = (
                    gated_grad[rows] * inner_slope_s[layer - 1, rows, cols]
                ).astype(BF)
            yield
            active_grad = dot_nn(up_n[layer - 1], inner_grad_s[layer - 1, :, cols])
            if index == chains - 1:
                down_acc[layer - 1] += dot_nt(branch_s[layer - 1], gated_s[layer - 1])
                up_acc[layer - 1] += dot_nt(act_s[layer - 1], inner_grad_s[layer - 1])
            yield

            def emit(rows, change, layer=layer):
                stream = stream_s[rows, cols] + change
                stream_s[rows, cols] = stream
                if layer > 1:
                    branch_s[layer - 2, rows, cols] = stream.astype(BF)

            norm_backward(layer, lambda rows: active_grad[rows], emit)
            yield

        def emit_pre(rows, change):
            pre_s[rows, cols] = change.astype(BF)

        norm_backward(0, lambda rows: stream_s[rows, cols], emit_pre)
        yield
        lat_grad[cols, :] = dot_tn(pre_s[:, cols], stem_t[...])
        yield

    running = []
    waiting = [chain(index) for index in range(chains)]
    while running or waiting:
        if waiting:
            running.append(waiting.pop(0))
        for member in list(running):
            try:
                next(member)
            except StopIteration:
                running.remove(member)

    stem_acc[...] += dot_nn(pre_s[...], lat_ref[...])
    table_acc[...] += dot_nt(pre_s[...], hot_s[...])

    @pl.when(step == pl.num_programs(0) - 1)
    def _():
        outs = (near_out, far_out)
        near_out[...] = jnp.zeros_like(near_out)
        far_out[...] = jnp.zeros_like(far_out)
        for at in range(0, DEPTH, D):
            end = min(D, ROWS - at)
            turned = head_acc[at : at + end, :]
            if end < D:
                turned = jnp.concatenate([turned, jnp.zeros((D - end, D), F32)], axis=0)
            head_wide[:, at : at + D] = turned.T
        lane_at = lax.broadcasted_iota(jnp.int32, (D, 128), 1)
        columns = jnp.zeros((D, 128), F32)
        for which in range(2 * (LAYERS + 1)):
            columns = jnp.where(lane_at == which, jnp.sum(norm_part[which], axis=1, keepdims=True), columns)
        norms = columns.T[0:16]
        for device in devices:
            data, model = device
            at = (data * packing.mp + model) * packing.own
            slots = [slot_of(order, data, model) for order in packing.orders]

            def keep(begin, value, lanes=slice(0, 128)):
                side, rows = packing.split(begin, begin + value.shape[0])
                outs[side][slots[side], rows, lanes] = value

            deep = slice(data * packing.deep, (data + 1) * packing.deep)
            wide = slice(model * packing.wide, (model + 1) * packing.wide)
            pieces = [stem_acc[deep, wide]] + [0.5 * up_acc[layer, deep, wide] for layer in range(LAYERS)]
            pieces += [0.5 * down_acc[layer, deep, wide] for layer in range(LAYERS)]
            for group in range(packing.groups):
                members = pieces[group * packing.per : (group + 1) * packing.per]
                keep(group * packing.deep, pad_lanes(jnp.concatenate(members, axis=1), 128))
            for tile in range(DEPTH // 128):
                keep(
                    packing.head_at + packing.own * tile,
                    head_wide[at : at + packing.own, tile * 128 : (tile + 1) * 128],
                )
            keep(packing.tail_at, table_acc[at : at + packing.own, :], slice(0, CODES))
            keep(
                packing.tail_at,
                norms[0 : 2 * (LAYERS + 1), at : at + packing.own],
                slice(NORM_LANE, NORM_LANE + packing.own),
            )


def train(packing, rows_all, latent, code, weight, value, reward, action, target, near, far):
    count = latent.shape[0]
    chains = CHAINS
    block = chains * LANES

    def full(shape):
        return pl.BlockSpec(shape, lambda i: (0,) * len(shape), pipeline_mode=pl.Buffered(1))

    def row():
        return pl.BlockSpec((block,), lambda i: (i,))

    packed = (packing.count, packing.half, 128)
    return pl.pallas_call(
        functools.partial(train_kernel, packing, rows_all, chains),
        grid=(count // block,),
        out_shape=[
            jax.ShapeDtypeStruct((count, D), F32),
            jax.ShapeDtypeStruct(packed, F32),
            jax.ShapeDtypeStruct(packed, F32),
        ],
        in_specs=[pl.BlockSpec((block, D), lambda i: (i, 0))] + [row() for _ in range(6)] + [full(packed)] * 2,
        out_specs=[pl.BlockSpec((block, D), lambda i: (i, 0))] + [full(packed)] * 2,
        scratch_shapes=[
            pltpu.VMEM((D, D), F32),
            pltpu.VMEM((D, CODES), F32),
            pltpu.VMEM((LAYERS, D, D), F32),
            pltpu.VMEM((LAYERS, D, D), F32),
            pltpu.VMEM((ROWS, D), F32),
            pltpu.VMEM((D, D), BF),
            pltpu.VMEM((D, CODES), BF),
            pltpu.VMEM((LAYERS, D, D), BF),
            pltpu.VMEM((LAYERS, D, D), BF),
            pltpu.VMEM((LAYERS, D, D), BF),
            pltpu.VMEM((LAYERS, D, D), BF),
            pltpu.VMEM((ROWS, D), BF),
            pltpu.VMEM((D, DEPTH), BF),
            pltpu.VMEM((1, LANES), F32),
            pltpu.VMEM((MATRICES, D, D), F32),
            pltpu.VMEM((D, DEPTH), F32),
            pltpu.VMEM((D, block), F32),
            pltpu.VMEM((LAYERS + 1, D, block), F32),
            pltpu.VMEM((LAYERS + 1, D, block), F32),
            pltpu.VMEM((LAYERS, D, block), F32),
            pltpu.VMEM((LAYERS + 1, 1, block), F32),
            pltpu.VMEM((LAYERS, D, block), BF),
            pltpu.VMEM((LAYERS, D, block), BF),
            pltpu.VMEM((LAYERS, D, block), BF),
            pltpu.VMEM((LAYERS, D, block), BF),
            pltpu.VMEM((ROWS, block), F32),
            pltpu.VMEM((DEPTH, block), BF),
            pltpu.VMEM((D, block), BF),
            pltpu.VMEM((D, block), BF),
            pltpu.VMEM((CODES, block), BF),
            pltpu.VMEM((2 * (LAYERS + 1), D, 128), F32),
            pltpu.VMEM((2 * (LAYERS + 1), D, 128), F32),
        ],
        compiler_params=pltpu.CompilerParams(
            dimension_semantics=("arbitrary",), vmem_limit_bytes=60 * 1024 * 1024
        ),
        name="train",
    )(latent, code, weight, value, reward, action, target, near, far)


def body(rows_all, packing, *args):
    latent, code, weight, value, reward, action, target = args[:7]
    groups = [args[7 + 3 * which : 10 + 3 * which] for which in range(6)]

    def turn(which, array):
        return jnp.swapaxes(array, -1, -2) if which in (0, 2, 4) else array

    groups = [tuple(turn(which, member) for member in group) for which, group in enumerate(groups)]
    stem, up, down, head, table, norm = (group[0] for group in groups)
    near, far = send_weights(packing, stem, up, down, head, table, norm, weight.reshape(-1, 128))
    lat_grad, near, far = train(packing, rows_all, latent, code, weight, value, reward, action, target, near, far)
    own, squares = reduce_grads(packing, near, far)
    outs = update(packing, rows_all, own, squares, groups)
    result = [outs[0].reshape(()), lat_grad]
    at = 1
    for which in range(6):
        for _ in range(4 if which < 5 else 3):
            result.append(turn(which, outs[at]))
            at += 1
    return tuple(result)


def solution(mesh):
    every = ("dp", "mp")
    states, flat = P(every, None), P(every)
    params = (P("mp", "dp"), P(None, "dp", "mp"), P(None, "mp", "dp"), P(every, None), P(None, every), P(None, None, every))
    in_specs = (states,) + (flat,) * 6 + tuple(spec for spec in params for _ in range(3))
    out_specs = (P(), states) + tuple(spec for which, spec in enumerate(params) for _ in range(4 if which < 5 else 3))
    packing = Packing(mesh.shape["dp"], mesh.shape["mp"])

    def run(*args):
        rows_all = args[0].shape[0] * packing.count
        return body(rows_all, packing, *args)

    return jax.shard_map(run, mesh=mesh, in_specs=in_specs, out_specs=out_specs, check_vma=False)
```

```python
import math
import functools

import jax
import jax.numpy as jnp
from jax import lax
from jax.experimental import pallas as pl
from jax.experimental.pallas import tpu as pltpu
from jax.sharding import PartitionSpec as P

D = 256
BINS = 601
ACTIONS = 4
CODES = 32
LAYERS = 4
STEP = 10

VALUE_AT = 0
REWARD_AT = 608
CHANCE_AT = 1216
POLICY_AT = 1248
ROWS = 1264
DEPTH = 1280

beta_one = 0.9
beta_two = 0.99
eps_adam = 1e-08
eps_norm = 1e-05
matrix_rate = 0.2
vector_rate = 0.6
decay_rate = 0.1
clip_scale = 3.0

GELU_A = math.sqrt(2.0 / math.pi)
GELU_B = GELU_A * 0.044715
LOG2E = 1.4426950408889634
LANES = 256
CHAINS = 4
PARTS = 4
UNIT, DELAY, STAGGER = 90, 250, 200
CHUNK = 32
BF = jnp.bfloat16
F32 = jnp.float32
MESH = pl.DeviceIdType.MESH
MATRICES = 1 + 2 * LAYERS
NORM_LANE = 32
SUM_LANE = 64
SUM_ROW = 10


def dot_nn(left, right):
    return lax.dot_general(left, right, (((1,), (0,)), ((), ())), preferred_element_type=F32)


def dot_nt(left, right):
    return lax.dot_general(left, right, (((1,), (1,)), ((), ())), preferred_element_type=F32)


def dot_tn(left, right):
    return lax.dot_general(left, right, (((0,), (0,)), ((), ())), preferred_element_type=F32)


def gelu_pair(v):
    square = v * v
    gate = 1.0 + jnp.tanh(v * (GELU_A + GELU_B * square))
    value = v * gate
    slope = gate + value * (2.0 - gate) * (GELU_A + 3.0 * GELU_B * square)
    return value, slope


def fold_rows(total, part):
    for at in range(0, part.shape[0], 8):
        piece = part[at : at + 8]
        total = piece if total is None else total + piece
    return total


def peak_rows(total, part):
    for at in range(0, part.shape[0], 8):
        piece = part[at : at + 8]
        total = piece if total is None else jnp.maximum(total, piece)
    return total


def orders_of(dp, mp):
    def step(axis, low, size):
        return (axis, low, size) if size > 1 else None

    far_dp, near_dp = step("dp", 2, dp // 2), step("dp", 1, 2)
    far_mp, near_mp = step("mp", 2, mp // 2), step("mp", 1, 2)
    return (
        [member for member in (far_dp, near_dp, far_mp, near_mp) if member],
        [member for member in (far_dp, far_mp, near_dp, near_mp) if member],
    )


def digit_of(step, data, model):
    axis, low, ways = step
    return ((data if axis == "dp" else model) // low) % ways


def slot_of(order, data, model):
    place, weight = 0, 1
    for step in order:
        place = place + digit_of(step, data, model) * weight
        weight *= step[2]
    return place


def partner_of(step, away):
    axis, low, ways = step
    index = lax.axis_index(axis)
    digit = (index // low) % ways
    other = (digit + away) % ways
    return {axis: index + (other - digit) * low}, other - digit


def sizes_of(order):
    sizes = [1]
    for step in order:
        sizes.append(sizes[-1] * step[2])
    return sizes


class Packing:
    def __init__(self, dp, mp):
        self.dp, self.mp, self.count = dp, mp, dp * mp
        self.deep, self.wide, self.own = D // dp, D // mp, D // (dp * mp)
        self.per = 128 // self.wide
        self.groups = -(-MATRICES // self.per)
        self.head_at = self.groups * self.deep
        self.tail_at = -(-(self.head_at + self.own * (DEPTH // 128)) // 16) * 16
        self.rows = -(-(self.tail_at + 16) // (16 * PARTS)) * 16 * PARTS
        self.part = self.rows // PARTS
        self.orders = [orders_of(dp, mp)[number % 2] for number in range(PARTS)]
        self.sizes = [sizes_of(order) for order in self.orders]
        self.most = max(step[2] for step in self.orders[0])

    def split(self, begin, end):
        side = begin // self.part
        assert (end - 1) // self.part == side
        return side, slice(begin - side * self.part, end - side * self.part)

    def shapes(self, dtype):
        return [jax.ShapeDtypeStruct((self.count, self.part, 128), dtype)] * PARTS

    def scratch(self, dtype):
        return [pltpu.VMEM((self.count, self.part, 128), dtype)] * PARTS


def pad_lanes(array, lanes):
    missing = lanes - array.shape[1]
    return array if missing == 0 else jnp.concatenate([array, jnp.zeros((array.shape[0], missing), array.dtype)], axis=1)


def spread_head(head):
    rows = head.shape[0]

    def blank(count):
        return jnp.zeros((rows, count), head.dtype)

    return jnp.concatenate(
        [
            head[:, :BINS],
            blank(REWARD_AT - BINS),
            head[:, BINS : 2 * BINS],
            blank(CHANCE_AT - REWARD_AT - BINS),
            head[:, 2 * BINS + ACTIONS :],
            head[:, 2 * BINS : 2 * BINS + ACTIONS],
            blank(DEPTH - POLICY_AT - ACTIONS),
        ],
        axis=1,
    )


def gather_head(padded):
    return jnp.concatenate(
        [
            padded[:, VALUE_AT : VALUE_AT + BINS],
            padded[:, REWARD_AT : REWARD_AT + BINS],
            padded[:, POLICY_AT : POLICY_AT + ACTIONS],
            padded[:, CHANCE_AT : CHANCE_AT + CODES],
        ],
        axis=1,
    )


def send_kernel(packing, *refs):
    stem, up, down, head, table, norm, weight = refs[:7]
    outs, kinds = refs[7 : 7 + PARTS], refs[7 + PARTS : 7 + 2 * PARTS]
    block, send_sem, recv_sem, keep_sem = refs[7 + 2 * PARTS :]
    partners = [(step, away) for step in packing.orders[0] for away in range(1, step[2])]
    barrier = pltpu.get_barrier_semaphore()
    for step, away in partners:
        pl.semaphore_signal(barrier, inc=1, device_id=partner_of(step, away)[0], device_id_type=MESH)

    block[...] = jnp.zeros_like(block)
    matrices = [stem[...]] + [up[layer] for layer in range(LAYERS)] + [down[layer] for layer in range(LAYERS)]
    for group in range(packing.groups):
        members = matrices[group * packing.per : (group + 1) * packing.per]
        block[group * packing.deep : (group + 1) * packing.deep, :] = pad_lanes(jnp.concatenate(members, axis=1), 128)
    padded = spread_head(head[...])
    for tile in range(DEPTH // 128):
        at = packing.head_at + packing.own * tile
        block[at : at + packing.own, :] = padded[:, tile * 128 : (tile + 1) * 128]
    at = packing.tail_at
    block[at : at + packing.own, 0:CODES] = table[...]
    for layer in range(LAYERS + 1):
        block[at + 2 * layer : at + 2 * layer + 2, NORM_LANE : NORM_LANE + packing.own] = norm[layer]
    amount = jnp.sum(jnp.sum(weight[...].astype(F32), axis=0, keepdims=True), axis=1, keepdims=True)
    amount = jnp.broadcast_to(amount, (1, 128))
    for row in range(SUM_ROW, SUM_ROW + 3):
        part = amount.astype(BF).astype(F32)
        block[at + row : at + row + 1, SUM_LANE:128] = part[:, SUM_LANE:128]
        amount = amount - part
    data, model = lax.axis_index("dp"), lax.axis_index("mp")
    slots = [slot_of(order, data, model) for order in packing.orders]
    for side in range(PARTS):
        kinds[side][slots[side]] = block[side * packing.part : (side + 1) * packing.part, :].astype(BF)

    pl.semaphore_wait(barrier, len(partners))

    def copies_of(side, number):
        step, size = packing.orders[side][number], packing.sizes[side][number]
        held = kinds[side].at[pl.ds((slots[side] // size) * size, size)]
        return [
            pltpu.make_async_remote_copy(
                src_ref=held,
                dst_ref=held,
                send_sem=send_sem.at[side, number, away],
                recv_sem=recv_sem.at[side, number, away],
                device_id=partner_of(step, away)[0],
                device_id_type=MESH,
            )
            for away in range(1, step[2])
        ]

    def kept(side, start, size, sem):
        return pltpu.make_async_copy(
            kinds[side].at[pl.ds(start, size)], outs[side].at[pl.ds(start, size)], keep_sem.at[side, sem]
        )

    steps = len(packing.orders[0])
    copies = [[copies_of(side, number) for number in range(steps)] for side in range(PARTS)]
    local = [kept(side, slots[side], 1, 0) for side in range(PARTS)]
    for member in local:
        member.start()
    for number in range(steps + 1):
        for side in range(PARTS):
            if number:
                for member in copies[side][number - 1]:
                    member.wait_recv()
            if number < steps:
                for member in copies[side][number]:
                    member.start()
            if number:
                step, size = packing.orders[side][number - 1], packing.sizes[side][number - 1]
                for away in range(1, step[2]):
                    start = (slots[side] // size) * size + partner_of(step, away)[1] * size
                    local.append(kept(side, start, size, number * packing.most + away))
                    local[-1].start()
    for member in local:
        member.wait()
    for side in range(PARTS):
        for number in range(steps):
            for member in copies[side][number]:
                member.wait_send()


def send_weights(packing, stem, up, down, head, table, norm, weight):
    steps = len(packing.orders[0])
    return pl.pallas_call(
        functools.partial(send_kernel, packing),
        out_shape=packing.shapes(BF),
        in_specs=[pl.BlockSpec()] * 7,
        out_specs=[pl.BlockSpec(memory_space=pl.ANY)] * PARTS,
        scratch_shapes=packing.scratch(BF)
        + [
            pltpu.VMEM((packing.rows, 128), F32),
            pltpu.SemaphoreType.DMA((PARTS, steps, packing.most)),
            pltpu.SemaphoreType.DMA((PARTS, steps, packing.most)),
            pltpu.SemaphoreType.DMA((PARTS, (steps + 1) * packing.most)),
        ],
        compiler_params=pltpu.CompilerParams(
            collective_id=0, has_side_effects=True, vmem_limit_bytes=60 * 1024 * 1024
        ),
        name="send_weights",
    )(stem, up, down, head, table, norm, weight)


def reduce_kernel(packing, *refs):
    given, own = refs[:PARTS], refs[PARTS]
    held, sent, got = (refs[PARTS * kind + 1 : PARTS * (kind + 1) + 1] for kind in (1, 2, 3))
    across, along, send_sem, recv_sem, part_send, part_recv = refs[4 * PARTS + 1 :]
    steps = len(packing.orders[0])
    data, model = lax.axis_index("dp"), lax.axis_index("mp")
    barrier = pltpu.get_barrier_semaphore()
    for away in range(1, packing.mp):
        pl.semaphore_signal(barrier, inc=1, device_id={"mp": (model + away) % packing.mp}, device_id_type=MESH)
    for away in range(1, packing.dp):
        pl.semaphore_signal(barrier, inc=1, device_id={"dp": (data + away) % packing.dp}, device_id_type=MESH)

    slots = [slot_of(order, data, model) for order in packing.orders]

    def source_of(side, number):
        return given[side] if number == steps - 1 else held[side]

    def mine_of(side, number):
        size = packing.sizes[side][number]
        return (slots[side] // size) * size

    def place_of(side, number, away):
        size = packing.sizes[side][number]
        return pl.ds(size * away, size)

    def pack(side, number):
        step, size = packing.orders[side][number], packing.sizes[side][number]
        for away in range(1, step[2]):
            block = mine_of(side, number) + partner_of(step, away)[1] * size
            sent[side][place_of(side, number, away)] = source_of(side, number)[pl.ds(block, size)].astype(BF)

    def copies_of(side, number):
        step = packing.orders[side][number]
        return [
            pltpu.make_async_remote_copy(
                src_ref=sent[side].at[place_of(side, number, away)],
                dst_ref=got[side].at[place_of(side, number, away)],
                send_sem=send_sem.at[side, number, away],
                recv_sem=recv_sem.at[side, number, away],
                device_id=partner_of(step, away)[0],
                device_id_type=MESH,
            )
            for away in range(1, step[2])
        ]

    def take(side, number):
        rows = pl.ds(mine_of(side, number), packing.sizes[side][number])
        total = source_of(side, number)[rows]
        for away in range(1, packing.orders[side][number][2]):
            total = total + got[side][place_of(side, number, away)].astype(F32)
        held[side][rows] = total

    copies = [[copies_of(side, number) for number in range(steps)] for side in range(PARTS)]
    for side in range(PARTS):
        pack(side, steps - 1)
    pl.semaphore_wait(barrier, packing.mp + packing.dp - 2)
    for number in range(steps - 1, -1, -1):
        for side in range(PARTS):
            if number < steps - 1:
                for member in copies[side][number + 1]:
                    member.wait_recv()
                take(side, number + 1)
                pack(side, number)
            for member in copies[side][number]:
                member.start()
    total = None
    for side in range(PARTS):
        for member in copies[side][0]:
            member.wait_recv()
        take(side, 0)
        block = held[side][slots[side]]
        own[side * packing.part : (side + 1) * packing.part, :] = block
        total = fold_rows(total, block * block)

    def exchange(axis, index, count, buffer, value, first):
        buffer[index] = value
        going = []
        for away in range(1, count):
            going.append(
                pltpu.make_async_remote_copy(
                    src_ref=buffer.at[index],
                    dst_ref=buffer.at[index],
                    send_sem=part_send.at[first + away],
                    recv_sem=part_recv.at[first + away],
                    device_id={axis: (index + away) % count},
                    device_id_type=MESH,
                )
            )
            going[-1].start()
        for member in going:
            member.wait_recv()
        whole = buffer[0]
        for other in range(1, count):
            whole = whole + buffer[other]
        return whole, going

    total, going = exchange("mp", model, packing.mp, across, total, 0)
    total, more = exchange("dp", data, packing.dp, along, total, packing.mp)
    own[packing.rows : packing.rows + 8, :] = total
    for member in going + more:
        member.wait_send()
    for side in range(PARTS):
        for number in range(steps):
            for member in copies[side][number]:
                member.wait_send()


def reduce_grads(packing, grads):
    steps = len(packing.orders[0])
    vmem = pl.BlockSpec(memory_space=pltpu.VMEM)
    return pl.pallas_call(
        functools.partial(reduce_kernel, packing),
        out_shape=jax.ShapeDtypeStruct((packing.rows + 8, 128), F32),
        in_specs=[vmem] * PARTS,
        out_specs=vmem,
        scratch_shapes=packing.scratch(F32)
        + packing.scratch(BF) * 2
        + [
            pltpu.VMEM((packing.mp, 8, 128), F32),
            pltpu.VMEM((packing.dp, 8, 128), F32),
            pltpu.SemaphoreType.DMA((PARTS, steps, packing.most)),
            pltpu.SemaphoreType.DMA((PARTS, steps, packing.most)),
            pltpu.SemaphoreType.DMA((packing.mp + packing.dp,)),
            pltpu.SemaphoreType.DMA((packing.mp + packing.dp,)),
        ],
        compiler_params=pltpu.CompilerParams(
            collective_id=1, has_side_effects=True, vmem_limit_bytes=60 * 1024 * 1024
        ),
        name="reduce_grads",
    )(*grads)


def adam_rows(weight, moment, square, grad, rate, decay):
    first = beta_one * moment + (1.0 - beta_one) * grad
    second = beta_two * square + (1.0 - beta_two) * grad * grad
    first_hat = first / (1.0 - beta_one**STEP)
    second_hat = second / (1.0 - beta_two**STEP)
    updated = weight - rate * (first_hat / (jnp.sqrt(second_hat) + eps_adam) + decay * weight)
    return (updated, first, second)


def update_kernel(packing, rows_all, own, *refs):
    ins, outs = refs[:18], refs[18:]
    grad_norm, outs = outs[0], outs[1:]
    squares = own[packing.rows : packing.rows + 8, :]
    whole = jnp.sum(jnp.sum(squares, axis=0, keepdims=True), axis=1, keepdims=True)
    norm = jnp.sqrt(whole)
    grad_norm[...] = norm
    ratio = jnp.minimum(1.0, clip_scale * math.sqrt(rows_all) / norm)

    def apply(which, index, grad, rate=matrix_rate, decay=decay_rate):
        weight, moment, square = (ins[3 * which + kind][index] for kind in range(3))
        base = 4 * which
        new, first, second = adam_rows(weight, moment, square, grad * ratio, rate, decay)
        outs[base][index] = new
        outs[base + 1][index] = first
        outs[base + 2][index] = second
        if which < 5:
            outs[base + 3][index] = new.astype(BF)

    def matrix(member):
        at = (member // packing.per) * packing.deep
        lane = (member % packing.per) * packing.wide
        return own[at : at + packing.deep, lane : lane + packing.wide]

    apply(0, ..., matrix(0))
    for layer in range(LAYERS):
        apply(1, layer, matrix(1 + layer))
        apply(2, layer, matrix(1 + LAYERS + layer))
    tiles = [
        own[packing.head_at + packing.own * tile : packing.head_at + packing.own * (tile + 1), :]
        for tile in range(DEPTH // 128)
    ]
    apply(3, ..., gather_head(jnp.concatenate(tiles, axis=1)))
    at = packing.tail_at
    apply(4, ..., own[at : at + packing.own, 0:CODES])
    for layer in range(LAYERS + 1):
        apply(
            5,
            layer,
            own[at + 2 * layer : at + 2 * layer + 2, NORM_LANE : NORM_LANE + packing.own],
            vector_rate,
            0.0,
        )


def update(packing, rows_all, own, groups):
    ins = [member for group in groups for member in group]
    outs = [jax.ShapeDtypeStruct((1, 1), F32)]
    for which, group in enumerate(groups):
        outs += [jax.ShapeDtypeStruct(group[0].shape, F32)] * 3
        if which < 5:
            outs.append(jax.ShapeDtypeStruct(group[0].shape, BF))
    return pl.pallas_call(
        functools.partial(update_kernel, packing, rows_all),
        out_shape=outs,
        in_specs=[pl.BlockSpec()] * (1 + len(ins)),
        out_specs=[pl.BlockSpec()] * len(outs),
        compiler_params=pltpu.CompilerParams(vmem_limit_bytes=48 * 1024 * 1024),
        name="update",
    )(own, *ins)


def train_kernel(
    packing,
    rows_all,
    chains,
    lat_ref,
    code_ref,
    weight_ref,
    value_ref,
    reward_ref,
    action_ref,
    target_ref,
    *refs,
):
    held, lat_grad, outs = refs[:PARTS], refs[PARTS], refs[PARTS + 1 : 2 * PARTS + 1]
    (
    stem_acc,
    table_acc,
    up_acc,
    down_acc,
    head_acc,
    stem_t,
    table_t,
    up_t,
    up_n,
    down_t,
    down_n,
    head_t,
    head_n,
    scale_s,
    stream_s,
    centered_s,
    slope_s,
    inner_slope_s,
    rstd_s,
    act_s,
    gated_s,
    branch_s,
    inner_grad_s,
    logit_s,
    low_s,
    top_s,
    pre_s,
    hot_s,
    norm_s,
    norm_part,
    ) = refs[2 * PARTS + 1 : -1]
    step = pl.program_id(0)
    tiles_wide = logit_s.shape[1] // 128
    chunks = packing.count * packing.part // D
    copy_sem = refs[-1]

    def chunk_at(buffers, chunk):
        layers = buffers[0].shape[0]
        which, chunk = divmod(chunk, layers * tiles_wide)
        layer, tile = divmod(chunk, tiles_wide)
        return buffers[which].at[layer, :, tile * 128 : (tile + 1) * 128]

    def packed_at(buffers, side, slot):
        chunk, row = divmod(slot * packing.part, D)
        return chunk_at(buffers, side * chunks + chunk), row

    def head_tile(tile):
        return (
            slice((tile // tiles_wide) * D, (tile // tiles_wide + 1) * D),
            slice((tile % tiles_wide) * 128, (tile % tiles_wide + 1) * 128),
        )

    devices = [(data, model) for data in range(packing.dp) for model in range(packing.mp)]

    @pl.when(step == 0)
    def _():
        arrived = [
            pltpu.make_async_copy(
                held[side].at[chunk * D : (chunk + 1) * D],
                chunk_at((act_s, gated_s), side * chunks + chunk),
                copy_sem.at[side, chunk],
            )
            for side in range(PARTS)
            for chunk in range(chunks)
        ]
        for member in arrived:
            member.start()
        for member in arrived:
            member.wait()

        def rows_of(device, begin, end):
            side, rows = packing.split(begin, end)
            place, row = packed_at((act_s, gated_s), side, slot_of(packing.orders[side], *device))
            return place[row : row + packing.part, :].astype(F32)[rows]

        wide_s = [stem_acc] + [up_acc.at[layer] for layer in range(LAYERS)] + [down_acc.at[layer] for layer in range(LAYERS)]
        for data in range(packing.dp):
            for group in range(packing.groups):
                begin = group * packing.deep
                parts = [rows_of((data, model), begin, begin + packing.deep) for model in range(packing.mp)]
                for member in range(min(packing.per, MATRICES - group * packing.per)):
                    lane = member * packing.wide
                    wide_s[group * packing.per + member][data * packing.deep : (data + 1) * packing.deep, :] = (
                        jnp.concatenate([part[:, lane : lane + packing.wide] for part in parts], axis=1)
                    )
        stem_t[...] = wide_s[0][...].astype(BF)
        for layer in range(LAYERS):
            half_up = 0.5 * wide_s[1 + layer][...]
            half_down = 0.5 * wide_s[1 + LAYERS + layer][...]
            up_n[layer] = half_up.astype(BF)
            up_t[layer] = half_up.T.astype(BF)
            down_t[layer] = half_down.astype(BF)
            down_n[layer] = half_down.T.astype(BF)
        norm_parts = []
        total = None
        for device in devices:
            at = (device[0] * packing.mp + device[1]) * packing.own
            for tile in range(DEPTH // 128):
                begin = packing.head_at + packing.own * tile
                rows, lanes = head_tile(tile)
                logit_s[rows.start + at : rows.start + at + packing.own, lanes] = rows_of(
                    device, begin, begin + packing.own
                )
            tail = rows_of(device, packing.tail_at, packing.tail_at + 16)
            table_acc[at : at + packing.own, :] = tail[0 : packing.own, 0:CODES]
            norm_parts.append(tail[:, NORM_LANE : NORM_LANE + packing.own])
            amount = tail[SUM_ROW : SUM_ROW + 1] + tail[SUM_ROW + 1 : SUM_ROW + 2] + tail[SUM_ROW + 2 : SUM_ROW + 3]
            total = amount if total is None else total + amount
        table_t[...] = table_acc[...].astype(BF)
        for tile in range(DEPTH // 128):
            at = tile * 128
            whole = logit_s[head_tile(tile)]
            head_n[:, at : at + 128] = whole.astype(BF)
            end = min(128, ROWS - at)
            head_t[at : at + end, :] = whole.T.astype(BF)[0:end]
        norms = jnp.concatenate(norm_parts, axis=1)
        columns = jnp.concatenate([norms, jnp.zeros((128 - norms.shape[0], D), F32)], axis=0).T
        for which in range(2 * (LAYERS + 1)):
            norm_s[which] = jnp.broadcast_to(columns[:, which : which + 1], (D, 128))
        scale_s[...] = jnp.broadcast_to(rows_all / total[:, SUM_LANE : SUM_LANE + 1], (1, LANES))

        stem_acc[...] = jnp.zeros_like(stem_acc)
        table_acc[...] = jnp.zeros_like(table_acc)
        up_acc[...] = jnp.zeros_like(up_acc)
        down_acc[...] = jnp.zeros_like(down_acc)
        head_acc[...] = jnp.zeros_like(head_acc)
        norm_part[...] = jnp.zeros_like(norm_part)
        low_s[...] = jnp.zeros_like(low_s)

    def norm_rows(which, at):
        half = norm_s[which, at : at + CHUNK, :]
        return jnp.concatenate([half] * (LANES // 128), axis=1)

    def add_norm(which, at, part):
        total = part[:, 0:128]
        for lane in range(128, LANES, 128):
            total = total + part[:, lane : lane + 128]
        norm_part[which, at : at + CHUNK, :] += total

    def spans(count):
        return [slice(at, min(at + CHUNK, count)) for at in range(0, count, CHUNK)]

    def chain(index):
        cols = slice(index * LANES, (index + 1) * LANES)

        def row_of(ref):
            return ref[cols].reshape(1, LANES)

        def norm_forward(layer, total, sink):
            mean = jnp.sum(total, axis=0, keepdims=True) * (1.0 / D)
            yield "wait", 40
            squares = None
            for rows in spans(D):
                centered = stream_s[rows, cols] - mean
                centered_s[layer, rows, cols] = centered
                squares = fold_rows(squares, centered * centered)
                yield "vector", 3
            spread = jnp.sum(squares, axis=0, keepdims=True) * (1.0 / D)
            rstd = lax.rsqrt(spread + eps_norm)
            rstd_s[layer, :, cols] = rstd
            yield "wait", 60
            total = None
            for rows in spans(D):
                scaled = centered_s[layer, rows, cols] * rstd
                value, slope = gelu_pair(
                    scaled * norm_rows(2 * layer, rows.start) + norm_rows(2 * layer + 1, rows.start)
                )
                if sink is None:
                    value = 0.5 * value
                    slope_s[layer, rows, cols] = 0.5 * slope
                    stream_s[rows, cols] = value
                    total = fold_rows(total, value)
                else:
                    slope_s[layer, rows, cols] = slope
                    sink[layer - 1, rows, cols] = value.astype(BF)
                yield "vector", 16
            return total

        def norm_backward(layer, grad_of, emit):
            rstd = rstd_s[layer, :, cols]
            first = second = None
            for rows in spans(D):
                grad = grad_of(rows) * slope_s[layer, rows, cols]
                centered = centered_s[layer, rows, cols]
                add_norm(2 * layer + 1, rows.start, grad)
                grad = grad * rstd
                add_norm(2 * layer, rows.start, grad * centered)
                wide = grad * norm_rows(2 * layer, rows.start)
                slope_s[layer, rows, cols] = wide
                first = fold_rows(first, wide)
                second = fold_rows(second, wide * centered)
                yield "vector", 9
            shift = jnp.sum(first, axis=0, keepdims=True) * (1.0 / D)
            slant = jnp.sum(second, axis=0, keepdims=True) * (1.0 / D) * (rstd * rstd)
            yield "wait", 50
            for rows in spans(D):
                emit(rows, (slope_s[layer, rows, cols] - shift) - centered_s[layer, rows, cols] * slant)
                yield "vector", 5

        hot = (lax.broadcasted_iota(jnp.int32, (CODES, LANES), 0) == row_of(code_ref)).astype(F32).astype(BF)
        hot_s[:, cols] = hot
        pre = dot_nt(stem_t[...], lat_ref[cols, :]) + dot_nn(table_t[...], hot)
        yield "product", 2
        total = None
        for rows in spans(D):
            stream_s[rows, cols] = pre[rows]
            total = fold_rows(total, pre[rows])
            yield "vector", 2
        total = yield from norm_forward(0, total, None)
        for layer in range(1, LAYERS + 1):
            yield from norm_forward(layer, total, act_s)
            inner = dot_nn(up_t[layer - 1], act_s[layer - 1, :, cols])
            yield "product", 1
            for rows in spans(D):
                value, slope = gelu_pair(inner[rows])
                inner_slope_s[layer - 1, rows, cols] = slope
                gated_s[layer - 1, rows, cols] = value.astype(BF)
                yield "vector", 13
            branch = dot_nn(down_t[layer - 1], gated_s[layer - 1, :, cols])
            yield "product", 1
            total = None
            for rows in spans(D):
                stream = stream_s[rows, cols] + branch[rows]
                if layer < LAYERS:
                    stream_s[rows, cols] = stream
                    total = fold_rows(total, stream)
                else:
                    top_s[rows, cols] = stream.astype(BF)
                yield "vector", 2
        logit_s[:, cols] = dot_nn(head_t[...], top_s[:, cols])
        yield "product", 5
        coef = row_of(weight_ref).astype(F32) * scale_s[...]
        sections = (
            (VALUE_AT, BINS, value_ref),
            (REWARD_AT, BINS, reward_ref),
            (CHANCE_AT, CODES, target_ref),
            (POLICY_AT, ACTIONS, action_ref),
        )
        for begin, count, target_ref_of in sections:
            padded = -(-count // 8) * 8
            if padded != count:
                last = slice(begin + padded - 8, begin + padded)
                keep = lax.broadcasted_iota(jnp.int32, (8, LANES), 0) < count - (padded - 8)
                logit_s[last, cols] = jnp.where(keep, logit_s[last, cols], -1e30)
            peak = None
            for part in spans(padded):
                rows = slice(begin + part.start, begin + part.stop)
                peak = peak_rows(peak, logit_s[rows, cols])
                yield "vector", 1
            peak = jnp.max(peak, axis=0, keepdims=True)
            yield "wait", 40
            mass = None
            for part in spans(padded):
                rows = slice(begin + part.start, begin + part.stop)
                power = jnp.exp2((logit_s[rows, cols] - peak) * LOG2E)
                logit_s[rows, cols] = power
                mass = fold_rows(mass, power)
                yield "vector", 4
            scale = coef / jnp.sum(mass, axis=0, keepdims=True)
            target = row_of(target_ref_of)
            yield "wait", 60
            stored = -(-count // 16) * 16
            for part in spans(padded):
                rows = slice(begin + part.start, begin + part.stop)
                soft = logit_s[rows, cols] * scale
                place = lax.broadcasted_iota(jnp.int32, soft.shape, 0) + part.start
                soft = jnp.where(place == target, soft - coef, soft)
                if part.stop == padded and padded != stored:
                    soft = jnp.concatenate([soft, jnp.zeros((stored - padded, LANES), F32)], axis=0)
                    rows = slice(begin + part.start, begin + stored)
                low_s[rows, cols] = soft.astype(BF)
                yield "vector", 5
        yield "ready", "head"
        grad = dot_nn(head_n[...], low_s[:, cols])
        yield "product", 5
        for rows in spans(D):
            stream_s[rows, cols] = grad[rows]
            branch_s[LAYERS % 2, rows, cols] = grad[rows].astype(BF)
            yield "vector", 1
        for layer in range(LAYERS, 0, -1):
            gated_grad = dot_nn(down_n[layer - 1], branch_s[layer % 2, :, cols])
            yield "product", 1
            if layer + 2 <= LAYERS:
                yield "until", ("block", layer + 2)
            for rows in spans(D):
                inner_grad_s[layer % 2, rows, cols] = (
                    gated_grad[rows] * inner_slope_s[layer - 1, rows, cols]
                ).astype(BF)
                yield "vector", 2
            active_grad = dot_nn(up_n[layer - 1], inner_grad_s[layer % 2, :, cols])
            yield "product", 1
            yield "ready", ("block", layer)

            def emit(rows, change, layer=layer):
                stream = stream_s[rows, cols] + change
                stream_s[rows, cols] = stream
                if layer > 1:
                    branch_s[(layer - 1) % 2, rows, cols] = stream.astype(BF)

            if layer + 1 <= LAYERS:
                yield "until", ("block", layer + 1)
            yield from norm_backward(layer, lambda rows: active_grad[rows], emit)

        def emit_pre(rows, change):
            pre_s[rows, cols] = change.astype(BF)

        yield from norm_backward(0, lambda rows: stream_s[rows, cols], emit_pre)
        lat_grad[cols, :] = dot_tn(pre_s[:, cols], stem_t[...])
        yield "product", 1
        yield "ready", "stem"

    def weight_grads(what):
        if what == "head":
            head_acc[...] += dot_nt(low_s[0:ROWS, :], top_s[...])
        elif what == "stem":
            stem_acc[...] += dot_nn(pre_s[...], lat_ref[...])
            table_acc[...] += dot_nt(pre_s[...], hot_s[...])
        else:
            layer = what[1]
            down_acc[layer - 1] += dot_nt(branch_s[layer % 2], gated_s[layer - 1])
            up_acc[layer - 1] += dot_nt(act_s[layer - 1], inner_grad_s[layer % 2])

    members = [chain(index) for index in range(chains)]
    ready_at, progress = [0] * chains, [index * STAGGER for index in range(chains)]
    now = product_free = 0
    counts, done, until = {}, set(), [None] * chains
    while members.count(None) < chains:
        alive = [index for index in range(chains) if members[index] is not None]
        alive = [index for index in alive if until[index] is None or until[index] in done]
        able = [index for index in alive if ready_at[index] <= now]
        if not able:
            now = min(ready_at[index] for index in alive)
            continue
        index = min(able, key=lambda number: progress[number])
        try:
            kind, amount = next(members[index])
        except StopIteration:
            members[index] = None
            continue
        if kind == "vector":
            cost = amount * (CHUNK // 8) * (LANES // 128) / 3
            now += cost
            progress[index] += cost
        elif kind == "product":
            product_free = max(now, product_free) + amount * UNIT
            ready_at[index] = product_free + DELAY
            progress[index] += amount * UNIT
        elif kind == "wait":
            ready_at[index] = now + amount
        elif kind == "until":
            until[index] = amount
        else:
            counts[amount] = counts.get(amount, 0) + 1
            if counts[amount] == chains:
                weight_grads(amount)
                done.add(amount)
                product_free = max(now, product_free) + UNIT * chains * (5 if amount == "head" else 2)

    @pl.when(step == pl.num_programs(0) - 1)
    def _():
        for tile in range(DEPTH // 128):
            at = tile * 128
            end = min(128, ROWS - at)
            turned = head_acc[at : at + end, :]
            if end < 128:
                turned = jnp.concatenate([turned, jnp.zeros((128 - end, D), F32)], axis=0)
            logit_s[head_tile(tile)] = turned.T
        lane_at = lax.broadcasted_iota(jnp.int32, (D, 128), 1)
        columns = jnp.zeros((D, 128), F32)
        for which in range(2 * (LAYERS + 1)):
            columns = jnp.where(lane_at == which, jnp.sum(norm_part[which], axis=1, keepdims=True), columns)
        norms = columns.T[0:16]
        def pieces_of(data, model):
            at = (data * packing.mp + model) * packing.own
            deep = slice(data * packing.deep, (data + 1) * packing.deep)
            wide = slice(model * packing.wide, (model + 1) * packing.wide)
            squares = [lambda: stem_acc[deep, wide]]
            squares += [lambda layer=layer: 0.5 * up_acc[layer, deep, wide] for layer in range(LAYERS)]
            squares += [lambda layer=layer: 0.5 * down_acc[layer, deep, wide] for layer in range(LAYERS)]
            for group in range(packing.groups):
                members = squares[group * packing.per : (group + 1) * packing.per]
                yield (
                    group * packing.deep,
                    slice(0, packing.wide * len(members)),
                    lambda members=members: jnp.concatenate([member() for member in members], axis=1),
                )
            for tile in range(DEPTH // 128):
                rows, lanes = head_tile(tile)
                rows = slice(rows.start + at, rows.start + at + packing.own)
                yield (
                    packing.head_at + packing.own * tile,
                    slice(0, 128),
                    lambda rows=rows, lanes=lanes: logit_s[rows, lanes],
                )
            own = slice(at, at + packing.own)
            yield packing.tail_at, slice(0, CODES), lambda: table_acc[own, :]
            yield (
                packing.tail_at,
                slice(NORM_LANE, NORM_LANE + packing.own),
                lambda: norms[0 : 2 * (LAYERS + 1), own],
            )

        leaving = []
        for side in range(PARTS):
            owners = {slot_of(packing.orders[side], *device): device for device in devices}
            for chunk in range(chunks):
                place = chunk_at((centered_s, slope_s), side * chunks + chunk)
                place[...] = jnp.zeros((D, 128), F32)
                for row in range(0, D, packing.part):
                    for begin, lanes, value in pieces_of(*owners[(chunk * D + row) // packing.part]):
                        if begin // packing.part == side:
                            rows = value()
                            first = row + begin - side * packing.part
                            place[first : first + rows.shape[0], lanes] = rows
                leaving.append(
                    pltpu.make_async_copy(
                        place, outs[side].at[chunk * D : (chunk + 1) * D], copy_sem.at[side, chunk]
                    )
                )
                leaving[-1].start()
        for member in leaving:
            member.wait()


def train(packing, rows_all, latent, code, weight, value, reward, action, target, packed):
    count = latent.shape[0]
    chains = CHAINS
    block = chains * LANES

    def row():
        return pl.BlockSpec((block,), lambda i: (i,))

    parts = [pl.BlockSpec(memory_space=pl.ANY)] * PARTS
    flat = jax.ShapeDtypeStruct((packing.count * packing.part, 128), F32)
    packed = [member.reshape(-1, 128) for member in packed]
    return pl.pallas_call(
        functools.partial(train_kernel, packing, rows_all, chains),
        grid=(count // block,),
        out_shape=[jax.ShapeDtypeStruct((count, D), F32)] + [flat] * PARTS,
        in_specs=[pl.BlockSpec((block, D), lambda i: (i, 0))] + [row() for _ in range(6)] + parts,
        out_specs=[pl.BlockSpec((block, D), lambda i: (i, 0))] + parts,
        scratch_shapes=[
            pltpu.VMEM((D, D), F32),
            pltpu.VMEM((D, CODES), F32),
            pltpu.VMEM((LAYERS, D, D), F32),
            pltpu.VMEM((LAYERS, D, D), F32),
            pltpu.VMEM((ROWS, D), F32),
            pltpu.VMEM((D, D), BF),
            pltpu.VMEM((D, CODES), BF),
            pltpu.VMEM((LAYERS, D, D), BF),
            pltpu.VMEM((LAYERS, D, D), BF),
            pltpu.VMEM((LAYERS, D, D), BF),
            pltpu.VMEM((LAYERS, D, D), BF),
            pltpu.VMEM((ROWS, D), BF),
            pltpu.VMEM((D, DEPTH), BF),
            pltpu.VMEM((1, LANES), F32),
            pltpu.VMEM((D, block), F32),
            pltpu.VMEM((LAYERS + 1, D, block), F32),
            pltpu.VMEM((LAYERS + 1, D, block), F32),
            pltpu.VMEM((LAYERS, D, block), F32),
            pltpu.VMEM((LAYERS + 1, 1, block), F32),
            pltpu.VMEM((LAYERS, D, block), BF),
            pltpu.VMEM((LAYERS, D, block), BF),
            pltpu.VMEM((2, D, block), BF),
            pltpu.VMEM((2, D, block), BF),
            pltpu.VMEM((ROWS, block), F32),
            pltpu.VMEM((DEPTH, block), BF),
            pltpu.VMEM((D, block), BF),
            pltpu.VMEM((D, block), BF),
            pltpu.VMEM((CODES, block), BF),
            pltpu.VMEM((2 * (LAYERS + 1), D, 128), F32),
            pltpu.VMEM((2 * (LAYERS + 1), D, 128), F32),
            pltpu.SemaphoreType.DMA((PARTS, packing.count * packing.part // D)),
        ],
        compiler_params=pltpu.CompilerParams(
            dimension_semantics=("arbitrary",), vmem_limit_bytes=62 * 1024 * 1024
        ),
        name="train",
    )(latent, code, weight, value, reward, action, target, *packed)


def body(rows_all, packing, *args):
    latent, code, weight, value, reward, action, target = args[:7]
    groups = [args[7 + 3 * which : 10 + 3 * which] for which in range(6)]

    def turn(which, array):
        return jnp.swapaxes(array, -1, -2) if which in (0, 2, 4) else array

    groups = [tuple(turn(which, member) for member in group) for which, group in enumerate(groups)]
    stem, up, down, head, table, norm = (group[0] for group in groups)
    packed = send_weights(packing, stem, up, down, head, table, norm, weight.reshape(-1, 128))
    lat_grad, *grads = train(packing, rows_all, latent, code, weight, value, reward, action, target, packed)
    own = reduce_grads(packing, [member.reshape(packing.count, packing.part, 128) for member in grads])
    outs = update(packing, rows_all, own, groups)
    result = [outs[0].reshape(()), lat_grad]
    at = 1
    for which in range(6):
        for _ in range(4 if which < 5 else 3):
            result.append(turn(which, outs[at]))
            at += 1
    return tuple(result)


def solution(mesh):
    every = ("dp", "mp")
    states, flat = P(every, None), P(every)
    params = (P("mp", "dp"), P(None, "dp", "mp"), P(None, "mp", "dp"), P(every, None), P(None, every), P(None, None, every))
    in_specs = (states,) + (flat,) * 6 + tuple(spec for spec in params for _ in range(3))
    out_specs = (P(), states) + tuple(spec for which, spec in enumerate(params) for _ in range(4 if which < 5 else 3))
    packing = Packing(mesh.shape["dp"], mesh.shape["mp"])

    def run(*args):
        rows_all = args[0].shape[0] * packing.count
        return body(rows_all, packing, *args)

    return jax.shard_map(run, mesh=mesh, in_specs=in_specs, out_specs=out_specs, check_vma=False)
```

```python
import functools
import math

import jax
import jax.numpy as jnp
from jax import lax
from jax.experimental import pallas as pl
from jax.experimental.pallas import tpu as pltpu
from jax.sharding import PartitionSpec as P

D = 256
BINS = 601
ACTIONS = 4
CODES = 32
LAYERS = 4
STEP = 10

VALUE_AT = 0
REWARD_AT = 608
CHANCE_AT = 1216
POLICY_AT = 1248
ROWS = 1264
DEPTH = 1280

beta_one = 0.9
beta_two = 0.99
eps_adam = 1e-08
eps_norm = 1e-05
matrix_rate = 0.2
vector_rate = 0.6
decay_rate = 0.1
clip_scale = 3.0

GELU_A = math.sqrt(2.0 / math.pi)
GELU_B = GELU_A * 0.044715
LOG2E = 1.4426950408889634
LANES = 256
CHAINS = 4
PARTS = 4
RING = 16
CHUNK = 16
BF = jnp.bfloat16
F32 = jnp.float32
MESH = pl.DeviceIdType.MESH
MATRICES = 1 + 2 * LAYERS
NORM_LANE = 32
SUM_LANE = 64
SUM_ROW = 10


def dot_nn(left, right):
    return lax.dot_general(left, right, (((1,), (0,)), ((), ())), preferred_element_type=F32)


def dot_nt(left, right):
    return lax.dot_general(left, right, (((1,), (1,)), ((), ())), preferred_element_type=F32)


def dot_tn(left, right):
    return lax.dot_general(left, right, (((0,), (0,)), ((), ())), preferred_element_type=F32)


def gelu_pair(v):
    square = v * v
    gate = 1.0 + jnp.tanh(v * (GELU_A + GELU_B * square))
    value = v * gate
    slope = gate + value * (2.0 - gate) * (GELU_A + 3.0 * GELU_B * square)
    return value, slope


def fold_rows(total, part):
    for at in range(0, part.shape[0], 8):
        piece = part[at : at + 8]
        total = piece if total is None else total + piece
    return total


def peak_rows(total, part):
    for at in range(0, part.shape[0], 8):
        piece = part[at : at + 8]
        total = piece if total is None else jnp.maximum(total, piece)
    return total


def orders_of(dp, mp):
    def step(axis, low, size):
        return (axis, low, size) if size > 1 else None

    far_dp, near_dp = step("dp", 2, dp // 2), step("dp", 1, 2)
    far_mp, near_mp = step("mp", 2, mp // 2), step("mp", 1, 2)
    return (
        [member for member in (far_dp, near_dp, far_mp, near_mp) if member],
        [member for member in (far_dp, far_mp, near_dp, near_mp) if member],
    )


def digit_of(step, data, model):
    axis, low, ways = step
    return ((data if axis == "dp" else model) // low) % ways


def slot_of(order, data, model):
    place, weight = 0, 1
    for step in order:
        place = place + digit_of(step, data, model) * weight
        weight *= step[2]
    return place


def partner_of(step, away):
    axis, low, ways = step
    index = lax.axis_index(axis)
    digit = (index // low) % ways
    other = (digit + away) % ways
    return {axis: index + (other - digit) * low}, other - digit


def sizes_of(order):
    sizes = [1]
    for step in order:
        sizes.append(sizes[-1] * step[2])
    return sizes


class Packing:
    def __init__(self, dp, mp):
        self.dp, self.mp, self.count = dp, mp, dp * mp
        self.deep, self.wide, self.own = D // dp, D // mp, D // (dp * mp)
        self.per = 128 // self.wide
        self.groups = -(-MATRICES // self.per)
        self.head_at = self.groups * self.deep
        self.tail_at = -(-(self.head_at + self.own * (DEPTH // 128)) // 16) * 16
        self.rows = -(-(self.tail_at + 16) // (16 * PARTS)) * 16 * PARTS
        self.part = self.rows // PARTS
        self.orders = [orders_of(dp, mp)[number % 2] for number in range(PARTS)]
        self.sizes = [sizes_of(order) for order in self.orders]
        self.most = max(step[2] for step in self.orders[0])

    def split(self, begin, end):
        side = begin // self.part
        assert (end - 1) // self.part == side
        return side, slice(begin - side * self.part, end - side * self.part)

    def shapes(self, dtype):
        return [jax.ShapeDtypeStruct((self.count, self.part, 128), dtype)] * PARTS

    def scratch(self, dtype):
        return [pltpu.VMEM((self.count, self.part, 128), dtype)] * PARTS


def pad_lanes(array, lanes):
    missing = lanes - array.shape[1]
    return array if missing == 0 else jnp.concatenate([array, jnp.zeros((array.shape[0], missing), array.dtype)], axis=1)


def spread_head(head):
    rows = head.shape[0]

    def blank(count):
        return jnp.zeros((rows, count), head.dtype)

    return jnp.concatenate(
        [
            head[:, :BINS],
            blank(REWARD_AT - BINS),
            head[:, BINS : 2 * BINS],
            blank(CHANCE_AT - REWARD_AT - BINS),
            head[:, 2 * BINS + ACTIONS :],
            head[:, 2 * BINS : 2 * BINS + ACTIONS],
            blank(DEPTH - POLICY_AT - ACTIONS),
        ],
        axis=1,
    )


def gather_head(padded):
    return jnp.concatenate(
        [
            padded[:, VALUE_AT : VALUE_AT + BINS],
            padded[:, REWARD_AT : REWARD_AT + BINS],
            padded[:, POLICY_AT : POLICY_AT + ACTIONS],
            padded[:, CHANCE_AT : CHANCE_AT + CODES],
        ],
        axis=1,
    )


def send_kernel(packing, *refs):
    stem, up, down, head, table, norm, weight = refs[:7]
    outs, kinds = refs[7 : 7 + PARTS], refs[7 + PARTS : 7 + 2 * PARTS]
    block, send_sem, recv_sem, keep_sem = refs[7 + 2 * PARTS :]
    partners = [(step, away) for step in packing.orders[0] for away in range(1, step[2])]
    barrier = pltpu.get_barrier_semaphore()
    for step, away in partners:
        pl.semaphore_signal(barrier, inc=1, device_id=partner_of(step, away)[0], device_id_type=MESH)

    block[...] = jnp.zeros_like(block)
    matrices = [stem[...]] + [up[layer] for layer in range(LAYERS)] + [down[layer] for layer in range(LAYERS)]
    for group in range(packing.groups):
        members = matrices[group * packing.per : (group + 1) * packing.per]
        block[group * packing.deep : (group + 1) * packing.deep, :] = pad_lanes(jnp.concatenate(members, axis=1), 128)
    padded = spread_head(head[...])
    for tile in range(DEPTH // 128):
        at = packing.head_at + packing.own * tile
        block[at : at + packing.own, :] = padded[:, tile * 128 : (tile + 1) * 128]
    at = packing.tail_at
    block[at : at + packing.own, 0:CODES] = table[...]
    for layer in range(LAYERS + 1):
        block[at + 2 * layer : at + 2 * layer + 2, NORM_LANE : NORM_LANE + packing.own] = norm[layer]
    amount = jnp.sum(jnp.sum(weight[...].astype(F32), axis=0, keepdims=True), axis=1, keepdims=True)
    amount = jnp.broadcast_to(amount, (1, 128))
    for row in range(SUM_ROW, SUM_ROW + 3):
        part = amount.astype(BF).astype(F32)
        block[at + row : at + row + 1, SUM_LANE:128] = part[:, SUM_LANE:128]
        amount = amount - part
    data, model = lax.axis_index("dp"), lax.axis_index("mp")
    slots = [slot_of(order, data, model) for order in packing.orders]
    for side in range(PARTS):
        kinds[side][slots[side]] = block[side * packing.part : (side + 1) * packing.part, :].astype(BF)

    pl.semaphore_wait(barrier, len(partners))

    def copies_of(side, number):
        step, size = packing.orders[side][number], packing.sizes[side][number]
        held = kinds[side].at[pl.ds((slots[side] // size) * size, size)]
        return [
            pltpu.make_async_remote_copy(
                src_ref=held,
                dst_ref=held,
                send_sem=send_sem.at[side, number, away],
                recv_sem=recv_sem.at[side, number, away],
                device_id=partner_of(step, away)[0],
                device_id_type=MESH,
            )
            for away in range(1, step[2])
        ]

    def kept(side, start, size, sem):
        return pltpu.make_async_copy(
            kinds[side].at[pl.ds(start, size)], outs[side].at[pl.ds(start, size)], keep_sem.at[side, sem]
        )

    steps = len(packing.orders[0])
    copies = [[copies_of(side, number) for number in range(steps)] for side in range(PARTS)]
    local = [kept(side, slots[side], 1, 0) for side in range(PARTS)]
    for member in local:
        member.start()
    for number in range(steps + 1):
        for side in range(PARTS):
            if number:
                for member in copies[side][number - 1]:
                    member.wait_recv()
            if number < steps:
                for member in copies[side][number]:
                    member.start()
            if number:
                step, size = packing.orders[side][number - 1], packing.sizes[side][number - 1]
                for away in range(1, step[2]):
                    start = (slots[side] // size) * size + partner_of(step, away)[1] * size
                    local.append(kept(side, start, size, number * packing.most + away))
                    local[-1].start()
    for member in local:
        member.wait()
    for side in range(PARTS):
        for number in range(steps):
            for member in copies[side][number]:
                member.wait_send()


def send_weights(packing, stem, up, down, head, table, norm, weight):
    steps = len(packing.orders[0])
    return pl.pallas_call(
        functools.partial(send_kernel, packing),
        out_shape=packing.shapes(BF),
        in_specs=[pl.BlockSpec()] * 7,
        out_specs=[pl.BlockSpec(memory_space=pl.ANY)] * PARTS,
        scratch_shapes=packing.scratch(BF)
        + [
            pltpu.VMEM((packing.rows, 128), F32),
            pltpu.SemaphoreType.DMA((PARTS, steps, packing.most)),
            pltpu.SemaphoreType.DMA((PARTS, steps, packing.most)),
            pltpu.SemaphoreType.DMA((PARTS, (steps + 1) * packing.most)),
        ],
        compiler_params=pltpu.CompilerParams(
            collective_id=0, has_side_effects=True, vmem_limit_bytes=60 * 1024 * 1024
        ),
        name="send_weights",
    )(stem, up, down, head, table, norm, weight)


def reduce_kernel(packing, *refs):
    given, own = refs[:PARTS], refs[PARTS]
    held, sent, got = (refs[PARTS * kind + 1 : PARTS * (kind + 1) + 1] for kind in (1, 2, 3))
    across, along, send_sem, recv_sem, part_send, part_recv, fetch_sem = refs[4 * PARTS + 1 :]
    fetches = [pltpu.make_async_copy(given[side], held[side], fetch_sem.at[side]) for side in range(PARTS)]
    for member in fetches:
        member.start()
    steps = len(packing.orders[0])
    data, model = lax.axis_index("dp"), lax.axis_index("mp")
    barrier = pltpu.get_barrier_semaphore()
    for away in range(1, packing.mp):
        pl.semaphore_signal(barrier, inc=1, device_id={"mp": (model + away) % packing.mp}, device_id_type=MESH)
    for away in range(1, packing.dp):
        pl.semaphore_signal(barrier, inc=1, device_id={"dp": (data + away) % packing.dp}, device_id_type=MESH)

    slots = [slot_of(order, data, model) for order in packing.orders]

    def mine_of(side, number):
        size = packing.sizes[side][number]
        return (slots[side] // size) * size

    def place_of(side, number, away):
        size = packing.sizes[side][number]
        return pl.ds(size * away, size)

    def pack(side, number):
        step, size = packing.orders[side][number], packing.sizes[side][number]
        for away in range(1, step[2]):
            block = mine_of(side, number) + partner_of(step, away)[1] * size
            sent[side][place_of(side, number, away)] = held[side][pl.ds(block, size)].astype(BF)

    def copies_of(side, number):
        step = packing.orders[side][number]
        return [
            pltpu.make_async_remote_copy(
                src_ref=sent[side].at[place_of(side, number, away)],
                dst_ref=got[side].at[place_of(side, number, away)],
                send_sem=send_sem.at[side, number, away],
                recv_sem=recv_sem.at[side, number, away],
                device_id=partner_of(step, away)[0],
                device_id_type=MESH,
            )
            for away in range(1, step[2])
        ]

    def take(side, number):
        rows = pl.ds(mine_of(side, number), packing.sizes[side][number])
        total = held[side][rows]
        for away in range(1, packing.orders[side][number][2]):
            total = total + got[side][place_of(side, number, away)].astype(F32)
        held[side][rows] = total

    copies = [[copies_of(side, number) for number in range(steps)] for side in range(PARTS)]
    pl.semaphore_wait(barrier, packing.mp + packing.dp - 2)
    for number in range(steps - 1, -1, -1):
        for side in range(PARTS):
            if number < steps - 1:
                for member in copies[side][number + 1]:
                    member.wait_recv()
                take(side, number + 1)
            else:
                fetches[side].wait()
            pack(side, number)
            for member in copies[side][number]:
                member.start()
    total = None
    for side in range(PARTS):
        for member in copies[side][0]:
            member.wait_recv()
        take(side, 0)
        block = held[side][slots[side]]
        own[side * packing.part : (side + 1) * packing.part, :] = block
        total = fold_rows(total, block * block)

    def exchange(axis, index, count, buffer, value, first):
        buffer[index] = value
        going = []
        for away in range(1, count):
            going.append(
                pltpu.make_async_remote_copy(
                    src_ref=buffer.at[index],
                    dst_ref=buffer.at[index],
                    send_sem=part_send.at[first + away],
                    recv_sem=part_recv.at[first + away],
                    device_id={axis: (index + away) % count},
                    device_id_type=MESH,
                )
            )
            going[-1].start()
        for member in going:
            member.wait_recv()
        whole = buffer[0]
        for other in range(1, count):
            whole = whole + buffer[other]
        return whole, going

    total, going = exchange("mp", model, packing.mp, across, total, 0)
    total, more = exchange("dp", data, packing.dp, along, total, packing.mp)
    own[packing.rows : packing.rows + 8, :] = total
    for member in going + more:
        member.wait_send()
    for side in range(PARTS):
        for number in range(steps):
            for member in copies[side][number]:
                member.wait_send()


def reduce_grads(packing, grads):
    steps = len(packing.orders[0])
    vmem = pl.BlockSpec(memory_space=pltpu.VMEM)
    return pl.pallas_call(
        functools.partial(reduce_kernel, packing),
        out_shape=jax.ShapeDtypeStruct((packing.rows + 8, 128), F32),
        in_specs=[pl.BlockSpec(memory_space=pl.ANY)] * PARTS,
        out_specs=vmem,
        scratch_shapes=packing.scratch(F32)
        + packing.scratch(BF) * 2
        + [
            pltpu.VMEM((packing.mp, 8, 128), F32),
            pltpu.VMEM((packing.dp, 8, 128), F32),
            pltpu.SemaphoreType.DMA((PARTS, steps, packing.most)),
            pltpu.SemaphoreType.DMA((PARTS, steps, packing.most)),
            pltpu.SemaphoreType.DMA((packing.mp + packing.dp,)),
            pltpu.SemaphoreType.DMA((packing.mp + packing.dp,)),
            pltpu.SemaphoreType.DMA((PARTS,)),
        ],
        compiler_params=pltpu.CompilerParams(
            collective_id=1, has_side_effects=True, vmem_limit_bytes=60 * 1024 * 1024
        ),
        name="reduce_grads",
    )(*grads)


def adam_rows(weight, moment, square, grad, rate, decay):
    first = beta_one * moment + (1.0 - beta_one) * grad
    second = beta_two * square + (1.0 - beta_two) * grad * grad
    first_hat = first / (1.0 - beta_one**STEP)
    second_hat = second / (1.0 - beta_two**STEP)
    updated = weight - rate * (first_hat / (jnp.sqrt(second_hat) + eps_adam) + decay * weight)
    return (updated, first, second)


def update_kernel(packing, rows_all, own, *refs):
    ins, outs = refs[:18], refs[18:]
    grad_norm, outs = outs[0], outs[1:]
    squares = own[packing.rows : packing.rows + 8, :]
    whole = jnp.sum(jnp.sum(squares, axis=0, keepdims=True), axis=1, keepdims=True)
    norm = jnp.sqrt(whole)
    grad_norm[...] = norm
    ratio = jnp.minimum(1.0, clip_scale * math.sqrt(rows_all) / norm)

    def apply(which, index, grad, rate=matrix_rate, decay=decay_rate):
        weight, moment, square = (ins[3 * which + kind][index] for kind in range(3))
        base = 4 * which
        new, first, second = adam_rows(weight, moment, square, grad * ratio, rate, decay)
        outs[base][index] = new
        outs[base + 1][index] = first
        outs[base + 2][index] = second
        if which < 5:
            outs[base + 3][index] = new.astype(BF)

    def matrix(member):
        at = (member // packing.per) * packing.deep
        lane = (member % packing.per) * packing.wide
        return own[at : at + packing.deep, lane : lane + packing.wide]

    apply(0, ..., matrix(0))
    for layer in range(LAYERS):
        apply(1, layer, matrix(1 + layer))
        apply(2, layer, matrix(1 + LAYERS + layer))
    tiles = [
        own[packing.head_at + packing.own * tile : packing.head_at + packing.own * (tile + 1), :]
        for tile in range(DEPTH // 128)
    ]
    apply(3, ..., gather_head(jnp.concatenate(tiles, axis=1)))
    at = packing.tail_at
    apply(4, ..., own[at : at + packing.own, 0:CODES])
    for layer in range(LAYERS + 1):
        apply(
            5,
            layer,
            own[at + 2 * layer : at + 2 * layer + 2, NORM_LANE : NORM_LANE + packing.own],
            vector_rate,
            0.0,
        )


def update(packing, rows_all, own, groups):
    ins = [member for group in groups for member in group]
    outs = [jax.ShapeDtypeStruct((1, 1), F32)]
    for which, group in enumerate(groups):
        outs += [jax.ShapeDtypeStruct(group[0].shape, F32)] * 3
        if which < 5:
            outs.append(jax.ShapeDtypeStruct(group[0].shape, BF))
    return pl.pallas_call(
        functools.partial(update_kernel, packing, rows_all),
        out_shape=outs,
        in_specs=[pl.BlockSpec()] * (1 + len(ins)),
        out_specs=[pl.BlockSpec()] * len(outs),
        compiler_params=pltpu.CompilerParams(vmem_limit_bytes=48 * 1024 * 1024),
        name="update",
    )(own, *ins)


def train_kernel(
    packing,
    rows_all,
    chains,
    lat_ref,
    code_ref,
    weight_ref,
    value_ref,
    reward_ref,
    action_ref,
    target_ref,
    *refs,
):
    held, lat_grad, outs = refs[:PARTS], refs[PARTS], refs[PARTS + 1 : 2 * PARTS + 1]
    (
        stem_acc,
        table_acc,
        up_acc,
        down_acc,
        head_acc,
        stem_t,
        table_t,
        up_t,
        up_n,
        down_t,
        down_n,
        head_t,
        head_n,
        scale_s,
        norm_s,
        norm_part,
        lat_last,
        pre_last,
        hot_last,
        arriving,
        departing,
        copy_sem,
    ) = refs[2 * PARTS + 1 :]
    step = pl.program_id(0)
    chunks = packing.count * packing.part // D

    def head_tile(tile):
        return head_acc.at[(tile // 2) * D : (tile // 2 + 1) * D, (tile % 2) * 128 : (tile % 2 + 1) * 128]

    devices = [(data, model) for data in range(packing.dp) for model in range(packing.mp)]

    @pl.when(step == 0)
    def _():
        arrived = [
            pltpu.make_async_copy(
                held[side].at[chunk * D : (chunk + 1) * D],
                arriving.at[side * chunks + chunk],
                copy_sem.at[side, chunk],
            )
            for side in range(PARTS)
            for chunk in range(chunks)
        ]
        for member in arrived:
            member.start()
        for member in arrived:
            member.wait()

        def rows_of(device, begin, end):
            side, rows = packing.split(begin, end)
            chunk, row = divmod(slot_of(packing.orders[side], *device) * packing.part, D)
            return arriving[side * chunks + chunk, row : row + packing.part, :].astype(F32)[rows]

        wide_s = [stem_acc] + [up_acc.at[layer] for layer in range(LAYERS)] + [down_acc.at[layer] for layer in range(LAYERS)]
        for data in range(packing.dp):
            for group in range(packing.groups):
                begin = group * packing.deep
                parts = [rows_of((data, model), begin, begin + packing.deep) for model in range(packing.mp)]
                for member in range(min(packing.per, MATRICES - group * packing.per)):
                    lane = member * packing.wide
                    wide_s[group * packing.per + member][data * packing.deep : (data + 1) * packing.deep, :] = (
                        jnp.concatenate([part[:, lane : lane + packing.wide] for part in parts], axis=1)
                    )
        stem_t[...] = wide_s[0][...].astype(BF)
        for layer in range(LAYERS):
            half_up = 0.5 * wide_s[1 + layer][...]
            half_down = 0.5 * wide_s[1 + LAYERS + layer][...]
            up_n[layer] = half_up.astype(BF)
            up_t[layer] = half_up.T.astype(BF)
            down_t[layer] = half_down.astype(BF)
            down_n[layer] = half_down.T.astype(BF)
        norm_parts = []
        total = None
        for device in devices:
            at = (device[0] * packing.mp + device[1]) * packing.own
            for tile in range(DEPTH // 128):
                begin = packing.head_at + packing.own * tile
                head_tile(tile)[at : at + packing.own, :] = rows_of(device, begin, begin + packing.own)
            tail = rows_of(device, packing.tail_at, packing.tail_at + 16)
            table_acc[at : at + packing.own, :] = tail[0 : packing.own, 0:CODES]
            norm_parts.append(tail[:, NORM_LANE : NORM_LANE + packing.own])
            amount = tail[SUM_ROW : SUM_ROW + 1] + tail[SUM_ROW + 1 : SUM_ROW + 2] + tail[SUM_ROW + 2 : SUM_ROW + 3]
            total = amount if total is None else total + amount
        table_t[...] = table_acc[...].astype(BF)
        for tile in range(DEPTH // 128):
            at = tile * 128
            whole = head_tile(tile)[...]
            head_n[:, at : at + 128] = whole.astype(BF)
            end = min(128, ROWS - at)
            head_t[at : at + end, :] = whole.T.astype(BF)[0:end]
        norms = jnp.concatenate(norm_parts, axis=1)
        columns = jnp.concatenate([norms, jnp.zeros((128 - norms.shape[0], D), F32)], axis=0).T
        for which in range(2 * (LAYERS + 1)):
            norm_s[which] = jnp.broadcast_to(columns[:, which : which + 1], (D, 128))
        scale_s[...] = jnp.broadcast_to(rows_all / total[:, SUM_LANE : SUM_LANE + 1], (1, LANES))

        stem_acc[...] = jnp.zeros_like(stem_acc)
        table_acc[...] = jnp.zeros_like(table_acc)
        up_acc[...] = jnp.zeros_like(up_acc)
        down_acc[...] = jnp.zeros_like(down_acc)
        head_acc[...] = jnp.zeros_like(head_acc)
        norm_part[...] = jnp.zeros_like(norm_part)
        lat_last[...] = jnp.zeros_like(lat_last)
        pre_last[...] = jnp.zeros_like(pre_last)
        hot_last[...] = jnp.zeros_like(hot_last)

    def norm_rows(which, at):
        half = norm_s[which, at : at + CHUNK, :]
        return jnp.concatenate([half] * (LANES // 128), axis=1)

    spans = [slice(at, at + CHUNK) for at in range(0, D, CHUNK)]
    norm_total = {}

    def add_norm(which, at, part):
        for lane in range(0, LANES, 128):
            piece = part[:, lane : lane + 128]
            norm_total[which, at] = norm_total[which, at] + piece if (which, at) in norm_total else piece

    def pieces(array, count=D, begin=0):
        return [array[begin + at : begin + min(at + CHUNK, count)] for at in range(0, count, CHUNK)]

    def joined(parts):
        return jnp.concatenate(parts, axis=0)

    def folded(parts):
        total = None
        for part in parts:
            total = fold_rows(total, part)
        return jnp.sum(total, axis=0, keepdims=True)

    def norm_forward(layer, stream):
        mean = folded(stream) * (1.0 / D)
        centered = [part - mean for part in stream]
        rstd = lax.rsqrt(folded([part * part for part in centered]) * (1.0 / D) + eps_norm)
        values, slopes = [], []
        for rows, part in zip(spans, centered):
            value, slope = gelu_pair(
                (part * rstd) * norm_rows(2 * layer, rows.start) + norm_rows(2 * layer + 1, rows.start)
            )
            values.append(value)
            slopes.append(slope)
        return values, (centered, rstd, slopes)

    def norm_backward(layer, grads, kept):
        centered, rstd, slopes = kept
        wide = []
        for rows, grad, part, slope in zip(spans, grads, centered, slopes):
            grad = grad * slope
            add_norm(2 * layer + 1, rows.start, grad)
            grad = grad * rstd
            add_norm(2 * layer, rows.start, grad * part)
            wide.append(grad * norm_rows(2 * layer, rows.start))
        shift = folded(wide) * (1.0 / D)
        slant = folded([grad * part for grad, part in zip(wide, centered)]) * (1.0 / D) * (rstd * rstd)
        return [(grad - shift) - part * slant for grad, part in zip(wide, centered)]

    acts, gateds, branches, inner_grads, lows, tops = ({} for _ in range(6))

    def beside(kept, *key):
        return jnp.concatenate([kept[(index,) + key] for index in range(chains)], axis=1)

    def chain(index):
        cols = slice(index * LANES, (index + 1) * LANES)

        def row_of(ref):
            return ref[cols].reshape(1, LANES)

        hot = (lax.broadcasted_iota(jnp.int32, (CODES, LANES), 0) == row_of(code_ref)).astype(F32).astype(BF)
        stream = pieces(dot_nt(stem_t[...], lat_ref[cols, :]) + dot_nn(table_t[...], hot))
        yield
        kept, inner_slopes = {}, {}
        values, kept[0] = norm_forward(0, stream)
        stream = [0.5 * value for value in values]
        yield
        for layer in range(1, LAYERS + 1):
            values, kept[layer] = norm_forward(layer, stream)
            acts[index, layer] = joined([value.astype(BF) for value in values])
            yield
            inner = dot_nn(up_t[layer - 1], acts[index, layer])
            yield
            both = [gelu_pair(part) for part in pieces(inner)]
            inner_slopes[layer] = [slope for _, slope in both]
            gateds[index, layer] = joined([value.astype(BF) for value, _ in both])
            yield
            branch = dot_nn(down_t[layer - 1], gateds[index, layer])
            yield
            stream = [part + change for part, change in zip(stream, pieces(branch))]
        tops[(index,)] = joined([part.astype(BF) for part in stream])
        yield
        logits = dot_nn(head_t[...], tops[(index,)])
        yield
        coef = row_of(weight_ref).astype(F32) * scale_s[...]
        sections = (
            (VALUE_AT, BINS, value_ref),
            (REWARD_AT, BINS, reward_ref),
            (CHANCE_AT, CODES, target_ref),
            (POLICY_AT, ACTIONS, action_ref),
        )
        low = []
        for begin, count, target_ref_of in sections:
            padded = -(-count // 8) * 8
            parts = [logits[begin + at : begin + min(at + CHUNK, padded)] for at in range(0, padded, CHUNK)]
            if padded != count:
                place = lax.broadcasted_iota(jnp.int32, parts[-1].shape, 0) + (padded - parts[-1].shape[0])
                parts[-1] = jnp.where(place < count, parts[-1], -1e30)
            peak = None
            for part in parts:
                peak = peak_rows(peak, part)
            peak = jnp.max(peak, axis=0, keepdims=True)
            powers = [jnp.exp2((part - peak) * LOG2E) for part in parts]
            scale = coef / folded(powers)
            target = row_of(target_ref_of)
            for number, power in enumerate(powers):
                soft = power * scale
                place = lax.broadcasted_iota(jnp.int32, soft.shape, 0) + number * CHUNK
                soft = jnp.where(place == target, soft - coef, soft)
                missing = -soft.shape[0] % 16
                if missing:
                    soft = jnp.concatenate([soft, jnp.zeros((missing, LANES), F32)], axis=0)
                low.append(soft.astype(BF))
            yield
        low.append(jnp.zeros((DEPTH - ROWS, LANES), BF))
        low = joined(low)
        lows[(index,)] = low[0:ROWS]
        grad = dot_nn(head_n[...], low)
        yield
        if index == chains - 1:
            head_acc[0:ROWS, :] += dot_nt(beside(lows), beside(tops))
        stream = pieces(grad)
        for layer in range(LAYERS, 0, -1):
            branches[index, layer] = joined([part.astype(BF) for part in stream])
            yield
            gated_grad = dot_nn(down_n[layer - 1], branches[index, layer])
            yield
            inner_grads[index, layer] = joined(
                [(part * slope).astype(BF) for part, slope in zip(pieces(gated_grad), inner_slopes[layer])]
            )
            yield
            active_grad = dot_nn(up_n[layer - 1], inner_grads[index, layer])
            if index == chains - 1:
                down_acc[layer - 1] += dot_nt(beside(branches, layer), beside(gateds, layer))
                up_acc[layer - 1] += dot_nt(beside(acts, layer), beside(inner_grads, layer))
            yield
            changes = norm_backward(layer, pieces(active_grad), kept[layer])
            stream = [part + change for part, change in zip(stream, changes)]
            yield
        values, slopes = kept[0][:2], [0.5 * slope for slope in kept[0][2]]
        pre = joined([part.astype(BF) for part in norm_backward(0, stream, (*values, slopes))])
        yield
        lat_grad[cols, :] = dot_tn(pre, stem_t[...])
        pre_last[:, cols] = pre
        hot_last[:, cols] = hot
        lat_last[cols, :] = lat_ref[cols, :]

    def stem_grads():
        stem_acc[...] += dot_nn(pre_last[...], lat_last[...])
        table_acc[...] += dot_nt(pre_last[...], hot_last[...])

    stem_grads()

    running = []
    waiting = [chain(index) for index in range(chains)]
    while running or waiting:
        if waiting:
            running.append(waiting.pop(0))
        for member in list(running):
            try:
                next(member)
            except StopIteration:
                running.remove(member)
    for (which, at), total in norm_total.items():
        norm_part[which, at : at + CHUNK, :] += total

    @pl.when(step == pl.num_programs(0) - 1)
    def _():
        stem_grads()
        for at in range(0, DEPTH, D):
            head_acc[at : at + D, :] = head_acc[at : at + D, :].T
        lane_at = lax.broadcasted_iota(jnp.int32, (D, 128), 1)
        columns = jnp.zeros((D, 128), F32)
        for which in range(2 * (LAYERS + 1)):
            columns = jnp.where(lane_at == which, jnp.sum(norm_part[which], axis=1, keepdims=True), columns)
        norms = columns.T[0:16]
        def pieces_of(data, model):
            at = (data * packing.mp + model) * packing.own
            deep = slice(data * packing.deep, (data + 1) * packing.deep)
            wide = slice(model * packing.wide, (model + 1) * packing.wide)
            squares = [lambda: stem_acc[deep, wide]]
            squares += [lambda layer=layer: 0.5 * up_acc[layer, deep, wide] for layer in range(LAYERS)]
            squares += [lambda layer=layer: 0.5 * down_acc[layer, deep, wide] for layer in range(LAYERS)]
            for group in range(packing.groups):
                members = squares[group * packing.per : (group + 1) * packing.per]
                yield (
                    group * packing.deep,
                    slice(0, packing.wide * len(members)),
                    lambda members=members: jnp.concatenate([member() for member in members], axis=1),
                )
            for tile in range(DEPTH // 128):
                yield (
                    packing.head_at + packing.own * tile,
                    slice(0, 128),
                    lambda tile=tile: head_tile(tile)[at : at + packing.own, :],
                )
            own = slice(at, at + packing.own)
            yield packing.tail_at, slice(0, CODES), lambda: table_acc[own, :]
            yield (
                packing.tail_at,
                slice(NORM_LANE, NORM_LANE + packing.own),
                lambda: norms[0 : 2 * (LAYERS + 1), own],
            )

        leaving = []
        for side in range(PARTS):
            owners = {slot_of(packing.orders[side], *device): device for device in devices}
            for chunk in range(chunks):
                number = side * chunks + chunk
                place = departing.at[number % RING]
                if number >= RING:
                    leaving[number - RING].wait()
                place[...] = jnp.zeros((D, 128), F32)
                for row in range(0, D, packing.part):
                    for begin, lanes, value in pieces_of(*owners[(chunk * D + row) // packing.part]):
                        if begin // packing.part == side:
                            rows = value()
                            first = row + begin - side * packing.part
                            place[first : first + rows.shape[0], lanes] = rows
                leaving.append(
                    pltpu.make_async_copy(
                        place, outs[side].at[chunk * D : (chunk + 1) * D], copy_sem.at[side, chunk]
                    )
                )
                leaving[-1].start()
        for member in leaving[-RING:]:
            member.wait()


def train(packing, rows_all, latent, code, weight, value, reward, action, target, packed):
    count = latent.shape[0]
    chains = CHAINS
    block = chains * LANES

    def row():
        return pl.BlockSpec((block,), lambda i: (i,))

    parts = [pl.BlockSpec(memory_space=pl.ANY)] * PARTS
    flat = jax.ShapeDtypeStruct((packing.count * packing.part, 128), F32)
    packed = [member.reshape(-1, 128) for member in packed]
    return pl.pallas_call(
        functools.partial(train_kernel, packing, rows_all, chains),
        grid=(count // block,),
        out_shape=[jax.ShapeDtypeStruct((count, D), F32)] + [flat] * PARTS,
        in_specs=[pl.BlockSpec((block, D), lambda i: (i, 0))]
        + [row() for _ in range(6)] + parts,
        out_specs=[pl.BlockSpec((block, D), lambda i: (i, 0))] + parts,
        scratch_shapes=[
            pltpu.VMEM((D, D), F32),
            pltpu.VMEM((D, CODES), F32),
            pltpu.VMEM((LAYERS, D, D), F32),
            pltpu.VMEM((LAYERS, D, D), F32),
            pltpu.VMEM((DEPTH, D), F32),
            pltpu.VMEM((D, D), BF),
            pltpu.VMEM((D, CODES), BF),
            pltpu.VMEM((LAYERS, D, D), BF),
            pltpu.VMEM((LAYERS, D, D), BF),
            pltpu.VMEM((LAYERS, D, D), BF),
            pltpu.VMEM((LAYERS, D, D), BF),
            pltpu.VMEM((ROWS, D), BF),
            pltpu.VMEM((D, DEPTH), BF),
            pltpu.VMEM((1, LANES), F32),
            pltpu.VMEM((2 * (LAYERS + 1), D, 128), F32),
            pltpu.VMEM((2 * (LAYERS + 1), D, 128), F32),
            pltpu.VMEM((block, D), BF),
            pltpu.VMEM((D, block), BF),
            pltpu.VMEM((CODES, block), BF),
            pltpu.VMEM((PARTS * packing.count * packing.part // D, D, 128), BF),
            pltpu.VMEM((RING, D, 128), F32),
            pltpu.SemaphoreType.DMA((PARTS, packing.count * packing.part // D)),
        ],
        compiler_params=pltpu.CompilerParams(
            dimension_semantics=("arbitrary",), vmem_limit_bytes=60 * 1024 * 1024
        ),
        name="train",
    )(latent, code, weight, value, reward, action, target, *packed)


def body(rows_all, packing, *args):
    latent, code, weight, value, reward, action, target = args[:7]
    groups = [args[7 + 3 * which : 10 + 3 * which] for which in range(6)]

    def turn(which, array):
        return jnp.swapaxes(array, -1, -2) if which in (0, 2, 4) else array

    groups = [tuple(turn(which, member) for member in group) for which, group in enumerate(groups)]
    stem, up, down, head, table, norm = (group[0] for group in groups)
    packed = send_weights(packing, stem, up, down, head, table, norm, weight.reshape(-1, 128))
    lat_grad, *grads = train(packing, rows_all, latent, code, weight, value, reward, action, target, packed)
    own = reduce_grads(packing, [member.reshape(packing.count, packing.part, 128) for member in grads])
    outs = update(packing, rows_all, own, groups)
    result = [outs[0].reshape(()), lat_grad]
    at = 1
    for which in range(6):
        for _ in range(4 if which < 5 else 3):
            result.append(turn(which, outs[at]))
            at += 1
    return tuple(result)


def solution(mesh):
    every = ("dp", "mp")
    states, flat = P(every, None), P(every)
    params = (P("mp", "dp"), P(None, "dp", "mp"), P(None, "mp", "dp"), P(every, None), P(None, every), P(None, None, every))
    in_specs = (states,) + (flat,) * 6 + tuple(spec for spec in params for _ in range(3))
    out_specs = (P(), states) + tuple(spec for which, spec in enumerate(params) for _ in range(4 if which < 5 else 3))
    packing = Packing(mesh.shape["dp"], mesh.shape["mp"])

    def run(*args):
        rows_all = args[0].shape[0] * packing.count
        return body(rows_all, packing, *args)

    return jax.shard_map(run, mesh=mesh, in_specs=in_specs, out_specs=out_specs, check_vma=False)
```

```python
import functools
import math

import jax
import jax.numpy as jnp
from jax import lax
from jax.experimental import pallas as pl
from jax.experimental.pallas import tpu as pltpu
from jax.sharding import PartitionSpec as P

D = 256
BINS = 601
ACTIONS = 4
CODES = 32
LAYERS = 4
STEP = 10

VALUE_AT = 0
REWARD_AT = 608
CHANCE_AT = 1216
POLICY_AT = 1248
ROWS = 1264
DEPTH = 1280

beta_one = 0.9
beta_two = 0.99
eps_adam = 1e-08
eps_norm = 1e-05
matrix_rate = 0.2
vector_rate = 0.6
decay_rate = 0.1
clip_scale = 3.0

GELU_A = math.sqrt(2.0 / math.pi)
GELU_B = GELU_A * 0.044715
LOG2E = 1.4426950408889634
LANES = 256
CHAINS = 4
PARTS = 4
RING = 16
CHUNK = 16
BF = jnp.bfloat16
F32 = jnp.float32
MESH = pl.DeviceIdType.MESH
MATRICES = 1 + 2 * LAYERS
NORM_LANE = 32
SUM_LANE = 64
SUM_ROW = 10


def dot_nn(left, right):
    return lax.dot_general(left, right, (((1,), (0,)), ((), ())), preferred_element_type=F32)


def dot_nt(left, right):
    return lax.dot_general(left, right, (((1,), (1,)), ((), ())), preferred_element_type=F32)


def dot_tn(left, right):
    return lax.dot_general(left, right, (((0,), (0,)), ((), ())), preferred_element_type=F32)


def gelu_pair(v):
    square = v * v
    gate = 1.0 + jnp.tanh(v * (GELU_A + GELU_B * square))
    value = v * gate
    slope = gate + value * (2.0 - gate) * (GELU_A + 3.0 * GELU_B * square)
    return value, slope


def fold_rows(total, part):
    for at in range(0, part.shape[0], 8):
        piece = part[at : at + 8]
        total = piece if total is None else total + piece
    return total


def peak_rows(total, part):
    for at in range(0, part.shape[0], 8):
        piece = part[at : at + 8]
        total = piece if total is None else jnp.maximum(total, piece)
    return total


def orders_of(dp, mp):
    def step(axis, low, size):
        return (axis, low, size) if size > 1 else None

    far_dp, near_dp = step("dp", 2, dp // 2), step("dp", 1, 2)
    far_mp, near_mp = step("mp", 2, mp // 2), step("mp", 1, 2)
    return (
        [member for member in (far_dp, near_dp, far_mp, near_mp) if member],
        [member for member in (far_dp, far_mp, near_dp, near_mp) if member],
    )


def digit_of(step, data, model):
    axis, low, ways = step
    return ((data if axis == "dp" else model) // low) % ways


def slot_of(order, data, model):
    place, weight = 0, 1
    for step in order:
        place = place + digit_of(step, data, model) * weight
        weight *= step[2]
    return place


def partner_of(step, away):
    axis, low, ways = step
    index = lax.axis_index(axis)
    digit = (index // low) % ways
    other = (digit + away) % ways
    return {axis: index + (other - digit) * low}, other - digit


def sizes_of(order):
    sizes = [1]
    for step in order:
        sizes.append(sizes[-1] * step[2])
    return sizes


class Packing:
    def __init__(self, dp, mp):
        self.dp, self.mp, self.count = dp, mp, dp * mp
        self.deep, self.wide, self.own = D // dp, D // mp, D // (dp * mp)
        self.per = 128 // self.wide
        self.groups = -(-MATRICES // self.per)
        self.head_at = self.groups * self.deep
        self.tail_at = -(-(self.head_at + self.own * (DEPTH // 128)) // 16) * 16
        self.rows = -(-(self.tail_at + 16) // (16 * PARTS)) * 16 * PARTS
        self.part = self.rows // PARTS
        self.orders = [orders_of(dp, mp)[number % 2] for number in range(PARTS)]
        self.sizes = [sizes_of(order) for order in self.orders]
        self.most = max(step[2] for step in self.orders[0])

    def split(self, begin, end):
        side = begin // self.part
        assert (end - 1) // self.part == side
        return side, slice(begin - side * self.part, end - side * self.part)

    def shapes(self, dtype):
        return [jax.ShapeDtypeStruct((self.count, self.part, 128), dtype)] * PARTS

    def scratch(self, dtype):
        return [pltpu.VMEM((self.count, self.part, 128), dtype)] * PARTS


def pad_lanes(array, lanes):
    missing = lanes - array.shape[1]
    return array if missing == 0 else jnp.concatenate([array, jnp.zeros((array.shape[0], missing), array.dtype)], axis=1)


def spread_head(head):
    rows = head.shape[0]

    def blank(count):
        return jnp.zeros((rows, count), head.dtype)

    return jnp.concatenate(
        [
            head[:, :BINS],
            blank(REWARD_AT - BINS),
            head[:, BINS : 2 * BINS],
            blank(CHANCE_AT - REWARD_AT - BINS),
            head[:, 2 * BINS + ACTIONS :],
            head[:, 2 * BINS : 2 * BINS + ACTIONS],
            blank(DEPTH - POLICY_AT - ACTIONS),
        ],
        axis=1,
    )


def gather_head(padded):
    return jnp.concatenate(
        [
            padded[:, VALUE_AT : VALUE_AT + BINS],
            padded[:, REWARD_AT : REWARD_AT + BINS],
            padded[:, POLICY_AT : POLICY_AT + ACTIONS],
            padded[:, CHANCE_AT : CHANCE_AT + CODES],
        ],
        axis=1,
    )


def send_kernel(packing, *refs):
    stem, up, down, head, table, norm, weight = refs[:7]
    outs, kinds = refs[7 : 7 + PARTS], refs[7 + PARTS : 7 + 2 * PARTS]
    block, send_sem, recv_sem, keep_sem = refs[7 + 2 * PARTS :]
    partners = [(step, away) for step in packing.orders[0] for away in range(1, step[2])]
    barrier = pltpu.get_barrier_semaphore()
    for step, away in partners:
        pl.semaphore_signal(barrier, inc=1, device_id=partner_of(step, away)[0], device_id_type=MESH)

    block[...] = jnp.zeros_like(block)
    matrices = [stem[...]] + [up[layer] for layer in range(LAYERS)] + [down[layer] for layer in range(LAYERS)]
    for group in range(packing.groups):
        members = matrices[group * packing.per : (group + 1) * packing.per]
        block[group * packing.deep : (group + 1) * packing.deep, :] = pad_lanes(jnp.concatenate(members, axis=1), 128)
    padded = spread_head(head[...])
    for tile in range(DEPTH // 128):
        at = packing.head_at + packing.own * tile
        block[at : at + packing.own, :] = padded[:, tile * 128 : (tile + 1) * 128]
    at = packing.tail_at
    block[at : at + packing.own, 0:CODES] = table[...]
    for layer in range(LAYERS + 1):
        block[at + 2 * layer : at + 2 * layer + 2, NORM_LANE : NORM_LANE + packing.own] = norm[layer]
    amount = jnp.sum(jnp.sum(weight[...].astype(F32), axis=0, keepdims=True), axis=1, keepdims=True)
    amount = jnp.broadcast_to(amount, (1, 128))
    for row in range(SUM_ROW, SUM_ROW + 3):
        part = amount.astype(BF).astype(F32)
        block[at + row : at + row + 1, SUM_LANE:128] = part[:, SUM_LANE:128]
        amount = amount - part
    data, model = lax.axis_index("dp"), lax.axis_index("mp")
    slots = [slot_of(order, data, model) for order in packing.orders]
    for side in range(PARTS):
        kinds[side][slots[side]] = block[side * packing.part : (side + 1) * packing.part, :].astype(BF)

    pl.semaphore_wait(barrier, len(partners))

    def copies_of(side, number):
        step, size = packing.orders[side][number], packing.sizes[side][number]
        held = kinds[side].at[pl.ds((slots[side] // size) * size, size)]
        return [
            pltpu.make_async_remote_copy(
                src_ref=held,
                dst_ref=held,
                send_sem=send_sem.at[side, number, away],
                recv_sem=recv_sem.at[side, number, away],
                device_id=partner_of(step, away)[0],
                device_id_type=MESH,
            )
            for away in range(1, step[2])
        ]

    def kept(side, start, size, sem):
        return pltpu.make_async_copy(
            kinds[side].at[pl.ds(start, size)], outs[side].at[pl.ds(start, size)], keep_sem.at[side, sem]
        )

    steps = len(packing.orders[0])
    copies = [[copies_of(side, number) for number in range(steps)] for side in range(PARTS)]
    local = [kept(side, slots[side], 1, 0) for side in range(PARTS)]
    for member in local:
        member.start()
    for number in range(steps + 1):
        for side in range(PARTS):
            if number:
                for member in copies[side][number - 1]:
                    member.wait_recv()
            if number < steps:
                for member in copies[side][number]:
                    member.start()
            if number:
                step, size = packing.orders[side][number - 1], packing.sizes[side][number - 1]
                for away in range(1, step[2]):
                    start = (slots[side] // size) * size + partner_of(step, away)[1] * size
                    local.append(kept(side, start, size, number * packing.most + away))
                    local[-1].start()
    for member in local:
        member.wait()
    for side in range(PARTS):
        for number in range(steps):
            for member in copies[side][number]:
                member.wait_send()


def send_weights(packing, stem, up, down, head, table, norm, weight):
    steps = len(packing.orders[0])
    return pl.pallas_call(
        functools.partial(send_kernel, packing),
        out_shape=packing.shapes(BF),
        in_specs=[pl.BlockSpec()] * 7,
        out_specs=[pl.BlockSpec(memory_space=pl.ANY)] * PARTS,
        scratch_shapes=packing.scratch(BF)
        + [
            pltpu.VMEM((packing.rows, 128), F32),
            pltpu.SemaphoreType.DMA((PARTS, steps, packing.most)),
            pltpu.SemaphoreType.DMA((PARTS, steps, packing.most)),
            pltpu.SemaphoreType.DMA((PARTS, (steps + 1) * packing.most)),
        ],
        compiler_params=pltpu.CompilerParams(
            collective_id=0, has_side_effects=True, vmem_limit_bytes=60 * 1024 * 1024
        ),
        name="send_weights",
    )(stem, up, down, head, table, norm, weight)


def reduce_kernel(packing, *refs):
    given, own = refs[:PARTS], refs[PARTS]
    held, sent, got = (refs[PARTS * kind + 1 : PARTS * (kind + 1) + 1] for kind in (1, 2, 3))
    across, along, send_sem, recv_sem, part_send, part_recv, fetch_sem = refs[4 * PARTS + 1 :]
    fetches = [pltpu.make_async_copy(given[side], held[side], fetch_sem.at[side]) for side in range(PARTS)]
    for member in fetches:
        member.start()
    steps = len(packing.orders[0])
    data, model = lax.axis_index("dp"), lax.axis_index("mp")
    barrier = pltpu.get_barrier_semaphore()
    for away in range(1, packing.mp):
        pl.semaphore_signal(barrier, inc=1, device_id={"mp": (model + away) % packing.mp}, device_id_type=MESH)
    for away in range(1, packing.dp):
        pl.semaphore_signal(barrier, inc=1, device_id={"dp": (data + away) % packing.dp}, device_id_type=MESH)

    slots = [slot_of(order, data, model) for order in packing.orders]

    def mine_of(side, number):
        size = packing.sizes[side][number]
        return (slots[side] // size) * size

    def place_of(side, number, away):
        size = packing.sizes[side][number]
        return pl.ds(size * away, size)

    def pack(side, number):
        step, size = packing.orders[side][number], packing.sizes[side][number]
        for away in range(1, step[2]):
            block = mine_of(side, number) + partner_of(step, away)[1] * size
            sent[side][place_of(side, number, away)] = held[side][pl.ds(block, size)].astype(BF)

    def copies_of(side, number):
        step = packing.orders[side][number]
        return [
            pltpu.make_async_remote_copy(
                src_ref=sent[side].at[place_of(side, number, away)],
                dst_ref=got[side].at[place_of(side, number, away)],
                send_sem=send_sem.at[side, number, away],
                recv_sem=recv_sem.at[side, number, away],
                device_id=partner_of(step, away)[0],
                device_id_type=MESH,
            )
            for away in range(1, step[2])
        ]

    def take(side, number):
        rows = pl.ds(mine_of(side, number), packing.sizes[side][number])
        total = held[side][rows]
        for away in range(1, packing.orders[side][number][2]):
            total = total + got[side][place_of(side, number, away)].astype(F32)
        held[side][rows] = total

    copies = [[copies_of(side, number) for number in range(steps)] for side in range(PARTS)]
    pl.semaphore_wait(barrier, packing.mp + packing.dp - 2)
    for number in range(steps - 1, -1, -1):
        for side in range(PARTS):
            if number < steps - 1:
                for member in copies[side][number + 1]:
                    member.wait_recv()
                take(side, number + 1)
            else:
                fetches[side].wait()
            pack(side, number)
            for member in copies[side][number]:
                member.start()
    total = None
    for side in range(PARTS):
        for member in copies[side][0]:
            member.wait_recv()
        take(side, 0)
        block = held[side][slots[side]]
        own[side * packing.part : (side + 1) * packing.part, :] = block
        total = fold_rows(total, block * block)

    def exchange(axis, index, count, buffer, value, first):
        buffer[index] = value
        going = []
        for away in range(1, count):
            going.append(
                pltpu.make_async_remote_copy(
                    src_ref=buffer.at[index],
                    dst_ref=buffer.at[index],
                    send_sem=part_send.at[first + away],
                    recv_sem=part_recv.at[first + away],
                    device_id={axis: (index + away) % count},
                    device_id_type=MESH,
                )
            )
            going[-1].start()
        for member in going:
            member.wait_recv()
        whole = buffer[0]
        for other in range(1, count):
            whole = whole + buffer[other]
        return whole, going

    total, going = exchange("mp", model, packing.mp, across, total, 0)
    total, more = exchange("dp", data, packing.dp, along, total, packing.mp)
    own[packing.rows : packing.rows + 8, :] = total
    for member in going + more:
        member.wait_send()
    for side in range(PARTS):
        for number in range(steps):
            for member in copies[side][number]:
                member.wait_send()


def reduce_grads(packing, grads):
    steps = len(packing.orders[0])
    vmem = pl.BlockSpec(memory_space=pltpu.VMEM)
    return pl.pallas_call(
        functools.partial(reduce_kernel, packing),
        out_shape=jax.ShapeDtypeStruct((packing.rows + 8, 128), F32),
        in_specs=[pl.BlockSpec(memory_space=pl.ANY)] * PARTS,
        out_specs=vmem,
        scratch_shapes=packing.scratch(F32)
        + packing.scratch(BF) * 2
        + [
            pltpu.VMEM((packing.mp, 8, 128), F32),
            pltpu.VMEM((packing.dp, 8, 128), F32),
            pltpu.SemaphoreType.DMA((PARTS, steps, packing.most)),
            pltpu.SemaphoreType.DMA((PARTS, steps, packing.most)),
            pltpu.SemaphoreType.DMA((packing.mp + packing.dp,)),
            pltpu.SemaphoreType.DMA((packing.mp + packing.dp,)),
            pltpu.SemaphoreType.DMA((PARTS,)),
        ],
        compiler_params=pltpu.CompilerParams(
            collective_id=1, has_side_effects=True, vmem_limit_bytes=60 * 1024 * 1024
        ),
        name="reduce_grads",
    )(*grads)


def adam_rows(weight, moment, square, grad, rate, decay):
    first = beta_one * moment + (1.0 - beta_one) * grad
    second = beta_two * square + (1.0 - beta_two) * grad * grad
    first_hat = first / (1.0 - beta_one**STEP)
    second_hat = second / (1.0 - beta_two**STEP)
    updated = weight - rate * (first_hat / (jnp.sqrt(second_hat) + eps_adam) + decay * weight)
    return (updated, first, second)


def update_kernel(packing, rows_all, own, *refs):
    ins, outs = refs[:18], refs[18:]
    grad_norm, outs = outs[0], outs[1:]
    squares = own[packing.rows : packing.rows + 8, :]
    whole = jnp.sum(jnp.sum(squares, axis=0, keepdims=True), axis=1, keepdims=True)
    norm = jnp.sqrt(whole)
    grad_norm[...] = norm
    ratio = jnp.minimum(1.0, clip_scale * math.sqrt(rows_all) / norm)

    def apply(which, index, grad, rate=matrix_rate, decay=decay_rate):
        weight, moment, square = (ins[3 * which + kind][index] for kind in range(3))
        base = 4 * which
        new, first, second = adam_rows(weight, moment, square, grad * ratio, rate, decay)
        outs[base][index] = new
        outs[base + 1][index] = first
        outs[base + 2][index] = second
        if which < 5:
            outs[base + 3][index] = new.astype(BF)

    def matrix(member):
        at = (member // packing.per) * packing.deep
        lane = (member % packing.per) * packing.wide
        return own[at : at + packing.deep, lane : lane + packing.wide]

    apply(0, ..., matrix(0))
    for layer in range(LAYERS):
        apply(1, layer, matrix(1 + layer))
        apply(2, layer, matrix(1 + LAYERS + layer))
    tiles = [
        own[packing.head_at + packing.own * tile : packing.head_at + packing.own * (tile + 1), :]
        for tile in range(DEPTH // 128)
    ]
    apply(3, ..., gather_head(jnp.concatenate(tiles, axis=1)))
    at = packing.tail_at
    apply(4, ..., own[at : at + packing.own, 0:CODES])
    for layer in range(LAYERS + 1):
        apply(
            5,
            layer,
            own[at + 2 * layer : at + 2 * layer + 2, NORM_LANE : NORM_LANE + packing.own],
            vector_rate,
            0.0,
        )


def update(packing, rows_all, own, groups):
    ins = [member for group in groups for member in group]
    outs = [jax.ShapeDtypeStruct((1, 1), F32)]
    for which, group in enumerate(groups):
        outs += [jax.ShapeDtypeStruct(group[0].shape, F32)] * 3
        if which < 5:
            outs.append(jax.ShapeDtypeStruct(group[0].shape, BF))
    return pl.pallas_call(
        functools.partial(update_kernel, packing, rows_all),
        out_shape=outs,
        in_specs=[pl.BlockSpec()] * (1 + len(ins)),
        out_specs=[pl.BlockSpec()] * len(outs),
        compiler_params=pltpu.CompilerParams(vmem_limit_bytes=48 * 1024 * 1024),
        name="update",
    )(own, *ins)


def train_kernel(
    packing,
    rows_all,
    chains,
    lat_ref,
    code_ref,
    weight_ref,
    value_ref,
    reward_ref,
    action_ref,
    target_ref,
    gate_ref,
    *refs,
):
    held, lat_grad, outs = refs[:PARTS], refs[PARTS], refs[PARTS + 1 : 2 * PARTS + 1]
    (
        stem_acc,
        table_acc,
        up_acc,
        down_acc,
        head_acc,
        stem_t,
        table_t,
        up_t,
        up_n,
        down_t,
        down_n,
        head_t,
        head_n,
        scale_s,
        norm_s,
        norm_part,
        lat_last,
        pre_last,
        hot_last,
        centered_s,
        slope_s,
        inner_slope_s,
        rstd_s,
        act_s,
        gated_s,
        grad_s,
        arriving,
        departing,
        copy_sem,
    ) = refs[2 * PARTS + 1 :]
    step = pl.program_id(0)
    chunks = packing.count * packing.part // D

    def head_tile(tile):
        return head_acc.at[(tile // 2) * D : (tile // 2 + 1) * D, (tile % 2) * 128 : (tile % 2 + 1) * 128]

    devices = [(data, model) for data in range(packing.dp) for model in range(packing.mp)]

    @pl.when(step == 0)
    def _():
        arrived = [
            pltpu.make_async_copy(
                held[side].at[chunk * D : (chunk + 1) * D],
                arriving.at[side * chunks + chunk],
                copy_sem.at[side, chunk],
            )
            for side in range(PARTS)
            for chunk in range(chunks)
        ]
        for member in arrived:
            member.start()
        for member in arrived:
            member.wait()

        def rows_of(device, begin, end):
            side, rows = packing.split(begin, end)
            chunk, row = divmod(slot_of(packing.orders[side], *device) * packing.part, D)
            return arriving[side * chunks + chunk, row : row + packing.part, :].astype(F32)[rows]

        wide_s = [stem_acc] + [up_acc.at[layer] for layer in range(LAYERS)] + [down_acc.at[layer] for layer in range(LAYERS)]
        for data in range(packing.dp):
            for group in range(packing.groups):
                begin = group * packing.deep
                parts = [rows_of((data, model), begin, begin + packing.deep) for model in range(packing.mp)]
                for member in range(min(packing.per, MATRICES - group * packing.per)):
                    lane = member * packing.wide
                    wide_s[group * packing.per + member][data * packing.deep : (data + 1) * packing.deep, :] = (
                        jnp.concatenate([part[:, lane : lane + packing.wide] for part in parts], axis=1)
                    )
        stem_t[...] = wide_s[0][...].astype(BF)
        for layer in range(LAYERS):
            half_up = 0.5 * wide_s[1 + layer][...]
            half_down = 0.5 * wide_s[1 + LAYERS + layer][...]
            up_n[layer] = half_up.astype(BF)
            up_t[layer] = half_up.T.astype(BF)
            down_t[layer] = half_down.astype(BF)
            down_n[layer] = half_down.T.astype(BF)
        norm_parts = []
        total = None
        for device in devices:
            at = (device[0] * packing.mp + device[1]) * packing.own
            for tile in range(DEPTH // 128):
                begin = packing.head_at + packing.own * tile
                head_tile(tile)[at : at + packing.own, :] = rows_of(device, begin, begin + packing.own)
            tail = rows_of(device, packing.tail_at, packing.tail_at + 16)
            table_acc[at : at + packing.own, :] = tail[0 : packing.own, 0:CODES]
            norm_parts.append(tail[:, NORM_LANE : NORM_LANE + packing.own])
            amount = tail[SUM_ROW : SUM_ROW + 1] + tail[SUM_ROW + 1 : SUM_ROW + 2] + tail[SUM_ROW + 2 : SUM_ROW + 3]
            total = amount if total is None else total + amount
        table_t[...] = table_acc[...].astype(BF)
        for tile in range(DEPTH // 128):
            at = tile * 128
            whole = head_tile(tile)[...]
            head_n[:, at : at + 128] = whole.astype(BF)
            end = min(128, ROWS - at)
            head_t[at : at + end, :] = whole.T.astype(BF)[0:end]
        norms = jnp.concatenate(norm_parts, axis=1)
        columns = jnp.concatenate([norms, jnp.zeros((128 - norms.shape[0], D), F32)], axis=0).T
        for which in range(2 * (LAYERS + 1)):
            norm_s[which] = jnp.broadcast_to(columns[:, which : which + 1], (D, 128))
        scale_s[...] = jnp.broadcast_to(rows_all / total[:, SUM_LANE : SUM_LANE + 1], (1, LANES))

        stem_acc[...] = jnp.zeros_like(stem_acc)
        table_acc[...] = jnp.zeros_like(table_acc)
        up_acc[...] = jnp.zeros_like(up_acc)
        down_acc[...] = jnp.zeros_like(down_acc)
        head_acc[...] = jnp.zeros_like(head_acc)
        norm_part[...] = jnp.zeros_like(norm_part)
        lat_last[...] = jnp.zeros_like(lat_last)
        pre_last[...] = jnp.zeros_like(pre_last)
        hot_last[...] = jnp.zeros_like(hot_last)

    def norm_rows(which, at):
        half = norm_s[which, at : at + CHUNK, :]
        return jnp.concatenate([half] * (LANES // 128), axis=1)

    spans = [slice(at, at + CHUNK) for at in range(0, D, CHUNK)]
    norm_total = {}

    def add_norm(which, at, part):
        for lane in range(0, LANES, 128):
            piece = part[:, lane : lane + 128]
            norm_total[which, at] = norm_total[which, at] + piece if (which, at) in norm_total else piece

    def pieces(array, count=D, begin=0):
        return [array[begin + at : begin + min(at + CHUNK, count)] for at in range(0, count, CHUNK)]

    def joined(parts):
        return jnp.concatenate(parts, axis=0)

    def folded(parts):
        total = None
        for part in parts:
            total = fold_rows(total, part)
        return jnp.sum(total, axis=0, keepdims=True)

    def norm_forward(layer, stream, cols):
        mean = folded(stream) * (1.0 / D)
        centered = [part - mean for part in stream]
        rstd = lax.rsqrt(folded([part * part for part in centered]) * (1.0 / D) + eps_norm)
        rstd_s[layer, :, cols] = rstd
        values = []
        for rows, part in zip(spans, centered):
            centered_s[layer, rows, cols] = part
            value, slope = gelu_pair(
                (part * rstd) * norm_rows(2 * layer, rows.start) + norm_rows(2 * layer + 1, rows.start)
            )
            values.append(value)
            slope_s[layer, rows, cols] = slope
        return values

    def norm_backward(layer, grads, cols):
        rstd = rstd_s[layer, :, cols]
        centered = [centered_s[layer, rows, cols] for rows in spans]
        wide = []
        for rows, grad, part in zip(spans, grads, centered):
            grad = grad * slope_s[layer, rows, cols]
            add_norm(2 * layer + 1, rows.start, grad)
            grad = grad * rstd
            add_norm(2 * layer, rows.start, grad * part)
            wide.append(grad * norm_rows(2 * layer, rows.start))
        shift = folded(wide) * (1.0 / D)
        slant = folded([grad * part for grad, part in zip(wide, centered)]) * (1.0 / D) * (rstd * rstd)
        return [(grad - shift) - part * slant for grad, part in zip(wide, centered)]

    branches, inner_grads, lows, tops = ({} for _ in range(4))

    def beside(kept, *key):
        return jnp.concatenate([kept[(index,) + key] for index in range(chains)], axis=1)

    def row_of(ref, cols):
        return ref[cols].reshape(1, LANES)

    def hot_of(cols):
        return (lax.broadcasted_iota(jnp.int32, (CODES, LANES), 0) == row_of(code_ref, cols)).astype(F32).astype(BF)

    def forward(index):
        cols = slice(index * LANES, (index + 1) * LANES)
        stream = pieces(dot_nt(stem_t[...], lat_ref[cols, :]) + dot_nn(table_t[...], hot_of(cols)))
        yield
        stream = [0.5 * value for value in norm_forward(0, stream, cols)]
        yield
        for layer in range(1, LAYERS + 1):
            act = joined([value.astype(BF) for value in norm_forward(layer, stream, cols)])
            act_s[layer - 1, :, cols] = act
            yield
            inner = dot_nn(up_t[layer - 1], act)
            yield
            gated = []
            for rows, part in zip(spans, pieces(inner)):
                value, slope = gelu_pair(part)
                inner_slope_s[layer - 1, rows, cols] = slope
                gated.append(value.astype(BF))
            gated = joined(gated)
            gated_s[layer - 1, :, cols] = gated
            yield
            branch = dot_nn(down_t[layer - 1], gated)
            yield
            stream = [part + change for part, change in zip(stream, pieces(branch))]
        tops[(index,)] = joined([part.astype(BF) for part in stream])
        yield
        logits = dot_nn(head_t[...], tops[(index,)])
        yield
        coef = row_of(weight_ref, cols).astype(F32) * scale_s[...]
        sections = (
            (VALUE_AT, BINS, value_ref),
            (REWARD_AT, BINS, reward_ref),
            (CHANCE_AT, CODES, target_ref),
            (POLICY_AT, ACTIONS, action_ref),
        )
        low = []
        for begin, count, target_ref_of in sections:
            padded = -(-count // 8) * 8
            parts = [logits[begin + at : begin + min(at + CHUNK, padded)] for at in range(0, padded, CHUNK)]
            if padded != count:
                place = lax.broadcasted_iota(jnp.int32, parts[-1].shape, 0) + (padded - parts[-1].shape[0])
                parts[-1] = jnp.where(place < count, parts[-1], -1e30)
            peak = None
            for part in parts:
                peak = peak_rows(peak, part)
            peak = jnp.max(peak, axis=0, keepdims=True)
            powers = [jnp.exp2((part - peak) * LOG2E) for part in parts]
            scale = coef / folded(powers)
            target = row_of(target_ref_of, cols)
            for number, power in enumerate(powers):
                soft = power * scale
                place = lax.broadcasted_iota(jnp.int32, soft.shape, 0) + number * CHUNK
                soft = jnp.where(place == target, soft - coef, soft)
                missing = -soft.shape[0] % 16
                if missing:
                    soft = jnp.concatenate([soft, jnp.zeros((missing, LANES), F32)], axis=0)
                low.append(soft.astype(BF))
            yield
        low.append(jnp.zeros((DEPTH - ROWS, LANES), BF))
        low = joined(low)
        lows[(index,)] = low[0:ROWS]
        grad_s[:, cols] = dot_nn(head_n[...], low)
        if index == chains - 1:
            head_acc[0:ROWS, :] += dot_nt(beside(lows), beside(tops))

    def backward(index):
        cols = slice(index * LANES, (index + 1) * LANES)
        stream = [grad_s[rows, cols] for rows in spans]
        for layer in range(LAYERS, 0, -1):
            branches[index, layer] = joined([part.astype(BF) for part in stream])
            yield
            gated_grad = dot_nn(down_n[layer - 1], branches[index, layer])
            yield
            inner_grads[index, layer] = joined(
                [
                    (part * inner_slope_s[layer - 1, rows, cols]).astype(BF)
                    for rows, part in zip(spans, pieces(gated_grad))
                ]
            )
            yield
            active_grad = dot_nn(up_n[layer - 1], inner_grads[index, layer])
            if index == chains - 1:
                down_acc[layer - 1] += dot_nt(beside(branches, layer), gated_s[layer - 1])
                up_acc[layer - 1] += dot_nt(act_s[layer - 1], beside(inner_grads, layer))
            yield
            changes = norm_backward(layer, pieces(active_grad), cols)
            stream = [part + change for part, change in zip(stream, changes)]
            yield
        pre = joined([part.astype(BF) for part in norm_backward(0, [0.5 * part for part in stream], cols)])
        yield
        lat_grad[cols, :] = dot_tn(pre, stem_t[...])
        pre_last[:, cols] = pre
        hot_last[:, cols] = hot_of(cols)
        lat_last[cols, :] = lat_ref[cols, :]

    def stem_grads():
        stem_acc[...] += dot_nn(pre_last[...], lat_last[...])
        table_acc[...] += dot_nt(pre_last[...], hot_last[...])

    def together(way):
        running, waiting = [], [way(index) for index in range(chains)]
        while running or waiting:
            if waiting:
                running.append(waiting.pop(0))
            for member in list(running):
                try:
                    next(member)
                except StopIteration:
                    running.remove(member)

    @pl.when(gate_ref[0] == 0)
    def _():
        stem_grads()
        together(forward)

    @pl.when(gate_ref[0] == 0)
    def _():
        together(backward)
        for (which, at), total in norm_total.items():
            norm_part[which, at : at + CHUNK, :] += total

    @pl.when(step == pl.num_programs(0) - 1)
    def _():
        stem_grads()
        for at in range(0, DEPTH, D):
            head_acc[at : at + D, :] = head_acc[at : at + D, :].T
        lane_at = lax.broadcasted_iota(jnp.int32, (D, 128), 1)
        columns = jnp.zeros((D, 128), F32)
        for which in range(2 * (LAYERS + 1)):
            columns = jnp.where(lane_at == which, jnp.sum(norm_part[which], axis=1, keepdims=True), columns)
        norms = columns.T[0:16]
        def pieces_of(data, model):
            at = (data * packing.mp + model) * packing.own
            deep = slice(data * packing.deep, (data + 1) * packing.deep)
            wide = slice(model * packing.wide, (model + 1) * packing.wide)
            squares = [lambda: stem_acc[deep, wide]]
            squares += [lambda layer=layer: 0.5 * up_acc[layer, deep, wide] for layer in range(LAYERS)]
            squares += [lambda layer=layer: 0.5 * down_acc[layer, deep, wide] for layer in range(LAYERS)]
            for group in range(packing.groups):
                members = squares[group * packing.per : (group + 1) * packing.per]
                yield (
                    group * packing.deep,
                    slice(0, packing.wide * len(members)),
                    lambda members=members: jnp.concatenate([member() for member in members], axis=1),
                )
            for tile in range(DEPTH // 128):
                yield (
                    packing.head_at + packing.own * tile,
                    slice(0, 128),
                    lambda tile=tile: head_tile(tile)[at : at + packing.own, :],
                )
            own = slice(at, at + packing.own)
            yield packing.tail_at, slice(0, CODES), lambda: table_acc[own, :]
            yield (
                packing.tail_at,
                slice(NORM_LANE, NORM_LANE + packing.own),
                lambda: norms[0 : 2 * (LAYERS + 1), own],
            )

        leaving = []
        for side in range(PARTS):
            owners = {slot_of(packing.orders[side], *device): device for device in devices}
            for chunk in range(chunks):
                number = side * chunks + chunk
                place = departing.at[number % RING]
                if number >= RING:
                    leaving[number - RING].wait()
                place[...] = jnp.zeros((D, 128), F32)
                for row in range(0, D, packing.part):
                    for begin, lanes, value in pieces_of(*owners[(chunk * D + row) // packing.part]):
                        if begin // packing.part == side:
                            rows = value()
                            first = row + begin - side * packing.part
                            place[first : first + rows.shape[0], lanes] = rows
                leaving.append(
                    pltpu.make_async_copy(
                        place, outs[side].at[chunk * D : (chunk + 1) * D], copy_sem.at[side, chunk]
                    )
                )
                leaving[-1].start()
        for member in leaving[-RING:]:
            member.wait()


def train(packing, rows_all, latent, code, weight, value, reward, action, target, packed):
    count = latent.shape[0]
    chains = CHAINS
    block = chains * LANES

    def row():
        return pl.BlockSpec((block,), lambda i: (i,))

    parts = [pl.BlockSpec(memory_space=pl.ANY)] * PARTS
    flat = jax.ShapeDtypeStruct((packing.count * packing.part, 128), F32)
    packed = [member.reshape(-1, 128) for member in packed]
    return pl.pallas_call(
        functools.partial(train_kernel, packing, rows_all, chains),
        grid=(count // block,),
        out_shape=[jax.ShapeDtypeStruct((count, D), F32)] + [flat] * PARTS,
        in_specs=[pl.BlockSpec((block, D), lambda i: (i, 0))]
        + [row() for _ in range(6)]
        + [pl.BlockSpec(memory_space=pltpu.SMEM)]
        + parts,
        out_specs=[pl.BlockSpec((block, D), lambda i: (i, 0))] + parts,
        scratch_shapes=[
            pltpu.VMEM((D, D), F32),
            pltpu.VMEM((D, CODES), F32),
            pltpu.VMEM((LAYERS, D, D), F32),
            pltpu.VMEM((LAYERS, D, D), F32),
            pltpu.VMEM((DEPTH, D), F32),
            pltpu.VMEM((D, D), BF),
            pltpu.VMEM((D, CODES), BF),
            pltpu.VMEM((LAYERS, D, D), BF),
            pltpu.VMEM((LAYERS, D, D), BF),
            pltpu.VMEM((LAYERS, D, D), BF),
            pltpu.VMEM((LAYERS, D, D), BF),
            pltpu.VMEM((ROWS, D), BF),
            pltpu.VMEM((D, DEPTH), BF),
            pltpu.VMEM((1, LANES), F32),
            pltpu.VMEM((2 * (LAYERS + 1), D, 128), F32),
            pltpu.VMEM((2 * (LAYERS + 1), D, 128), F32),
            pltpu.VMEM((block, D), BF),
            pltpu.VMEM((D, block), BF),
            pltpu.VMEM((CODES, block), BF),
            pltpu.VMEM((LAYERS + 1, D, block), F32),
            pltpu.VMEM((LAYERS + 1, D, block), F32),
            pltpu.VMEM((LAYERS, D, block), F32),
            pltpu.VMEM((LAYERS + 1, 1, block), F32),
            pltpu.VMEM((LAYERS, D, block), BF),
            pltpu.VMEM((LAYERS, D, block), BF),
            pltpu.VMEM((D, block), F32),
            pltpu.VMEM((PARTS * packing.count * packing.part // D, D, 128), BF),
            pltpu.VMEM((RING, D, 128), F32),
            pltpu.SemaphoreType.DMA((PARTS, packing.count * packing.part // D)),
        ],
        compiler_params=pltpu.CompilerParams(
            dimension_semantics=("arbitrary",), vmem_limit_bytes=60 * 1024 * 1024
        ),
        name="train",
    )(latent, code, weight, value, reward, action, target, jnp.zeros((1,), jnp.int32), *packed)


def body(rows_all, packing, *args):
    latent, code, weight, value, reward, action, target = args[:7]
    groups = [args[7 + 3 * which : 10 + 3 * which] for which in range(6)]

    def turn(which, array):
        return jnp.swapaxes(array, -1, -2) if which in (0, 2, 4) else array

    groups = [tuple(turn(which, member) for member in group) for which, group in enumerate(groups)]
    stem, up, down, head, table, norm = (group[0] for group in groups)
    packed = send_weights(packing, stem, up, down, head, table, norm, weight.reshape(-1, 128))
    lat_grad, *grads = train(packing, rows_all, latent, code, weight, value, reward, action, target, packed)
    own = reduce_grads(packing, [member.reshape(packing.count, packing.part, 128) for member in grads])
    outs = update(packing, rows_all, own, groups)
    result = [outs[0].reshape(()), lat_grad]
    at = 1
    for which in range(6):
        for _ in range(4 if which < 5 else 3):
            result.append(turn(which, outs[at]))
            at += 1
    return tuple(result)


def solution(mesh):
    every = ("dp", "mp")
    states, flat = P(every, None), P(every)
    params = (P("mp", "dp"), P(None, "dp", "mp"), P(None, "mp", "dp"), P(every, None), P(None, every), P(None, None, every))
    in_specs = (states,) + (flat,) * 6 + tuple(spec for spec in params for _ in range(3))
    out_specs = (P(), states) + tuple(spec for which, spec in enumerate(params) for _ in range(4 if which < 5 else 3))
    packing = Packing(mesh.shape["dp"], mesh.shape["mp"])

    def run(*args):
        rows_all = args[0].shape[0] * packing.count
        return body(rows_all, packing, *args)

    return jax.shard_map(run, mesh=mesh, in_specs=in_specs, out_specs=out_specs, check_vma=False)
```

```python
import functools
import math

import jax
import jax.numpy as jnp
from jax import lax
from jax.experimental import pallas as pl
from jax.experimental.pallas import tpu as pltpu
from jax.sharding import PartitionSpec as P

D = 256
BINS = 601
ACTIONS = 4
CODES = 32
LAYERS = 4
STEP = 10

VALUE_AT = 0
REWARD_AT = 608
CHANCE_AT = 1216
POLICY_AT = 1248
ROWS = 1264
DEPTH = 1280

beta_one = 0.9
beta_two = 0.99
eps_adam = 1e-08
eps_norm = 1e-05
matrix_rate = 0.2
vector_rate = 0.6
decay_rate = 0.1
clip_scale = 3.0

GELU_A = math.sqrt(2.0 / math.pi)
GELU_B = GELU_A * 0.044715
LOG2E = 1.4426950408889634
LANES = 256
CHAINS = 4
PARTS = 4
RING = 16
CHUNK = 16
BF = jnp.bfloat16
F32 = jnp.float32
MESH = pl.DeviceIdType.MESH
MATRICES = 1 + 2 * LAYERS
NORM_LANE = 32
SUM_LANE = 64
SUM_ROW = 10


def dot_nn(left, right):
    return lax.dot_general(left, right, (((1,), (0,)), ((), ())), preferred_element_type=F32)


def dot_nt(left, right):
    return lax.dot_general(left, right, (((1,), (1,)), ((), ())), preferred_element_type=F32)


def dot_tn(left, right):
    return lax.dot_general(left, right, (((0,), (0,)), ((), ())), preferred_element_type=F32)


def gelu_pair(v):
    square = v * v
    gate = 1.0 + jnp.tanh(v * (GELU_A + GELU_B * square))
    value = v * gate
    slope = gate + value * (2.0 - gate) * (GELU_A + 3.0 * GELU_B * square)
    return value, slope


def fold_rows(total, part):
    for at in range(0, part.shape[0], 8):
        piece = part[at : at + 8]
        total = piece if total is None else total + piece
    return total


def peak_rows(total, part):
    for at in range(0, part.shape[0], 8):
        piece = part[at : at + 8]
        total = piece if total is None else jnp.maximum(total, piece)
    return total


def orders_of(dp, mp):
    def step(axis, low, size):
        return (axis, low, size) if size > 1 else None

    far_dp, near_dp = step("dp", 2, dp // 2), step("dp", 1, 2)
    far_mp, near_mp = step("mp", 2, mp // 2), step("mp", 1, 2)
    return (
        [member for member in (far_dp, near_dp, far_mp, near_mp) if member],
        [member for member in (far_dp, far_mp, near_dp, near_mp) if member],
    )


def digit_of(step, data, model):
    axis, low, ways = step
    return ((data if axis == "dp" else model) // low) % ways


def slot_of(order, data, model):
    place, weight = 0, 1
    for step in order:
        place = place + digit_of(step, data, model) * weight
        weight *= step[2]
    return place


def partner_of(step, away):
    axis, low, ways = step
    index = lax.axis_index(axis)
    digit = (index // low) % ways
    other = (digit + away) % ways
    return {axis: index + (other - digit) * low}, other - digit


def sizes_of(order):
    sizes = [1]
    for step in order:
        sizes.append(sizes[-1] * step[2])
    return sizes


class Packing:
    def __init__(self, dp, mp):
        self.dp, self.mp, self.count = dp, mp, dp * mp
        self.deep, self.wide, self.own = D // dp, D // mp, D // (dp * mp)
        self.per = 128 // self.wide
        self.groups = -(-MATRICES // self.per)
        self.head_at = self.groups * self.deep
        self.tail_at = -(-(self.head_at + self.own * (DEPTH // 128)) // 16) * 16
        self.rows = -(-(self.tail_at + 16) // (16 * PARTS)) * 16 * PARTS
        self.part = self.rows // PARTS
        self.orders = [orders_of(dp, mp)[number % 2] for number in range(PARTS)]
        self.sizes = [sizes_of(order) for order in self.orders]
        self.most = max(step[2] for step in self.orders[0])

    def split(self, begin, end):
        side = begin // self.part
        assert (end - 1) // self.part == side
        return side, slice(begin - side * self.part, end - side * self.part)

    def shapes(self, dtype):
        return [jax.ShapeDtypeStruct((self.count, self.part, 128), dtype)] * PARTS

    def scratch(self, dtype):
        return [pltpu.VMEM((self.count, self.part, 128), dtype)] * PARTS


def pad_lanes(array, lanes):
    missing = lanes - array.shape[1]
    return array if missing == 0 else jnp.concatenate([array, jnp.zeros((array.shape[0], missing), array.dtype)], axis=1)


def spread_head(head):
    rows = head.shape[0]

    def blank(count):
        return jnp.zeros((rows, count), head.dtype)

    return jnp.concatenate(
        [
            head[:, :BINS],
            blank(REWARD_AT - BINS),
            head[:, BINS : 2 * BINS],
            blank(CHANCE_AT - REWARD_AT - BINS),
            head[:, 2 * BINS + ACTIONS :],
            head[:, 2 * BINS : 2 * BINS + ACTIONS],
            blank(DEPTH - POLICY_AT - ACTIONS),
        ],
        axis=1,
    )


def gather_head(padded):
    return jnp.concatenate(
        [
            padded[:, VALUE_AT : VALUE_AT + BINS],
            padded[:, REWARD_AT : REWARD_AT + BINS],
            padded[:, POLICY_AT : POLICY_AT + ACTIONS],
            padded[:, CHANCE_AT : CHANCE_AT + CODES],
        ],
        axis=1,
    )


def send_kernel(packing, *refs):
    stem, up, down, head, table, norm, weight = refs[:7]
    outs, kinds = refs[7 : 7 + PARTS], refs[7 + PARTS : 7 + 2 * PARTS]
    block, send_sem, recv_sem, keep_sem = refs[7 + 2 * PARTS :]
    partners = [(step, away) for step in packing.orders[0] for away in range(1, step[2])]
    barrier = pltpu.get_barrier_semaphore()
    for step, away in partners:
        pl.semaphore_signal(barrier, inc=1, device_id=partner_of(step, away)[0], device_id_type=MESH)

    block[...] = jnp.zeros_like(block)
    matrices = [stem[...]] + [up[layer] for layer in range(LAYERS)] + [down[layer] for layer in range(LAYERS)]
    for group in range(packing.groups):
        members = matrices[group * packing.per : (group + 1) * packing.per]
        block[group * packing.deep : (group + 1) * packing.deep, :] = pad_lanes(jnp.concatenate(members, axis=1), 128)
    padded = spread_head(head[...])
    for tile in range(DEPTH // 128):
        at = packing.head_at + packing.own * tile
        block[at : at + packing.own, :] = padded[:, tile * 128 : (tile + 1) * 128]
    at = packing.tail_at
    block[at : at + packing.own, 0:CODES] = table[...]
    for layer in range(LAYERS + 1):
        block[at + 2 * layer : at + 2 * layer + 2, NORM_LANE : NORM_LANE + packing.own] = norm[layer]
    amount = jnp.sum(jnp.sum(weight[...].astype(F32), axis=0, keepdims=True), axis=1, keepdims=True)
    amount = jnp.broadcast_to(amount, (1, 128))
    for row in range(SUM_ROW, SUM_ROW + 3):
        part = amount.astype(BF).astype(F32)
        block[at + row : at + row + 1, SUM_LANE:128] = part[:, SUM_LANE:128]
        amount = amount - part
    data, model = lax.axis_index("dp"), lax.axis_index("mp")
    slots = [slot_of(order, data, model) for order in packing.orders]
    for side in range(PARTS):
        kinds[side][slots[side]] = block[side * packing.part : (side + 1) * packing.part, :].astype(BF)

    pl.semaphore_wait(barrier, len(partners))

    def copies_of(side, number):
        step, size = packing.orders[side][number], packing.sizes[side][number]
        held = kinds[side].at[pl.ds((slots[side] // size) * size, size)]
        return [
            pltpu.make_async_remote_copy(
                src_ref=held,
                dst_ref=held,
                send_sem=send_sem.at[side, number, away],
                recv_sem=recv_sem.at[side, number, away],
                device_id=partner_of(step, away)[0],
                device_id_type=MESH,
            )
            for away in range(1, step[2])
        ]

    def kept(side, start, size, sem):
        return pltpu.make_async_copy(
            kinds[side].at[pl.ds(start, size)], outs[side].at[pl.ds(start, size)], keep_sem.at[side, sem]
        )

    steps = len(packing.orders[0])
    copies = [[copies_of(side, number) for number in range(steps)] for side in range(PARTS)]
    local = [kept(side, slots[side], 1, 0) for side in range(PARTS)]
    for member in local:
        member.start()
    for number in range(steps + 1):
        for side in range(PARTS):
            if number:
                for member in copies[side][number - 1]:
                    member.wait_recv()
            if number < steps:
                for member in copies[side][number]:
                    member.start()
            if number:
                step, size = packing.orders[side][number - 1], packing.sizes[side][number - 1]
                for away in range(1, step[2]):
                    start = (slots[side] // size) * size + partner_of(step, away)[1] * size
                    local.append(kept(side, start, size, number * packing.most + away))
                    local[-1].start()
    for member in local:
        member.wait()
    for side in range(PARTS):
        for number in range(steps):
            for member in copies[side][number]:
                member.wait_send()


def send_weights(packing, stem, up, down, head, table, norm, weight):
    steps = len(packing.orders[0])
    return pl.pallas_call(
        functools.partial(send_kernel, packing),
        out_shape=packing.shapes(BF),
        in_specs=[pl.BlockSpec()] * 7,
        out_specs=[pl.BlockSpec(memory_space=pl.ANY)] * PARTS,
        scratch_shapes=packing.scratch(BF)
        + [
            pltpu.VMEM((packing.rows, 128), F32),
            pltpu.SemaphoreType.DMA((PARTS, steps, packing.most)),
            pltpu.SemaphoreType.DMA((PARTS, steps, packing.most)),
            pltpu.SemaphoreType.DMA((PARTS, (steps + 1) * packing.most)),
        ],
        compiler_params=pltpu.CompilerParams(
            collective_id=0, has_side_effects=True, vmem_limit_bytes=60 * 1024 * 1024
        ),
        name="send_weights",
    )(stem, up, down, head, table, norm, weight)


def reduce_kernel(packing, *refs):
    given, own = refs[:PARTS], refs[PARTS]
    held, sent, got = (refs[PARTS * kind + 1 : PARTS * (kind + 1) + 1] for kind in (1, 2, 3))
    across, along, send_sem, recv_sem, part_send, part_recv, fetch_sem = refs[4 * PARTS + 1 :]
    fetches = [pltpu.make_async_copy(given[side], held[side], fetch_sem.at[side]) for side in range(PARTS)]
    for member in fetches:
        member.start()
    steps = len(packing.orders[0])
    data, model = lax.axis_index("dp"), lax.axis_index("mp")
    barrier = pltpu.get_barrier_semaphore()
    for away in range(1, packing.mp):
        pl.semaphore_signal(barrier, inc=1, device_id={"mp": (model + away) % packing.mp}, device_id_type=MESH)
    for away in range(1, packing.dp):
        pl.semaphore_signal(barrier, inc=1, device_id={"dp": (data + away) % packing.dp}, device_id_type=MESH)

    slots = [slot_of(order, data, model) for order in packing.orders]

    def mine_of(side, number):
        size = packing.sizes[side][number]
        return (slots[side] // size) * size

    def place_of(side, number, away):
        size = packing.sizes[side][number]
        return pl.ds(size * away, size)

    def pack(side, number):
        step, size = packing.orders[side][number], packing.sizes[side][number]
        for away in range(1, step[2]):
            block = mine_of(side, number) + partner_of(step, away)[1] * size
            sent[side][place_of(side, number, away)] = held[side][pl.ds(block, size)].astype(BF)

    def copies_of(side, number):
        step = packing.orders[side][number]
        return [
            pltpu.make_async_remote_copy(
                src_ref=sent[side].at[place_of(side, number, away)],
                dst_ref=got[side].at[place_of(side, number, away)],
                send_sem=send_sem.at[side, number, away],
                recv_sem=recv_sem.at[side, number, away],
                device_id=partner_of(step, away)[0],
                device_id_type=MESH,
            )
            for away in range(1, step[2])
        ]

    def take(side, number):
        rows = pl.ds(mine_of(side, number), packing.sizes[side][number])
        total = held[side][rows]
        for away in range(1, packing.orders[side][number][2]):
            total = total + got[side][place_of(side, number, away)].astype(F32)
        held[side][rows] = total

    copies = [[copies_of(side, number) for number in range(steps)] for side in range(PARTS)]
    pl.semaphore_wait(barrier, packing.mp + packing.dp - 2)
    for number in range(steps - 1, -1, -1):
        for side in range(PARTS):
            if number < steps - 1:
                for member in copies[side][number + 1]:
                    member.wait_recv()
                take(side, number + 1)
            else:
                fetches[side].wait()
            pack(side, number)
            for member in copies[side][number]:
                member.start()
    total = None
    for side in range(PARTS):
        for member in copies[side][0]:
            member.wait_recv()
        take(side, 0)
        block = held[side][slots[side]]
        own[side * packing.part : (side + 1) * packing.part, :] = block
        total = fold_rows(total, block * block)

    def exchange(axis, index, count, buffer, value, first):
        buffer[index] = value
        going = []
        for away in range(1, count):
            going.append(
                pltpu.make_async_remote_copy(
                    src_ref=buffer.at[index],
                    dst_ref=buffer.at[index],
                    send_sem=part_send.at[first + away],
                    recv_sem=part_recv.at[first + away],
                    device_id={axis: (index + away) % count},
                    device_id_type=MESH,
                )
            )
            going[-1].start()
        for member in going:
            member.wait_recv()
        whole = buffer[0]
        for other in range(1, count):
            whole = whole + buffer[other]
        return whole, going

    total, going = exchange("mp", model, packing.mp, across, total, 0)
    total, more = exchange("dp", data, packing.dp, along, total, packing.mp)
    own[packing.rows : packing.rows + 8, :] = total
    for member in going + more:
        member.wait_send()
    for side in range(PARTS):
        for number in range(steps):
            for member in copies[side][number]:
                member.wait_send()


def reduce_grads(packing, grads):
    steps = len(packing.orders[0])
    vmem = pl.BlockSpec(memory_space=pltpu.VMEM)
    return pl.pallas_call(
        functools.partial(reduce_kernel, packing),
        out_shape=jax.ShapeDtypeStruct((packing.rows + 8, 128), F32),
        in_specs=[pl.BlockSpec(memory_space=pl.ANY)] * PARTS,
        out_specs=vmem,
        scratch_shapes=packing.scratch(F32)
        + packing.scratch(BF) * 2
        + [
            pltpu.VMEM((packing.mp, 8, 128), F32),
            pltpu.VMEM((packing.dp, 8, 128), F32),
            pltpu.SemaphoreType.DMA((PARTS, steps, packing.most)),
            pltpu.SemaphoreType.DMA((PARTS, steps, packing.most)),
            pltpu.SemaphoreType.DMA((packing.mp + packing.dp,)),
            pltpu.SemaphoreType.DMA((packing.mp + packing.dp,)),
            pltpu.SemaphoreType.DMA((PARTS,)),
        ],
        compiler_params=pltpu.CompilerParams(
            collective_id=1, has_side_effects=True, vmem_limit_bytes=60 * 1024 * 1024
        ),
        name="reduce_grads",
    )(*grads)


def adam_rows(weight, moment, square, grad, rate, decay):
    first = beta_one * moment + (1.0 - beta_one) * grad
    second = beta_two * square + (1.0 - beta_two) * grad * grad
    first_hat = first / (1.0 - beta_one**STEP)
    second_hat = second / (1.0 - beta_two**STEP)
    updated = weight - rate * (first_hat / (jnp.sqrt(second_hat) + eps_adam) + decay * weight)
    return (updated, first, second)


def update_kernel(packing, rows_all, own, *refs):
    ins, outs = refs[:18], refs[18:]
    grad_norm, outs = outs[0], outs[1:]
    squares = own[packing.rows : packing.rows + 8, :]
    whole = jnp.sum(jnp.sum(squares, axis=0, keepdims=True), axis=1, keepdims=True)
    norm = jnp.sqrt(whole)
    grad_norm[...] = norm
    ratio = jnp.minimum(1.0, clip_scale * math.sqrt(rows_all) / norm)

    def apply(which, index, grad, rate=matrix_rate, decay=decay_rate):
        weight, moment, square = (ins[3 * which + kind][index] for kind in range(3))
        base = 4 * which
        new, first, second = adam_rows(weight, moment, square, grad * ratio, rate, decay)
        outs[base][index] = new
        outs[base + 1][index] = first
        outs[base + 2][index] = second
        if which < 5:
            outs[base + 3][index] = new.astype(BF)

    def matrix(member):
        at = (member // packing.per) * packing.deep
        lane = (member % packing.per) * packing.wide
        return own[at : at + packing.deep, lane : lane + packing.wide]

    apply(0, ..., matrix(0))
    for layer in range(LAYERS):
        apply(1, layer, matrix(1 + layer))
        apply(2, layer, matrix(1 + LAYERS + layer))
    tiles = [
        own[packing.head_at + packing.own * tile : packing.head_at + packing.own * (tile + 1), :]
        for tile in range(DEPTH // 128)
    ]
    apply(3, ..., gather_head(jnp.concatenate(tiles, axis=1)))
    at = packing.tail_at
    apply(4, ..., own[at : at + packing.own, 0:CODES])
    for layer in range(LAYERS + 1):
        apply(
            5,
            layer,
            own[at + 2 * layer : at + 2 * layer + 2, NORM_LANE : NORM_LANE + packing.own],
            vector_rate,
            0.0,
        )


def update(packing, rows_all, own, groups):
    ins = [member for group in groups for member in group]
    outs = [jax.ShapeDtypeStruct((1, 1), F32)]
    for which, group in enumerate(groups):
        outs += [jax.ShapeDtypeStruct(group[0].shape, F32)] * 3
        if which < 5:
            outs.append(jax.ShapeDtypeStruct(group[0].shape, BF))
    return pl.pallas_call(
        functools.partial(update_kernel, packing, rows_all),
        out_shape=outs,
        in_specs=[pl.BlockSpec()] * (1 + len(ins)),
        out_specs=[pl.BlockSpec()] * len(outs),
        compiler_params=pltpu.CompilerParams(vmem_limit_bytes=48 * 1024 * 1024),
        name="update",
    )(own, *ins)


def train_kernel(
    packing,
    rows_all,
    chains,
    lat_ref,
    code_ref,
    weight_ref,
    value_ref,
    reward_ref,
    action_ref,
    target_ref,
    *refs,
):
    held, lat_grad, outs = refs[:PARTS], refs[PARTS], refs[PARTS + 1 : 2 * PARTS + 1]
    (
        stem_acc,
        table_acc,
        up_acc,
        down_acc,
        head_acc,
        stem_t,
        table_t,
        up_t,
        up_n,
        down_t,
        down_n,
        head_t,
        head_n,
        scale_s,
        norm_s,
        norm_part,
        lat_last,
        pre_last,
        hot_last,
        arriving,
        departing,
        copy_sem,
    ) = refs[2 * PARTS + 1 :]
    step = pl.program_id(0)
    chunks = packing.count * packing.part // D

    def head_tile(tile):
        return head_acc.at[(tile // 2) * D : (tile // 2 + 1) * D, (tile % 2) * 128 : (tile % 2 + 1) * 128]

    devices = [(data, model) for data in range(packing.dp) for model in range(packing.mp)]

    @pl.when(step == 0)
    def _():
        arrived = [
            pltpu.make_async_copy(
                held[side].at[chunk * D : (chunk + 1) * D],
                arriving.at[side * chunks + chunk],
                copy_sem.at[side, chunk],
            )
            for side in range(PARTS)
            for chunk in range(chunks)
        ]
        for member in arrived:
            member.start()
        for member in arrived:
            member.wait()

        def rows_of(device, begin, end):
            side, rows = packing.split(begin, end)
            chunk, row = divmod(slot_of(packing.orders[side], *device) * packing.part, D)
            return arriving[side * chunks + chunk, row : row + packing.part, :].astype(F32)[rows]

        wide_s = [stem_acc] + [up_acc.at[layer] for layer in range(LAYERS)] + [down_acc.at[layer] for layer in range(LAYERS)]
        for data in range(packing.dp):
            for group in range(packing.groups):
                begin = group * packing.deep
                parts = [rows_of((data, model), begin, begin + packing.deep) for model in range(packing.mp)]
                for member in range(min(packing.per, MATRICES - group * packing.per)):
                    lane = member * packing.wide
                    wide_s[group * packing.per + member][data * packing.deep : (data + 1) * packing.deep, :] = (
                        jnp.concatenate([part[:, lane : lane + packing.wide] for part in parts], axis=1)
                    )
        stem_t[...] = wide_s[0][...].astype(BF)
        for layer in range(LAYERS):
            half_up = 0.5 * wide_s[1 + layer][...]
            half_down = 0.5 * wide_s[1 + LAYERS + layer][...]
            up_n[layer] = half_up.astype(BF)
            up_t[layer] = half_up.T.astype(BF)
            down_t[layer] = half_down.astype(BF)
            down_n[layer] = half_down.T.astype(BF)
        norm_parts = []
        total = None
        for device in devices:
            at = (device[0] * packing.mp + device[1]) * packing.own
            for tile in range(DEPTH // 128):
                begin = packing.head_at + packing.own * tile
                head_tile(tile)[at : at + packing.own, :] = rows_of(device, begin, begin + packing.own)
            tail = rows_of(device, packing.tail_at, packing.tail_at + 16)
            table_acc[at : at + packing.own, :] = tail[0 : packing.own, 0:CODES]
            norm_parts.append(tail[:, NORM_LANE : NORM_LANE + packing.own])
            amount = tail[SUM_ROW : SUM_ROW + 1] + tail[SUM_ROW + 1 : SUM_ROW + 2] + tail[SUM_ROW + 2 : SUM_ROW + 3]
            total = amount if total is None else total + amount
        table_t[...] = table_acc[...].astype(BF)
        for tile in range(DEPTH // 128):
            at = tile * 128
            whole = head_tile(tile)[...]
            head_n[:, at : at + 128] = whole.astype(BF)
            end = min(128, ROWS - at)
            head_t[at : at + end, :] = whole.T.astype(BF)[0:end]
        norms = jnp.concatenate(norm_parts, axis=1)
        columns = jnp.concatenate([norms, jnp.zeros((128 - norms.shape[0], D), F32)], axis=0).T
        for which in range(2 * (LAYERS + 1)):
            norm_s[which] = jnp.broadcast_to(columns[:, which : which + 1], (D, 128))
        scale_s[...] = jnp.broadcast_to(rows_all / total[:, SUM_LANE : SUM_LANE + 1], (1, LANES))

        stem_acc[...] = jnp.zeros_like(stem_acc)
        table_acc[...] = jnp.zeros_like(table_acc)
        up_acc[...] = jnp.zeros_like(up_acc)
        down_acc[...] = jnp.zeros_like(down_acc)
        head_acc[...] = jnp.zeros_like(head_acc)
        norm_part[...] = jnp.zeros_like(norm_part)
        lat_last[...] = jnp.zeros_like(lat_last)
        pre_last[...] = jnp.zeros_like(pre_last)
        hot_last[...] = jnp.zeros_like(hot_last)

    def norm_rows(which, at):
        half = norm_s[which, at : at + CHUNK, :]
        return jnp.concatenate([half] * (LANES // 128), axis=1)

    spans = [slice(at, at + CHUNK) for at in range(0, D, CHUNK)]
    norm_total = {}

    def add_norm(which, at, part):
        for lane in range(0, LANES, 128):
            piece = part[:, lane : lane + 128]
            norm_total[which, at] = norm_total[which, at] + piece if (which, at) in norm_total else piece

    def pieces(array, count=D, begin=0):
        return [array[begin + at : begin + min(at + CHUNK, count)] for at in range(0, count, CHUNK)]

    def joined(parts):
        return jnp.concatenate(parts, axis=0)

    def folded(parts):
        total = None
        for part in parts:
            total = fold_rows(total, part)
        return jnp.sum(total, axis=0, keepdims=True)

    marks = {}

    def mark(index, what, row):
        marks[index, what] = jnp.minimum(jnp.abs(row), 0.0)

    def after(index, what, row):
        return row if index == 0 else row + marks[index - 1, what]

    def norm_forward(index, layer, stream):
        mean = after(index, ("norm", layer), folded(stream) * (1.0 / D))
        centered = [part - mean for part in stream]
        rstd = lax.rsqrt(folded([part * part for part in centered]) * (1.0 / D) + eps_norm)
        values, slopes = [], []
        for rows, part in zip(spans, centered):
            value, slope = gelu_pair(
                (part * rstd) * norm_rows(2 * layer, rows.start) + norm_rows(2 * layer + 1, rows.start)
            )
            values.append(value)
            slopes.append(slope)
        mark(index, ("norm", layer), values[-1][0:1])
        return values, (centered, rstd, slopes)

    def norm_backward(index, layer, grads, kept):
        centered, rstd, slopes = kept
        rstd = after(index, ("back", layer), rstd)
        wide = []
        for rows, grad, part, slope in zip(spans, grads, centered, slopes):
            grad = grad * slope
            add_norm(2 * layer + 1, rows.start, grad)
            grad = grad * rstd
            add_norm(2 * layer, rows.start, grad * part)
            wide.append(grad * norm_rows(2 * layer, rows.start))
        shift = folded(wide) * (1.0 / D)
        slant = folded([grad * part for grad, part in zip(wide, centered)]) * (1.0 / D) * (rstd * rstd)
        changes = [(grad - shift) - part * slant for grad, part in zip(wide, centered)]
        mark(index, ("back", layer), changes[-1][0:1])
        return changes

    acts, gateds, branches, inner_grads, lows, tops = ({} for _ in range(6))

    def beside(kept, *key):
        return jnp.concatenate([kept[(index,) + key] for index in range(chains)], axis=1)

    def chain(index):
        cols = slice(index * LANES, (index + 1) * LANES)

        def row_of(ref):
            return ref[cols].reshape(1, LANES)

        hot = (lax.broadcasted_iota(jnp.int32, (CODES, LANES), 0) == row_of(code_ref)).astype(F32).astype(BF)
        stream = pieces(dot_nt(stem_t[...], lat_ref[cols, :]) + dot_nn(table_t[...], hot))
        yield
        kept, inner_slopes = {}, {}
        values, kept[0] = norm_forward(index, 0, stream)
        stream = [0.5 * value for value in values]
        yield
        for layer in range(1, LAYERS + 1):
            values, kept[layer] = norm_forward(index, layer, stream)
            acts[index, layer] = joined([value.astype(BF) for value in values])
            yield
            inner = dot_nn(up_t[layer - 1], acts[index, layer])
            yield
            both = [gelu_pair(part) for part in pieces(inner)]
            inner_slopes[layer] = [slope for _, slope in both]
            gateds[index, layer] = joined([value.astype(BF) for value, _ in both])
            yield
            branch = dot_nn(down_t[layer - 1], gateds[index, layer])
            yield
            stream = [part + change for part, change in zip(stream, pieces(branch))]
        tops[(index,)] = joined([part.astype(BF) for part in stream])
        yield
        logits = dot_nn(head_t[...], tops[(index,)])
        yield
        coef = row_of(weight_ref).astype(F32) * scale_s[...]
        sections = (
            (VALUE_AT, BINS, value_ref),
            (REWARD_AT, BINS, reward_ref),
            (CHANCE_AT, CODES, target_ref),
            (POLICY_AT, ACTIONS, action_ref),
        )
        low = []
        for begin, count, target_ref_of in sections:
            padded = -(-count // 8) * 8
            parts = [logits[begin + at : begin + min(at + CHUNK, padded)] for at in range(0, padded, CHUNK)]
            if padded != count:
                place = lax.broadcasted_iota(jnp.int32, parts[-1].shape, 0) + (padded - parts[-1].shape[0])
                parts[-1] = jnp.where(place < count, parts[-1], -1e30)
            peak = None
            for part in parts:
                peak = peak_rows(peak, part)
            peak = after(index, ("head", begin), jnp.max(peak, axis=0, keepdims=True))
            powers = [jnp.exp2((part - peak) * LOG2E) for part in parts]
            scale = coef / folded(powers)
            target = row_of(target_ref_of)
            for number, power in enumerate(powers):
                soft = power * scale
                place = lax.broadcasted_iota(jnp.int32, soft.shape, 0) + number * CHUNK
                soft = jnp.where(place == target, soft - coef, soft)
                missing = -soft.shape[0] % 16
                if missing:
                    soft = jnp.concatenate([soft, jnp.zeros((missing, LANES), F32)], axis=0)
                low.append(soft.astype(BF))
            mark(index, ("head", begin), scale)
            yield
        low.append(jnp.zeros((DEPTH - ROWS, LANES), BF))
        low = joined(low)
        lows[(index,)] = low[0:ROWS]
        grad = dot_nn(head_n[...], low)
        yield
        if index == chains - 1:
            head_acc[0:ROWS, :] += dot_nt(beside(lows), beside(tops))
        stream = pieces(grad)
        for layer in range(LAYERS, 0, -1):
            branches[index, layer] = joined([part.astype(BF) for part in stream])
            yield
            gated_grad = dot_nn(down_n[layer - 1], branches[index, layer])
            yield
            inner_grads[index, layer] = joined(
                [(part * slope).astype(BF) for part, slope in zip(pieces(gated_grad), inner_slopes[layer])]
            )
            yield
            active_grad = dot_nn(up_n[layer - 1], inner_grads[index, layer])
            if index == chains - 1:
                down_acc[layer - 1] += dot_nt(beside(branches, layer), beside(gateds, layer))
                up_acc[layer - 1] += dot_nt(beside(acts, layer), beside(inner_grads, layer))
            yield
            changes = norm_backward(index, layer, pieces(active_grad), kept[layer])
            stream = [part + change for part, change in zip(stream, changes)]
            yield
        values, slopes = kept[0][:2], [0.5 * slope for slope in kept[0][2]]
        pre = joined([part.astype(BF) for part in norm_backward(index, 0, stream, (*values, slopes))])
        yield
        lat_grad[cols, :] = dot_tn(pre, stem_t[...])
        pre_last[:, cols] = pre
        hot_last[:, cols] = hot
        lat_last[cols, :] = lat_ref[cols, :]

    def stem_grads():
        stem_acc[...] += dot_nn(pre_last[...], lat_last[...])
        table_acc[...] += dot_nt(pre_last[...], hot_last[...])

    stem_grads()

    running = []
    waiting = [chain(index) for index in range(chains)]
    while running or waiting:
        if waiting:
            running.append(waiting.pop(0))
        for member in list(running):
            try:
                next(member)
            except StopIteration:
                running.remove(member)
    for (which, at), total in norm_total.items():
        norm_part[which, at : at + CHUNK, :] += total

    @pl.when(step == pl.num_programs(0) - 1)
    def _():
        stem_grads()
        for at in range(0, DEPTH, D):
            head_acc[at : at + D, :] = head_acc[at : at + D, :].T
        lane_at = lax.broadcasted_iota(jnp.int32, (D, 128), 1)
        columns = jnp.zeros((D, 128), F32)
        for which in range(2 * (LAYERS + 1)):
            columns = jnp.where(lane_at == which, jnp.sum(norm_part[which], axis=1, keepdims=True), columns)
        norms = columns.T[0:16]
        def pieces_of(data, model):
            at = (data * packing.mp + model) * packing.own
            deep = slice(data * packing.deep, (data + 1) * packing.deep)
            wide = slice(model * packing.wide, (model + 1) * packing.wide)
            squares = [lambda: stem_acc[deep, wide]]
            squares += [lambda layer=layer: 0.5 * up_acc[layer, deep, wide] for layer in range(LAYERS)]
            squares += [lambda layer=layer: 0.5 * down_acc[layer, deep, wide] for layer in range(LAYERS)]
            for group in range(packing.groups):
                members = squares[group * packing.per : (group + 1) * packing.per]
                yield (
                    group * packing.deep,
                    slice(0, packing.wide * len(members)),
                    lambda members=members: jnp.concatenate([member() for member in members], axis=1),
                )
            for tile in range(DEPTH // 128):
                yield (
                    packing.head_at + packing.own * tile,
                    slice(0, 128),
                    lambda tile=tile: head_tile(tile)[at : at + packing.own, :],
                )
            own = slice(at, at + packing.own)
            yield packing.tail_at, slice(0, CODES), lambda: table_acc[own, :]
            yield (
                packing.tail_at,
                slice(NORM_LANE, NORM_LANE + packing.own),
                lambda: norms[0 : 2 * (LAYERS + 1), own],
            )

        leaving = []
        for side in range(PARTS):
            owners = {slot_of(packing.orders[side], *device): device for device in devices}
            for chunk in range(chunks):
                number = side * chunks + chunk
                place = departing.at[number % RING]
                if number >= RING:
                    leaving[number - RING].wait()
                place[...] = jnp.zeros((D, 128), F32)
                for row in range(0, D, packing.part):
                    for begin, lanes, value in pieces_of(*owners[(chunk * D + row) // packing.part]):
                        if begin // packing.part == side:
                            rows = value()
                            first = row + begin - side * packing.part
                            place[first : first + rows.shape[0], lanes] = rows
                leaving.append(
                    pltpu.make_async_copy(
                        place, outs[side].at[chunk * D : (chunk + 1) * D], copy_sem.at[side, chunk]
                    )
                )
                leaving[-1].start()
        for member in leaving[-RING:]:
            member.wait()


def train(packing, rows_all, latent, code, weight, value, reward, action, target, packed):
    count = latent.shape[0]
    chains = CHAINS
    block = chains * LANES

    def row():
        return pl.BlockSpec((block,), lambda i: (i,))

    parts = [pl.BlockSpec(memory_space=pl.ANY)] * PARTS
    flat = jax.ShapeDtypeStruct((packing.count * packing.part, 128), F32)
    packed = [member.reshape(-1, 128) for member in packed]
    return pl.pallas_call(
        functools.partial(train_kernel, packing, rows_all, chains),
        grid=(count // block,),
        out_shape=[jax.ShapeDtypeStruct((count, D), F32)] + [flat] * PARTS,
        in_specs=[pl.BlockSpec((block, D), lambda i: (i, 0))]
        + [row() for _ in range(6)] + parts,
        out_specs=[pl.BlockSpec((block, D), lambda i: (i, 0))] + parts,
        scratch_shapes=[
            pltpu.VMEM((D, D), F32),
            pltpu.VMEM((D, CODES), F32),
            pltpu.VMEM((LAYERS, D, D), F32),
            pltpu.VMEM((LAYERS, D, D), F32),
            pltpu.VMEM((DEPTH, D), F32),
            pltpu.VMEM((D, D), BF),
            pltpu.VMEM((D, CODES), BF),
            pltpu.VMEM((LAYERS, D, D), BF),
            pltpu.VMEM((LAYERS, D, D), BF),
            pltpu.VMEM((LAYERS, D, D), BF),
            pltpu.VMEM((LAYERS, D, D), BF),
            pltpu.VMEM((ROWS, D), BF),
            pltpu.VMEM((D, DEPTH), BF),
            pltpu.VMEM((1, LANES), F32),
            pltpu.VMEM((2 * (LAYERS + 1), D, 128), F32),
            pltpu.VMEM((2 * (LAYERS + 1), D, 128), F32),
            pltpu.VMEM((block, D), BF),
            pltpu.VMEM((D, block), BF),
            pltpu.VMEM((CODES, block), BF),
            pltpu.VMEM((PARTS * packing.count * packing.part // D, D, 128), BF),
            pltpu.VMEM((RING, D, 128), F32),
            pltpu.SemaphoreType.DMA((PARTS, packing.count * packing.part // D)),
        ],
        compiler_params=pltpu.CompilerParams(
            dimension_semantics=("arbitrary",), vmem_limit_bytes=62 * 1024 * 1024
        ),
        name="train",
    )(latent, code, weight, value, reward, action, target, *packed)


def body(rows_all, packing, *args):
    latent, code, weight, value, reward, action, target = args[:7]
    groups = [args[7 + 3 * which : 10 + 3 * which] for which in range(6)]

    def turn(which, array):
        return jnp.swapaxes(array, -1, -2) if which in (0, 2, 4) else array

    groups = [tuple(turn(which, member) for member in group) for which, group in enumerate(groups)]
    stem, up, down, head, table, norm = (group[0] for group in groups)
    packed = send_weights(packing, stem, up, down, head, table, norm, weight.reshape(-1, 128))
    lat_grad, *grads = train(packing, rows_all, latent, code, weight, value, reward, action, target, packed)
    own = reduce_grads(packing, [member.reshape(packing.count, packing.part, 128) for member in grads])
    outs = update(packing, rows_all, own, groups)
    result = [outs[0].reshape(()), lat_grad]
    at = 1
    for which in range(6):
        for _ in range(4 if which < 5 else 3):
            result.append(turn(which, outs[at]))
            at += 1
    return tuple(result)


def solution(mesh):
    every = ("dp", "mp")
    states, flat = P(every, None), P(every)
    params = (P("mp", "dp"), P(None, "dp", "mp"), P(None, "mp", "dp"), P(every, None), P(None, every), P(None, None, every))
    in_specs = (states,) + (flat,) * 6 + tuple(spec for spec in params for _ in range(3))
    out_specs = (P(), states) + tuple(spec for which, spec in enumerate(params) for _ in range(4 if which < 5 else 3))
    packing = Packing(mesh.shape["dp"], mesh.shape["mp"])

    def run(*args):
        rows_all = args[0].shape[0] * packing.count
        return body(rows_all, packing, *args)

    return jax.shard_map(run, mesh=mesh, in_specs=in_specs, out_specs=out_specs, check_vma=False)
```
